128 devices in a mesh: row: 16 (over x, z_hi, core), col: 8 (over z_lo, y).
Axes of the slice: x: 4, y: 4, z: 4 (z_hi: 2, z_lo: 2; z = z_hi * 2 + z_lo), core: 2. Of those that a mesh axis runs over, the one named last changes fastest.
Arguments:
- scene: bfloat16 [1024, 2048, 128], P('row', 'col'), may hold values from -6 to 6
- conv_first: bfloat16 [3, 3, 128, 128], replicated, may hold values from -0.1875 to 0.1875
- conv_second: bfloat16 [3, 3, 128, 128], replicated, may hold values from -0.1875 to 0.1875
- embed_weight: bfloat16 [8192, 768], P('row'), may hold values from -0.0625 to 0.0625
- router_weight: bfloat16 [768, 16], replicated, may hold values from -0.21875 to 0.21875
- expert_ids: int32 [16, 8, 256, 1], P('row', 'col'), may hold values from 0 to 15; in each aligned block of 256 rows (0 to 255, 256 to 511, ..., all dimensions but the last counted through in order) at most 48 rows name the same one
- expert_up: bfloat16 [16, 768, 3072], P('col'), may hold values from -0.21875 to 0.21875
- expert_down: bfloat16 [16, 3072, 768], P('col'), may hold values from -0.109375 to 0.109375
Outputs:
- mixed: bfloat16 [16, 8, 256, 768], P('row', 'col')
The draws below stay inside these ranges and needn't reach their ends.
Inputs may be any that keep to these rules, and one draw needn't show every extreme that they name: `expert_ids`: within the tokens of one block (a, b), no expert is named by more than 48 tokens, a bound that some block reaches.
All inputs are finite; a program needn't handle non-finite values.
Results may differ from the reference program's by a relative error of at most 0.014.
Values may be sent and summed in bfloat16 or wider, within the bound.
No kernel may reach another device: no remote copies, remote signals or barrier semaphores. Data moves between devices by JAX's collectives and lax.ppermute only.
A program may use at most 128 MiB of HBM per device.

```python
import math
import jax
import jax.numpy as jnp
import numpy as np
from jax import lax

C = 128
D = 768
FF = 3072
PATCH = 8
TILE_H = 64
TILE_W = 256
TOK = 256
PATCH_IN = 8192
EXPERTS = 16
CAP = 48
SCENE_H = 1024
SCENE_W = 2048
N_ROW = 16
N_COL = 8


def level_of(key, extent, split, least, largest):
    factor_of, own = 1.0, jax.random.fold_in(key, 6)
    for dim, blocks in split:
        heights = jnp.exp(jax.random.uniform(jax.random.fold_in(own, dim), (blocks,), jnp.float32, least / len(split), largest / len(split)))
        factor_of = factor_of * jnp.repeat(heights, extent[dim] // blocks).reshape([-1 if axis == dim else 1 for axis in range(len(extent))])
    return factor_of


def shared_out(stream_key, own, number, rows, number_of, top, bound, skew):
    order = jax.random.permutation(stream_key, number_of)
    packed, usual = shares(number_of, rows * top, bound, skew, True), shares(number_of, rows * top, bound, skew, False)
    places = jnp.arange(number_of)

    def named(lengths, turn):
        used = int((lengths > 0).sum())
        fixed = max(1, used // 4)
        shifted = fixed + (places - fixed + turn * (used - fixed)) % max(1, number_of - fixed)
        return jnp.zeros((number_of,), jnp.int32).at[order[jnp.where(places < fixed, places, shifted)]].set(jnp.asarray(lengths, jnp.int32))

    lengths = jnp.where(number % 4 == 0, named(packed, number // 4), named(usual, number - number // 4 - 1))
    mixed = jax.random.permutation(jax.random.fold_in(own, 3), number_of)
    giver, receiver = mixed[0:number_of // 2 * 2:2], mixed[1:number_of // 2 * 2:2]
    slack = jnp.minimum(lengths[giver] - 1, bound - lengths[receiver]) // 2
    slack = jnp.where((giver == order[0]) | (receiver == order[0]) | (lengths[receiver] == 0), 0, jnp.maximum(slack, 0))
    shifted = jax.random.randint(jax.random.fold_in(own, 4), (number_of // 2,), 0, 1 << 20) % (slack + 1)
    lengths = lengths.at[giver].add(-shifted).at[receiver].add(shifted)
    labels = jnp.searchsorted(jnp.cumsum(lengths), jnp.arange(rows * top), side="right").astype(jnp.int32)
    table = labels.reshape(top, rows).T
    table = table[jax.random.permutation(jax.random.fold_in(own, 1), rows)]
    turn = jax.random.randint(jax.random.fold_in(own, 2), (rows, 1), 0, top)
    return jnp.take_along_axis(table, (jnp.arange(top)[None, :] + turn) % top, axis=1)


def shares(count, total, bound, lean, full):
    weights = [(1 << 20) // math.isqrt(grade ** lean) + 1 for grade in range(1, count + 1)]
    largest = bound if full else min(bound, max(-(-total // count), total * weights[0] // sum(weights)))
    least = 1 if total - largest >= count - 1 else 0
    counts, rest = [largest] + [least] * (count - 1), total - largest - least * (count - 1)
    while rest > 0:
        movable = [i for i in range(1, count) if counts[i] < largest] or [i for i in range(1, count) if counts[i] < bound]
        mass, budget = sum([weights[i] for i in movable]), rest
        for i in movable:
            addition = min(bound - counts[i], max(1, budget * weights[i] // mass), rest)
            counts[i] = counts[i] + addition
            rest = rest - addition
    return np.array(counts)


def normal_values(stream_key, dims, spread, bound, shards=(), held_as=jnp.bfloat16):
    entries = spread * jax.random.normal(stream_key, dims, jnp.float32)
    if shards:
        entries = entries * level_of(stream_key, dims, shards, -0.22, 0.18)
    return jnp.clip(entries, -bound, bound).astype(held_as)


def setup_inputs(seed: int = 0) -> dict:
    streams_of = jax.random.split(jax.random.key(seed), 9)
    scene = normal_values(streams_of[0], (SCENE_H, SCENE_W, C), 1.0, 6.0, ((0, 16), (1, 8)))
    conv_first = normal_values(streams_of[1], (3, 3, C, C), (9 * C) ** -0.5, 0.1875)
    conv_second = normal_values(streams_of[2], (3, 3, C, C), (9 * C) ** -0.5, 0.1875)
    embed_weight = normal_values(streams_of[3], (PATCH_IN, D), PATCH_IN ** -0.5, 0.0625, ((0, 16),))
    router_weight = normal_values(streams_of[4], (D, EXPERTS), D ** -0.5, 0.21875)
    expert_ids_keys = jax.random.split(jax.random.fold_in(streams_of[5], 1), N_ROW * N_COL * TOK // TOK)
    expert_ids_turns = jax.random.permutation(jax.random.fold_in(streams_of[5], 3), N_ROW * N_COL * TOK // TOK)
    expert_ids = jax.vmap(lambda own, number: shared_out(jax.random.fold_in(streams_of[5], 2), own, number, TOK, EXPERTS, 1, CAP, 2))(expert_ids_keys, expert_ids_turns).reshape((N_ROW, N_COL, TOK, 1))
    expert_up = normal_values(streams_of[6], (EXPERTS, D, FF), D ** -0.5, 0.21875, ((0, 8),))
    expert_down = normal_values(streams_of[7], (EXPERTS, FF, D), FF ** -0.5, 0.109375, ((0, 8),))
    return {"scene": scene, "conv_first": conv_first, "conv_second": conv_second, "embed_weight": embed_weight, "router_weight": router_weight, "expert_ids": expert_ids, "expert_up": expert_up, "expert_down": expert_down}


def conv_same(field, weight):
    result = lax.conv_general_dilated(field[None].astype(jnp.float32), weight.astype(jnp.float32), (1, 1), 'SAME', dimension_numbers=('NHWC', 'HWIO', 'NHWC'), precision=lax.Precision.HIGHEST)
    return result[0]

def place_rows(position, rows):
    return jnp.zeros((EXPERTS * CAP, D), jnp.bfloat16).at[position].set(rows)

def take_rows(table, position):
    return table[position]

def run_expert(inputs):
    rows, upper, lower = inputs
    hidden = jax.nn.gelu(jnp.dot(rows, upper, preferred_element_type=jnp.float32)).astype(jnp.bfloat16)
    return jnp.dot(hidden, lower, preferred_element_type=jnp.float32).astype(jnp.bfloat16)

def reference(scene, conv_first, conv_second, embed_weight, router_weight, expert_ids, expert_up, expert_down):
    hidden_first = jax.nn.relu(conv_same(scene, conv_first)).astype(jnp.bfloat16)
    feature = (scene.astype(jnp.float32) + conv_same(hidden_first, conv_second)).astype(jnp.bfloat16)
    devices = N_ROW * N_COL
    grid = feature.reshape(N_ROW, TILE_H // PATCH, PATCH, N_COL, TILE_W // PATCH, PATCH, C)
    grid = grid.transpose(0, 3, 1, 4, 2, 5, 6).reshape(devices * TOK, PATCH_IN)
    embedded = jnp.dot(grid, embed_weight, preferred_element_type=jnp.float32).astype(jnp.bfloat16)
    wide = embedded.astype(jnp.float32)
    normed = (wide * lax.rsqrt(lax.optimization_barrier(jnp.mean(wide * wide, axis=-1, keepdims=True)) + 1e-06)).astype(jnp.bfloat16)
    scores = jnp.dot(normed, router_weight, preferred_element_type=jnp.float32).reshape(devices, TOK, EXPERTS)
    routing = expert_ids.reshape(devices, TOK).astype(jnp.int32)
    one_hot = (routing[:, :, None] == jnp.arange(EXPERTS, dtype=jnp.int32)).astype(jnp.int32)
    gating = jax.nn.sigmoid(lax.optimization_barrier(jnp.sum(scores * one_hot.astype(jnp.float32), axis=-1)))
    ranking = jnp.cumsum(one_hot, axis=1, dtype=jnp.int32) - 1
    slot_index = lax.optimization_barrier(jnp.sum(ranking * one_hot, axis=-1)).astype(jnp.int32)
    position = (routing * CAP + slot_index).astype(jnp.int32)
    buffers = jax.vmap(place_rows)(position, normed.reshape(devices, TOK, D))
    stacked = buffers.reshape(devices, EXPERTS, CAP, D).transpose(1, 0, 2, 3).reshape(EXPERTS, devices * CAP, D)
    outputs = lax.map(run_expert, (stacked, expert_up, expert_down))
    returned = outputs.reshape(EXPERTS, devices, CAP, D).transpose(1, 0, 2, 3).reshape(devices, EXPERTS * CAP, D)
    expert_out = jax.vmap(take_rows)(returned, position)
    mixed = embedded.reshape(devices, TOK, D).astype(jnp.float32) + gating[:, :, None] * expert_out.astype(jnp.float32)
    return mixed.astype(jnp.bfloat16).reshape(N_ROW, N_COL, TOK, D)
```

```python
import functools

import jax
import jax.numpy as jnp
from jax import lax
from jax.experimental import pallas as pl
from jax.experimental.pallas import tpu as pltpu
from jax.sharding import PartitionSpec as P

ROWS, COLS, CH = 64, 256, 128
WIDE = 272
DIM, FF, CAP, TOK = 768, 3072, 48, 256
SLOTS = 8 * CAP
FIRST = 5
F32, BF16 = jnp.float32, jnp.bfloat16
ANY = pl.BlockSpec(memory_space=pl.ANY)
VMEM = pl.BlockSpec(memory_space=pltpu.VMEM)
SMEM = pl.BlockSpec(memory_space=pltpu.SMEM)


def params():
    return pltpu.CompilerParams(vmem_limit_bytes=56 * 2**20)


def hop(dx=0, dy=0, dh=0, dl=0, dc=0):
    pairs = []
    for x in range(4):
        for h in range(2):
            for c in range(2):
                for low in range(2):
                    for y in range(4):
                        here = (x * 4 + h * 2 + c) * 8 + low * 4 + y
                        there = (
                            ((x + dx) % 4 * 4 + (h + dh) % 2 * 2 + (c + dc) % 2) * 8
                            + (low + dl) % 2 * 4
                            + (y + dy) % 4
                        )
                        pairs.append((here, there))
    return pairs


def send(value, **step):
    return lax.ppermute(value, ("row", "col"), hop(**step))


def pair_weights(source, target):
    zero = jnp.zeros((CH, CH), BF16)
    for j in range(4):
        for dx in range(3):
            rows = pl.ds(j * CH, CH)
            target[rows, pl.ds(dx * 256, CH)] = source[j, dx] if j < 3 else zero
            target[rows, pl.ds(dx * 256 + CH, CH)] = source[j - 1, dx] if j > 0 else zero


def pair_conv(source, weights, pair):
    taps = jnp.concatenate([source[2 * pair + j] for j in range(4)], axis=1)
    parts = jnp.dot(taps, weights[...], preferred_element_type=F32)
    left = pltpu.roll(parts[:, 0:256], 1, 0)
    right = pltpu.roll(parts[:, 512:768], WIDE - 1, 0)
    return left + parts[:, 256:512] + right


def conv_kernel(
    start, steps, place, scene, top, bottom, strip, first, second, keep, other,
    block, hidden, rows, w1, w2, sems,
):
    step = pl.program_id(0)
    height = 8 * steps + 4
    base = 8 * start - 2
    chunks = []
    for k in range(steps):
        lo, hi = (0, 12) if k == 0 else (4 + 8 * k, 12 + 8 * k)
        copies = []
        if base + lo < 0:
            copies.append((top, block.at[0:2, 0:COLS]))
        a, b = max(base + lo, 0), min(base + hi, ROWS)
        copies.append((scene.at[a:b], block.at[a - base : b - base, 0:COLS]))
        if base + hi > ROWS:
            copies.append((bottom, block.at[height - 2 : height, 0:COLS]))
        copies.append((strip.at[base + lo + 2 : base + hi + 2], block.at[lo:hi, COLS:WIDE]))
        chunks.append(
            [pltpu.make_async_copy(s, d, sems.at[k, n]) for n, (s, d) in enumerate(copies)]
        )
    place_row, place_col, core = place[0], place[1], place[2]
    tail = lax.broadcasted_iota(jnp.int32, (16, 256), 0)
    cut = ((place_col == 0) & (tail >= 8)) | ((place_col == 7) & (tail < 8))
    edge = jnp.where(cut, 0.0, 1.0).astype(F32)

    def conv_first(pair):
        value = jnp.maximum(pair_conv(block, w1, pair), 0.0)
        body, ends = value[0:COLS].astype(BF16), (value[COLS:WIDE] * edge).astype(BF16)
        for i in range(2):
            hidden[2 * pair + i, 0:COLS] = body[:, i * CH : (i + 1) * CH]
            hidden[2 * pair + i, COLS:WIDE] = ends[:, i * CH : (i + 1) * CH]

    @pl.when(step == 0)
    def _():
        for chunk in chunks:
            for copy in chunk:
                copy.start()
        pair_weights(first, w1)
        pair_weights(second, w2)
        for copy in chunks[0]:
            copy.wait()
        conv_first(0)
        if start == 0:

            @pl.when(place_row == 0)
            def _():
                hidden[0] = jnp.zeros((WIDE, CH), BF16)

    for k in range(1, steps):

        @pl.when(step == k)
        def _(k=k):
            for copy in chunks[k]:
                copy.wait()

    for i in range(4):
        conv_first(4 * step + 1 + i)
    if 8 * (start + steps) == ROWS:

        @pl.when((step == steps - 1) & (place_row == 15))
        def _():
            hidden[8 * steps + 1] = jnp.zeros((WIDE, CH), BF16)

    for i in range(4):
        pair = 4 * step + i
        value = pair_conv(hidden, w2, pair)[0:COLS]
        for n in range(2):
            cells = block[2 * pair + 2 + n, 0:COLS].astype(F32)
            rows[pl.ds((2 * i + n) * COLS, COLS), :] = value[:, n * CH : (n + 1) * CH] + cells
    for dy in range(8):
        for j in range(4):
            low = rows[pl.ds(dy * COLS + j, 32, stride=8), :]
            high = rows[pl.ds(dy * COLS + 4 + j, 32, stride=8), :]
            lanes = pl.ds(j * CH, CH)
            keep[dy, :, lanes] = jnp.where(core == 0, low, high).astype(BF16)
            other[dy, :, lanes] = jnp.where(core == 0, high, low).astype(BF16)


def conv_call(start, steps, *args):
    shape = jax.ShapeDtypeStruct((8, 32 * steps, 512), BF16)
    out = pl.BlockSpec((8, 32, 512), lambda i: (0, i, 0))
    return pl.pallas_call(
        functools.partial(conv_kernel, start, steps),
        grid=(steps,),
        in_specs=[SMEM, ANY, ANY, ANY, ANY, VMEM, VMEM],
        out_specs=[out, out],
        out_shape=[shape, shape],
        scratch_shapes=[
            pltpu.VMEM((8 * steps + 4, WIDE, CH), BF16),
            pltpu.VMEM((8 * steps + 2, WIDE, CH), BF16),
            pltpu.VMEM((8 * COLS, CH), F32),
            pltpu.VMEM((512, 768), BF16),
            pltpu.VMEM((512, 768), BF16),
            pltpu.SemaphoreType.DMA((steps, 4)),
        ],
        compiler_params=params(),
        name=f"convs_{start}",
    )(*args)


def embed_kernel(layout, has_sum, order, *refs):
    tokens, pieces = refs[0:4], refs[4 : 4 + len(layout)]
    rest = refs[4 + len(layout) :]
    given, rest = (rest[0:2], rest[2:]) if has_sum else ((), rest)
    own, partner, lhs, rhs, lhs_sems, rhs_sems = rest
    copies = []
    for n, (which, offset, depth) in enumerate(layout):
        k = order[which]
        here, at = [], 0
        for m, source in enumerate(tokens):
            count = source.shape[1]
            here.append(
                pltpu.make_async_copy(
                    source.at[k, :, pl.ds(offset, depth)],
                    lhs.at[n, pl.ds(at, count), pl.ds(0, depth)],
                    lhs_sems.at[n, m],
                )
            )
            at += count
        here.append(
            pltpu.make_async_copy(pieces[n], rhs.at[n, pl.ds(0, depth)], rhs_sems.at[n])
        )
        copies.append(here)
    for here in copies:
        for copy in here:
            copy.start()
    for n, (which, offset, depth) in enumerate(layout):
        for copy in copies[n]:
            copy.wait()
        for target, at, base in ((partner, TOK, 1), (own, 0, 0)):
            part = jnp.dot(
                lhs[n, pl.ds(at, TOK), 0:depth], rhs[n, 0:depth], preferred_element_type=F32
            )
            if n == 0 and not has_sum:
                target[...] = part
            elif n == 0:
                target[...] = given[base][...] + part
            else:
                target[...] += part


def embed_call(name, order, tokens, pieces, sums=()):
    layout = tuple((which, offset, array.shape[0]) for array, which, offset in pieces)
    count = len(pieces)
    shape = jax.ShapeDtypeStruct((TOK, DIM), F32)
    return pl.pallas_call(
        functools.partial(embed_kernel, layout, bool(sums)),
        in_specs=[SMEM] + [ANY] * (4 + count) + [VMEM] * len(sums),
        out_specs=[VMEM, VMEM],
        out_shape=[shape, shape],
        scratch_shapes=[
            pltpu.VMEM((count, 2 * TOK, 512), BF16),
            pltpu.VMEM((count, 512, DIM), BF16),
            pltpu.SemaphoreType.DMA((count, 4)),
            pltpu.SemaphoreType.DMA((count,)),
        ],
        compiler_params=params(),
        name=name,
    )(order, *tokens, *[array for array, _, _ in pieces], *sums)


def route_kernel(own, came, router, ids_row, ids_col, embedded, out0, out1, gate, place):
    value = (own[...] + came[...]).astype(BF16)
    embedded[...] = value
    wide = value.astype(F32)
    scale = lax.rsqrt(jnp.mean(wide * wide, axis=-1, keepdims=True) + 1e-06)
    normed = (wide * scale).astype(BF16)
    scores = jnp.dot(normed, router[...], preferred_element_type=F32)
    across = lax.broadcasted_iota(jnp.int32, (TOK, TOK), 1)
    down = lax.broadcasted_iota(jnp.int32, (TOK, TOK), 0)
    col, row = ids_col[...], ids_row[...]
    hot = jnp.where(col == lax.broadcasted_iota(jnp.int32, (TOK, 16), 1), 1.0, 0.0)
    gate[...] = jax.nn.sigmoid(jnp.sum(scores * hot, axis=-1, keepdims=True))
    earlier = jnp.where(across < down, 1.0, 0.0).astype(BF16)
    counts = jnp.dot(earlier, hot.astype(BF16), preferred_element_type=F32)
    rank = jnp.sum(counts * hot, axis=-1, keepdims=True).astype(jnp.int32)
    place[...] = (col & 1) * SLOTS + (col >> 1) * CAP + rank
    hot_t = jnp.where(row == lax.broadcasted_iota(jnp.int32, (16, TOK), 0), 1.0, 0.0)
    later = jnp.where(down < across, 1.0, 0.0).astype(BF16)
    counts_t = jnp.dot(hot_t.astype(BF16), later, preferred_element_type=F32)
    rank_t = jnp.sum(counts_t * hot_t, axis=0, keepdims=True).astype(jnp.int32)
    place_t = (row & 1) * SLOTS + (row >> 1) * CAP + rank_t
    slot = lax.broadcasted_iota(jnp.int32, (SLOTS, TOK), 0)
    for n, out in enumerate((out0, out1)):
        pick = jnp.where(slot + n * SLOTS == place_t, 1.0, 0.0).astype(BF16)
        out[...] = jnp.dot(pick, normed, preferred_element_type=F32).astype(BF16)


def route_call(*args):
    shapes = [((TOK, DIM), BF16), ((SLOTS, DIM), BF16), ((SLOTS, DIM), BF16)]
    shapes += [((TOK, 1), F32), ((TOK, 1), jnp.int32)]
    return pl.pallas_call(
        route_kernel,
        in_specs=[VMEM] * 5,
        out_specs=[VMEM] * 5,
        out_shape=[jax.ShapeDtypeStruct(*shape) for shape in shapes],
        compiler_params=params(),
        name="route",
    )(*args)


def expert_kernel(rows, up, down, out, total):
    step = pl.program_id(0)
    z = jnp.dot(rows[...], up[...], preferred_element_type=F32)
    act = 0.5 * z * (1.0 + jnp.tanh(0.7978845608028654 * (z + 0.044715 * (z * z * z))))
    part = jnp.dot(act.astype(BF16), down[...], preferred_element_type=F32)

    @pl.when(step == 0)
    def _():
        total[...] = part

    @pl.when(step > 0)
    def _():
        total[...] += part

    @pl.when(step == pl.num_programs(0) - 1)
    def _():
        out[...] = total[...].astype(BF16)


def expert_call(which, rows, up, down, width=768):
    whole = pl.BlockSpec((SLOTS, DIM), lambda i: (0, 0))
    return pl.pallas_call(
        expert_kernel,
        grid=(FF // width,),
        in_specs=[
            whole,
            pl.BlockSpec((None, DIM, width), lambda i: (which, 0, i)),
            pl.BlockSpec((None, width, DIM), lambda i: (which, i, 0)),
        ],
        out_specs=whole,
        out_shape=jax.ShapeDtypeStruct((SLOTS, DIM), BF16),
        scratch_shapes=[pltpu.VMEM((SLOTS, DIM), F32)],
        compiler_params=params(),
        name=f"expert_{which}",
    )(rows, up, down)


def mix_kernel(embedded, gate, place, back0, back1, out):
    slot = lax.broadcasted_iota(jnp.int32, (TOK, SLOTS), 1)
    result = None
    for n, back in enumerate((back0, back1)):
        pick = jnp.where(slot + n * SLOTS == place[...], 1.0, 0.0).astype(BF16)
        part = jnp.dot(pick, back[...], preferred_element_type=F32)
        result = part if result is None else result + part
    out[...] = (embedded[...].astype(F32) + gate[...] * result).astype(BF16)


def mix_call(*args):
    return pl.pallas_call(
        mix_kernel,
        in_specs=[VMEM] * 5,
        out_specs=VMEM,
        out_shape=jax.ShapeDtypeStruct((TOK, DIM), BF16),
        compiler_params=params(),
        name="mix",
    )(*args)


def neighbours(value, axis, ahead):
    count = lax.axis_size(axis)
    pairs = [(i, i + 1) for i in range(count - 1)]
    return lax.ppermute(value, axis, pairs if ahead else [(j, i) for i, j in pairs])


def exchange(value):
    value = value.reshape(8, CAP, DIM)
    return lax.all_to_all(value, "col", 0, 0, tiled=True).reshape(SLOTS, DIM)


def local(
    scene, conv_first, conv_second, embed_weight, router_weight, expert_ids, expert_up, expert_down
):
    row, col = lax.axis_index("row"), lax.axis_index("col")
    x, high, core = row // 4, row // 2 % 2, row % 2
    place = jnp.stack([row, col, core]).astype(jnp.int32)

    top = neighbours(scene[ROWS - 2 :], "row", True)
    bottom = neighbours(scene[:2], "row", False)
    left_own = jnp.concatenate([top[:, :2], scene[:, :2], bottom[:, :2]], axis=0)
    right_own = jnp.concatenate([top[:, -2:], scene[:, -2:], bottom[:, -2:]], axis=0)
    left = neighbours(right_own, "col", True)
    right = neighbours(left_own, "col", False)
    strip = jnp.concatenate([right, jnp.zeros((ROWS + 4, 12, CH), BF16), left], axis=1)

    w = embed_weight
    w_minus, w_plus, w_high = send(w, dx=1), send(w, dx=-1), send(w, dh=1, dl=1)
    scene_args = (place, scene, top, bottom, strip, conv_first, conv_second)
    keep0, other0 = conv_call(0, FIRST, *scene_args)
    keep0, other0, w_minus, w_plus, w_high = lax.optimization_barrier(
        (keep0, other0, w_minus, w_plus, w_high)
    )
    w_far0, w_far1 = send(w_minus[:256], dx=1), send(w_plus[256:], dx=-1)
    w_high_minus, w_high_plus = send(w_high, dx=1), send(w_high, dx=-1)
    came0 = send(other0, dc=1)
    keep1, other1 = conv_call(FIRST, 8 - FIRST, *scene_args)
    came1 = send(other1, dc=1)
    w_high_far0, w_high_far1 = send(w_far0, dh=1, dl=1), send(w_far1, dh=1, dl=1)

    shards = [(a % 4) * 2 + (b % 2) for b in (high, high + 1) for a in (x, x - 1, x + 1, x + 2)]
    order = jnp.stack(shards).astype(jnp.int32)
    tokens = (keep0, keep1, came0, came1)
    sums = embed_call(
        "embed_a", order, tokens, [(w, 0, 0), (w_minus, 1, 0), (w_plus, 2, 0), (w_high, 4, 0)]
    )
    sums = embed_call(
        "embed_b",
        order,
        tokens,
        [(w_far0, 3, 0), (w_far1, 3, 256), (w_high_minus, 5, 0), (w_high_plus, 6, 0)],
        sums,
    )
    own, partner = embed_call(
        "embed_c", order, tokens, [(w_high_far0, 7, 0), (w_high_far1, 7, 256)], sums
    )
    came = send(partner, dc=1)
    embedded, out0, out1, gate, slots = route_call(
        own, came, router_weight, expert_ids.reshape(1, TOK), expert_ids.reshape(TOK, 1)
    )
    in0, in1 = exchange(out0), exchange(out1)
    back0 = exchange(expert_call(0, in0, expert_up, expert_down))
    back1 = exchange(expert_call(1, in1, expert_up, expert_down))
    return mix_call(embedded, gate, slots, back0, back1).reshape(1, 1, TOK, DIM)


def solution(mesh):
    return jax.shard_map(
        local,
        mesh=mesh,
        in_specs=(
            P("row", "col", None),
            P(),
            P(),
            P("row", None),
            P(),
            P("row", "col", None, None),
            P("col", None, None),
            P("col", None, None),
        ),
        out_specs=P("row", "col", None, None),
        check_vma=False,
    )
```

```python
import functools

import jax
import jax.numpy as jnp
from jax import lax
from jax.experimental import pallas as pl
from jax.experimental.pallas import tpu as pltpu
from jax.sharding import PartitionSpec as P

ROWS, COLS, CH = 64, 256, 128
WIDE = 272
DIM, FF, CAP, TOK = 768, 3072, 48, 256
SLOTS = 8 * CAP
FIRST = 4
F32, BF16 = jnp.float32, jnp.bfloat16
ANY = pl.BlockSpec(memory_space=pl.ANY)
VMEM = pl.BlockSpec(memory_space=pltpu.VMEM)
SMEM = pl.BlockSpec(memory_space=pltpu.SMEM)


def params(mib):
    return pltpu.CompilerParams(vmem_limit_bytes=mib * 2**20)


def cost(micros):
    return pl.CostEstimate(flops=int(micros * 1.15e9), bytes_accessed=0, transcendentals=0)


def hop(dx=0, dy=0, dh=0, dl=0, dc=0):
    pairs = []
    for x in range(4):
        for h in range(2):
            for c in range(2):
                for low in range(2):
                    for y in range(4):
                        here = (x * 4 + h * 2 + c) * 8 + low * 4 + y
                        there = (
                            ((x + dx) % 4 * 4 + (h + dh) % 2 * 2 + (c + dc) % 2) * 8
                            + (low + dl) % 2 * 4
                            + (y + dy) % 4
                        )
                        pairs.append((here, there))
    return pairs


def send(value, **step):
    return lax.ppermute(value, ("row", "col"), hop(**step))


def pair_weights(source, target):
    zero = jnp.zeros((CH, CH), BF16)
    for j in range(4):
        for dx in range(3):
            rows = pl.ds(j * CH, CH)
            target[rows, pl.ds(dx * 256, CH)] = source[j, dx] if j < 3 else zero
            target[rows, pl.ds(dx * 256 + CH, CH)] = source[j - 1, dx] if j > 0 else zero


def pair_conv(source, weights, pair):
    taps = jnp.concatenate([source[2 * pair + j] for j in range(4)], axis=1)
    parts = jnp.dot(taps, weights[...], preferred_element_type=F32)
    left = pltpu.roll(parts[:, 0:256], 1, 0)
    right = pltpu.roll(parts[:, 512:768], WIDE - 1, 0)
    return left + parts[:, 256:512] + right


def conv_kernel(start, steps, place, scene, top, bottom, strip, first, second, *refs):
    patches, block, hidden, rows, w1, w2, sems = refs[-7:]
    step = pl.program_id(0)
    height = 8 * steps + 4
    base = 8 * start - 2
    chunks = []
    for k in range(steps):
        lo, hi = (0, 12) if k == 0 else (4 + 8 * k, 12 + 8 * k)
        copies = []
        if base + lo < 0:
            copies.append((top, block.at[0:2, 0:COLS]))
        a, b = max(base + lo, 0), min(base + hi, ROWS)
        copies.append((scene.at[a:b], block.at[a - base : b - base, 0:COLS]))
        if base + hi > ROWS:
            copies.append((bottom, block.at[height - 2 : height, 0:COLS]))
        copies.append((strip.at[base + lo + 2 : base + hi + 2], block.at[lo:hi, COLS:WIDE]))
        chunks.append(
            [pltpu.make_async_copy(s, d, sems.at[k, n]) for n, (s, d) in enumerate(copies)]
        )
    place_row, place_col = place[0], place[1]
    tail = lax.broadcasted_iota(jnp.int32, (16, 256), 0)
    cut = ((place_col == 0) & (tail >= 8)) | ((place_col == 7) & (tail < 8))
    edge = jnp.where(cut, 0.0, 1.0).astype(F32)

    def conv_first(pair):
        value = jnp.maximum(pair_conv(block, w1, pair), 0.0)
        body, ends = value[0:COLS].astype(BF16), (value[COLS:WIDE] * edge).astype(BF16)
        for i in range(2):
            hidden[2 * pair + i, 0:COLS] = body[:, i * CH : (i + 1) * CH]
            hidden[2 * pair + i, COLS:WIDE] = ends[:, i * CH : (i + 1) * CH]

    @pl.when(step == 0)
    def _():
        for chunk in chunks:
            for copy in chunk:
                copy.start()
        pair_weights(first, w1)
        pair_weights(second, w2)
        for copy in chunks[0]:
            copy.wait()
        conv_first(0)
        if start == 0:

            @pl.when(place_row == 0)
            def _():
                hidden[0] = jnp.zeros((WIDE, CH), BF16)

    for k in range(1, steps):

        @pl.when(step == k)
        def _(k=k):
            for copy in chunks[k]:
                copy.wait()

    for i in range(4):
        conv_first(4 * step + 1 + i)
    if 8 * (start + steps) == ROWS:

        @pl.when((step == steps - 1) & (place_row == 15))
        def _():
            hidden[8 * steps + 1] = jnp.zeros((WIDE, CH), BF16)

    for i in range(4):
        pair = 4 * step + i
        value = pair_conv(hidden, w2, pair)[0:COLS]
        for n in range(2):
            cells = block[2 * pair + 2 + n, 0:COLS].astype(F32)
            rows[pl.ds((2 * i + n) * COLS, COLS), :] = value[:, n * CH : (n + 1) * CH] + cells
    for dy in range(8):
        for j in range(8):
            cells = rows[pl.ds(dy * COLS + j, 32, stride=8), :]
            patches[j // 4, dy, :, pl.ds(j % 4 * CH, CH)] = cells.astype(BF16)


def conv_call(start, steps, *args):
    given = len(args) - 7
    return pl.pallas_call(
        functools.partial(conv_kernel, start, steps),
        grid=(steps,),
        in_specs=[SMEM, ANY, ANY, ANY, ANY, VMEM, VMEM] + [ANY] * given,
        out_specs=pl.BlockSpec((2, 8, 32, 512), lambda i: (0, 0, start + i, 0)),
        out_shape=jax.ShapeDtypeStruct((2, 8, TOK, 512), BF16),
        scratch_shapes=[
            pltpu.VMEM((8 * steps + 4, WIDE, CH), BF16),
            pltpu.VMEM((8 * steps + 2, WIDE, CH), BF16),
            pltpu.VMEM((8 * COLS, CH), F32),
            pltpu.VMEM((512, 768), BF16),
            pltpu.VMEM((512, 768), BF16),
            pltpu.SemaphoreType.DMA((steps, 4)),
        ],
        input_output_aliases={7: 0} if given else {},
        compiler_params=params(20),
        cost_estimate=cost(12),
        name=f"convs_{start}",
    )(*args)


def embed_kernel(layout, has_sum, order, tokens, *refs):
    count = sum(len(parts) for _, parts in layout)
    pieces, rest = refs[:count], refs[count:]
    given, rest = (rest[0:2], rest[2:]) if has_sum else ((), rest)
    own, partner, lhs, rhs, lhs_sems, rhs_sems = rest
    copies, at = [], 0
    for n, (which, parts) in enumerate(layout):
        k = order[which]
        here = [
            pltpu.make_async_copy(
                tokens.at[order[12 + m], k], lhs.at[n, pl.ds(m * TOK, TOK)], lhs_sems.at[n, m]
            )
            for m in range(2)
        ]
        for m, (first, quarter) in enumerate(parts):
            if quarter is None:
                source, target = pieces[at], rhs.at[n]
            else:
                target = rhs.at[n, pl.ds(pl.multiple_of(order[quarter] * 128, 128), 128)]
                source = pieces[at].at[first : first + 128]
            here.append(pltpu.make_async_copy(source, target, rhs_sems.at[n, m]))
            at += 1
        copies.append(here)
    for here in copies:
        for copy in here:
            copy.start()
    for n in range(len(layout)):
        for copy in copies[n]:
            copy.wait()
        for m, target in ((1, partner), (0, own)):
            part = jnp.dot(lhs[n, pl.ds(m * TOK, TOK)], rhs[n], preferred_element_type=F32)
            if n == 0 and not has_sum:
                target[...] = part
            elif n == 0:
                target[...] = given[m][...] + part
            else:
                target[...] += part


def embed_call(name, order, tokens, shards, sums=()):
    layout = tuple((which, tuple(part[1:] for part in parts)) for which, parts in shards)
    arrays = [part[0] for _, parts in shards for part in parts]
    shape = jax.ShapeDtypeStruct((TOK, DIM), F32)
    count = len(shards)
    return pl.pallas_call(
        functools.partial(embed_kernel, layout, bool(sums)),
        in_specs=[SMEM] + [ANY] * (1 + len(arrays)) + [VMEM] * len(sums),
        out_specs=[VMEM, VMEM],
        out_shape=[shape, shape],
        scratch_shapes=[
            pltpu.VMEM((count, 2 * TOK, 512), BF16),
            pltpu.VMEM((count, 512, DIM), BF16),
            pltpu.SemaphoreType.DMA((count, 2)),
            pltpu.SemaphoreType.DMA((count, 4)),
        ],
        compiler_params=params(20),
        cost_estimate=cost(4),
        name=name,
    )(order, tokens, *arrays, *sums)


def route_kernel(own, came, router, ids_row, ids_col, embedded, out0, out1, gate, place):
    value = (own[...] + came[...]).astype(BF16)
    embedded[...] = value
    wide = value.astype(F32)
    scale = lax.rsqrt(jnp.mean(wide * wide, axis=-1, keepdims=True) + 1e-06)
    normed = (wide * scale).astype(BF16)
    scores = jnp.dot(normed, router[...], preferred_element_type=F32)
    across = lax.broadcasted_iota(jnp.int32, (TOK, TOK), 1)
    down = lax.broadcasted_iota(jnp.int32, (TOK, TOK), 0)
    col, row = ids_col[...], ids_row[...]
    hot = jnp.where(col == lax.broadcasted_iota(jnp.int32, (TOK, 16), 1), 1.0, 0.0)
    gate[...] = jax.nn.sigmoid(jnp.sum(scores * hot, axis=-1, keepdims=True))
    earlier = jnp.where(across < down, 1.0, 0.0).astype(BF16)
    counts = jnp.dot(earlier, hot.astype(BF16), preferred_element_type=F32)
    rank = jnp.sum(counts * hot, axis=-1, keepdims=True).astype(jnp.int32)
    place[...] = (col & 1) * SLOTS + (col >> 1) * CAP + rank
    hot_t = jnp.where(row == lax.broadcasted_iota(jnp.int32, (16, TOK), 0), 1.0, 0.0)
    later = jnp.where(down < across, 1.0, 0.0).astype(BF16)
    counts_t = jnp.dot(hot_t.astype(BF16), later, preferred_element_type=F32)
    rank_t = jnp.sum(counts_t * hot_t, axis=0, keepdims=True).astype(jnp.int32)
    place_t = (row & 1) * SLOTS + (row >> 1) * CAP + rank_t
    slot = lax.broadcasted_iota(jnp.int32, (SLOTS, TOK), 0)
    for n, out in enumerate((out0, out1)):
        pick = jnp.where(slot + n * SLOTS == place_t, 1.0, 0.0).astype(BF16)
        out[...] = jnp.dot(pick, normed, preferred_element_type=F32).astype(BF16)


def route_call(*args):
    shapes = [((TOK, DIM), BF16), ((SLOTS, DIM), BF16), ((SLOTS, DIM), BF16)]
    shapes += [((TOK, 1), F32), ((TOK, 1), jnp.int32)]
    return pl.pallas_call(
        route_kernel,
        in_specs=[VMEM] * 5,
        out_specs=[VMEM] * 5,
        out_shape=[jax.ShapeDtypeStruct(*shape) for shape in shapes],
        compiler_params=params(16),
        cost_estimate=cost(3),
        name="route",
    )(*args)


def expert_kernel(which, rows, up, down, out, hidden):
    for at in range(0, FF, 512):
        z = jnp.dot(rows[...], up[which, :, at : at + 512], preferred_element_type=F32)
        act = 0.5 * z * (1.0 + jnp.tanh(0.7978845608028654 * (z + 0.044715 * (z * z * z))))
        hidden[:, at : at + 512] = act.astype(BF16)
    out[...] = jnp.dot(hidden[...], down[which], preferred_element_type=F32).astype(BF16)


def expert_call(which, rows, up, down):
    return pl.pallas_call(
        functools.partial(expert_kernel, which),
        in_specs=[VMEM] * 3,
        out_specs=VMEM,
        out_shape=jax.ShapeDtypeStruct((SLOTS, DIM), BF16),
        scratch_shapes=[pltpu.VMEM((SLOTS, FF), BF16)],
        compiler_params=params(30),
        cost_estimate=cost(5),
        name=f"expert_{which}",
    )(rows, up, down)


def mix_kernel(embedded, gate, place, back0, back1, out):
    slot = lax.broadcasted_iota(jnp.int32, (TOK, SLOTS), 1)
    result = None
    for n, back in enumerate((back0, back1)):
        pick = jnp.where(slot + n * SLOTS == place[...], 1.0, 0.0).astype(BF16)
        part = jnp.dot(pick, back[...], preferred_element_type=F32)
        result = part if result is None else result + part
    out[...] = (embedded[...].astype(F32) + gate[...] * result).astype(BF16)


def mix_call(*args):
    return pl.pallas_call(
        mix_kernel,
        in_specs=[VMEM] * 5,
        out_specs=VMEM,
        out_shape=jax.ShapeDtypeStruct((TOK, DIM), BF16),
        compiler_params=params(12),
        cost_estimate=cost(2),
        name="mix",
    )(*args)


def neighbours(value, axis, ahead):
    count = lax.axis_size(axis)
    pairs = [(i, i + 1) for i in range(count - 1)]
    return lax.ppermute(value, axis, pairs if ahead else [(j, i) for i, j in pairs])


def exchange(value):
    value = value.reshape(8, CAP, DIM)
    return lax.all_to_all(value, "col", 0, 0, tiled=True).reshape(SLOTS, DIM)


def local(
    scene, conv_first, conv_second, embed_weight, router_weight, expert_ids, expert_up, expert_down
):
    row, col = lax.axis_index("row"), lax.axis_index("col")
    x, high, core = row >> 2, (row >> 1) & 1, row & 1
    place = jnp.stack([row, col]).astype(jnp.int32)

    top = neighbours(scene[ROWS - 2 :], "row", True)
    bottom = neighbours(scene[:2], "row", False)
    left_own = jnp.concatenate([top[:, :2], scene[:, :2], bottom[:, :2]], axis=0)
    right_own = jnp.concatenate([top[:, -2:], scene[:, -2:], bottom[:, -2:]], axis=0)
    left = neighbours(right_own, "col", True)
    right = neighbours(left_own, "col", False)
    strip = jnp.concatenate([right, jnp.zeros((ROWS + 4, 12, CH), BF16), left], axis=1)

    w, y = embed_weight, col & 3
    w_minus, w_plus, w_high = send(w, dx=1), send(w, dx=-1), send(w, dh=1, dl=1)
    later, strip = lax.optimization_barrier((w, strip))
    quarter = lax.dynamic_slice_in_dim(later, y * 128, 128, 0)
    far, high_far = send(quarter, dx=2), send(quarter, dx=2, dh=1, dl=1)
    scene_args = (place, scene, top, bottom, strip, conv_first, conv_second)
    patches = conv_call(0, FIRST, *scene_args)
    patches, w_minus, w_plus, w_high, far, high_far = lax.optimization_barrier(
        (patches, w_minus, w_plus, w_high, far, high_far)
    )
    w_high_minus, w_high_plus = send(w_minus, dh=1, dl=1), send(w_high, dx=-1)
    fars = jnp.concatenate([far, high_far], axis=0)
    fars = (fars, send(fars, dy=1), send(fars, dy=-1), send(fars, dy=2))
    patches = conv_call(FIRST, 8 - FIRST, *scene_args, patches)
    pairs = [[i, i + 1] for i in range(0, 16, 2)]
    patches = lax.all_to_all(patches, "row", 0, 0, axis_index_groups=pairs, tiled=True)

    shards = [(a & 3) * 2 + (b & 1) for b in (high, high + 1) for a in (x, x - 1, x + 1, x + 2)]
    order = shards + [y, (y + 3) & 3, (y + 1) & 3, (y + 2) & 3, core, 1 - core]
    order = jnp.stack(order).astype(jnp.int32)
    whole = [(0, w), (1, w_minus), (2, w_plus), (4, w_high), (5, w_high_minus), (6, w_high_plus)]
    whole = [(which, [(array, 0, None)]) for which, array in whole]
    parts = [
        (which, [(array, first, 8 + n) for n, array in enumerate(fars)])
        for which, first in ((3, 0), (7, 128))
    ]
    sums = embed_call("embed_a", order, patches, whole[:4])
    own, partner = embed_call("embed_b", order, patches, parts + whole[4:], sums)
    came = send(partner, dc=1)
    embedded, out0, out1, gate, slots = route_call(
        own, came, router_weight, expert_ids.reshape(1, TOK), expert_ids.reshape(TOK, 1)
    )
    in0, in1 = exchange(out0), exchange(out1)
    back0 = exchange(expert_call(0, in0, expert_up, expert_down))
    back1 = exchange(expert_call(1, in1, expert_up, expert_down))
    return mix_call(embedded, gate, slots, back0, back1).reshape(1, 1, TOK, DIM)


def solution(mesh):
    return jax.shard_map(
        local,
        mesh=mesh,
        in_specs=(
            P("row", "col", None),
            P(),
            P(),
            P("row", None),
            P(),
            P("row", "col", None, None),
            P("col", None, None),
            P("col", None, None),
        ),
        out_specs=P("row", "col", None, None),
        check_vma=False,
    )
```

```python
import functools

import jax
import jax.numpy as jnp
from jax import lax
from jax.experimental import pallas as pl
from jax.experimental.pallas import tpu as pltpu
from jax.sharding import PartitionSpec as P

ROWS, COLS, CH = 64, 256, 128
WIDE = 272
DIM, FF, CAP, TOK = 768, 3072, 48, 256
SLOTS = 8 * CAP
STEPS = ROWS // 8
F32, BF16 = jnp.float32, jnp.bfloat16
ANY = pl.BlockSpec(memory_space=pl.ANY)
VMEM = pl.BlockSpec(memory_space=pltpu.VMEM)
SMEM = pl.BlockSpec(memory_space=pltpu.SMEM)
HBM = pl.BlockSpec(memory_space=pltpu.HBM)


def params(mib):
    return pltpu.CompilerParams(vmem_limit_bytes=mib * 2**20)


def cost(micros):
    return pl.CostEstimate(flops=int(micros * 1.15e9), bytes_accessed=0, transcendentals=0)


def hop(dx=0, dy=0, dh=0, dl=0, dc=0):
    pairs = []
    for x in range(4):
        for h in range(2):
            for c in range(2):
                for low in range(2):
                    for y in range(4):
                        here = (x * 4 + h * 2 + c) * 8 + low * 4 + y
                        there = (
                            ((x + dx) % 4 * 4 + (h + dh) % 2 * 2 + (c + dc) % 2) * 8
                            + (low + dl) % 2 * 4
                            + (y + dy) % 4
                        )
                        pairs.append((here, there))
    return pairs


def send(value, **step):
    return lax.ppermute(value, ("row", "col"), hop(**step))


def pair_weights(source, target):
    zero = jnp.zeros((CH, CH), BF16)
    for j in range(4):
        for dx in range(3):
            rows = pl.ds(j * CH, CH)
            target[rows, pl.ds(dx * 256, CH)] = source[j, dx] if j < 3 else zero
            target[rows, pl.ds(dx * 256 + CH, CH)] = source[j - 1, dx] if j > 0 else zero


def pair_conv(source, weights, pair):
    taps = jnp.concatenate([source[2 * pair + j] for j in range(4)], axis=1)
    parts = jnp.dot(taps, weights[...], preferred_element_type=F32)
    left = pltpu.roll(parts[:, 0:256], 1, 0)
    right = pltpu.roll(parts[:, 512:768], WIDE - 1, 0)
    return left + parts[:, 256:512] + right


def conv_kernel(
    place, scene, top, bottom, strip, first, second, patches,
    block, hidden, rows, w1, w2, first_in, second_in, sems, weight_sems,
):
    step = pl.program_id(0)
    chunks = []
    for k in range(STEPS):
        lo, hi = (0, 12) if k == 0 else (4 + 8 * k, 12 + 8 * k)
        a, b = max(lo - 2, 0), min(hi - 2, ROWS)
        copies = [(scene.at[a:b], block.at[a + 2 : b + 2, 0:COLS])]
        if k == 0:
            copies.append((top, block.at[0:2, 0:COLS]))
        if k == STEPS - 1:
            copies.append((bottom, block.at[ROWS + 2 : ROWS + 4, 0:COLS]))
        copies.append((strip.at[lo:hi], block.at[lo:hi, COLS:WIDE]))
        chunks.append(
            [pltpu.make_async_copy(s, d, sems.at[k, n]) for n, (s, d) in enumerate(copies)]
        )
    weights = [
        pltpu.make_async_copy(first, first_in, weight_sems.at[0]),
        pltpu.make_async_copy(second, second_in, weight_sems.at[1]),
    ]
    place_row, place_col = place[0], place[1]
    tail = lax.broadcasted_iota(jnp.int32, (16, 256), 0)
    cut = ((place_col == 0) & (tail >= 8)) | ((place_col == 7) & (tail < 8))
    edge = jnp.where(cut, 0.0, 1.0).astype(F32)

    def conv_first(pair):
        value = jnp.maximum(pair_conv(block, w1, pair), 0.0)
        body, ends = value[0:COLS].astype(BF16), (value[COLS:WIDE] * edge).astype(BF16)
        for i in range(2):
            hidden[2 * pair + i, 0:COLS] = body[:, i * CH : (i + 1) * CH]
            hidden[2 * pair + i, COLS:WIDE] = ends[:, i * CH : (i + 1) * CH]

    @pl.when(step == 0)
    def _():
        for chunk in [chunks[0], weights] + chunks[1:]:
            for copy in chunk:
                copy.start()
        for copy in weights:
            copy.wait()
        pair_weights(first_in, w1)
        pair_weights(second_in, w2)
        for copy in chunks[0]:
            copy.wait()
        conv_first(0)

        @pl.when(place_row == 0)
        def _():
            hidden[0] = jnp.zeros((WIDE, CH), BF16)

    for k in range(1, STEPS):

        @pl.when(step == k)
        def _(k=k):
            for copy in chunks[k]:
                copy.wait()

    for i in range(4):
        conv_first(4 * step + 1 + i)

    @pl.when((step == STEPS - 1) & (place_row == 15))
    def _():
        hidden[ROWS + 1] = jnp.zeros((WIDE, CH), BF16)

    for i in range(4):
        pair = 4 * step + i
        value = pair_conv(hidden, w2, pair)[0:COLS]
        for n in range(2):
            cells = block[2 * pair + 2 + n, 0:COLS].astype(F32)
            rows[pl.ds((2 * i + n) * COLS, COLS), :] = value[:, n * CH : (n + 1) * CH] + cells
    for dy in range(8):
        for j in range(8):
            cells = rows[pl.ds(dy * COLS + j, 32, stride=8), :]
            patches[j // 4, dy, :, pl.ds(j % 4 * CH, CH)] = cells.astype(BF16)


def conv_call(*args):
    return pl.pallas_call(
        conv_kernel,
        grid=(STEPS,),
        in_specs=[SMEM, HBM, ANY, ANY, ANY, HBM, HBM],
        out_specs=pl.BlockSpec((2, 8, 32, 512), lambda i: (0, 0, i, 0)),
        out_shape=jax.ShapeDtypeStruct((2, 8, TOK, 512), BF16),
        scratch_shapes=[
            pltpu.VMEM((ROWS + 4, WIDE, CH), BF16),
            pltpu.VMEM((ROWS + 2, WIDE, CH), BF16),
            pltpu.VMEM((8 * COLS, CH), F32),
            pltpu.VMEM((512, 768), BF16),
            pltpu.VMEM((512, 768), BF16),
            pltpu.VMEM((3, 3, CH, CH), BF16),
            pltpu.VMEM((3, 3, CH, CH), BF16),
            pltpu.SemaphoreType.DMA((STEPS, 4)),
            pltpu.SemaphoreType.DMA((2,)),
        ],
        compiler_params=params(60),
        cost_estimate=cost(20),
        name="convs",
    )(*args)


def embed_kernel(layout, has_sum, order, tokens, *refs):
    count = sum(len(parts) for _, parts in layout)
    pieces, rest = refs[:count], refs[count:]
    given, rest = (rest[0:2], rest[2:]) if has_sum else ((), rest)
    own, partner, lhs, rhs, lhs_sems, rhs_sems = rest
    copies, at = [], 0
    for n, (which, parts) in enumerate(layout):
        k = order[which]
        here = [
            pltpu.make_async_copy(
                tokens.at[order[8 + m], k], lhs.at[n, pl.ds(m * TOK, TOK)], lhs_sems.at[n, m]
            )
            for m in range(2)
        ]
        for m, (first, count) in enumerate(parts):
            target = rhs.at[n, pl.ds(first, count)]
            here.append(pltpu.make_async_copy(pieces[at], target, rhs_sems.at[n, m]))
            at += 1
        copies.append(here)
    for here in copies:
        for copy in here:
            copy.start()
    for n in range(len(layout)):
        for copy in copies[n]:
            copy.wait()
        for m, target in ((1, partner), (0, own)):
            part = jnp.dot(lhs[n, pl.ds(m * TOK, TOK)], rhs[n], preferred_element_type=F32)
            if n == 0 and not has_sum:
                target[...] = part
            elif n == 0:
                target[...] = given[m][...] + part
            else:
                target[...] += part


def embed_call(name, order, tokens, shards, sums=()):
    layout, arrays = [], []
    for which, parts in shards:
        heights = [part.shape[0] for part in parts]
        layout.append((which, [(sum(heights[:m]), count) for m, count in enumerate(heights)]))
        arrays.extend(parts)
    shape = jax.ShapeDtypeStruct((TOK, DIM), F32)
    count = len(shards)
    return pl.pallas_call(
        functools.partial(embed_kernel, layout, bool(sums)),
        in_specs=[SMEM] + [ANY] * (1 + len(arrays)) + [VMEM] * len(sums),
        out_specs=[VMEM, VMEM],
        out_shape=[shape, shape],
        scratch_shapes=[
            pltpu.VMEM((count, 2 * TOK, 512), BF16),
            pltpu.VMEM((count, 512, DIM), BF16),
            pltpu.SemaphoreType.DMA((count, 2)),
            pltpu.SemaphoreType.DMA((count, 4)),
        ],
        compiler_params=params(20),
        cost_estimate=cost(4),
        name=name,
    )(order, tokens, *arrays, *sums)


def route_kernel(own, came, router, ids_row, ids_col, embedded, out0, out1, gate, place):
    value = (own[...] + came[...]).astype(BF16)
    embedded[...] = value
    wide = value.astype(F32)
    scale = lax.rsqrt(jnp.mean(wide * wide, axis=-1, keepdims=True) + 1e-06)
    normed = (wide * scale).astype(BF16)
    scores = jnp.dot(normed, router[...], preferred_element_type=F32)
    across = lax.broadcasted_iota(jnp.int32, (TOK, TOK), 1)
    down = lax.broadcasted_iota(jnp.int32, (TOK, TOK), 0)
    col, row = ids_col[...], ids_row[...]
    hot = jnp.where(col == lax.broadcasted_iota(jnp.int32, (TOK, 16), 1), 1.0, 0.0)
    gate[...] = jax.nn.sigmoid(jnp.sum(scores * hot, axis=-1, keepdims=True))
    earlier = jnp.where(across < down, 1.0, 0.0).astype(BF16)
    counts = jnp.dot(earlier, hot.astype(BF16), preferred_element_type=F32)
    rank = jnp.sum(counts * hot, axis=-1, keepdims=True).astype(jnp.int32)
    place[...] = (col & 1) * SLOTS + (col >> 1) * CAP + rank
    hot_t = jnp.where(row == lax.broadcasted_iota(jnp.int32, (16, TOK), 0), 1.0, 0.0)
    later = jnp.where(down < across, 1.0, 0.0).astype(BF16)
    counts_t = jnp.dot(hot_t.astype(BF16), later, preferred_element_type=F32)
    rank_t = jnp.sum(counts_t * hot_t, axis=0, keepdims=True).astype(jnp.int32)
    place_t = (row & 1) * SLOTS + (row >> 1) * CAP + rank_t
    slot = lax.broadcasted_iota(jnp.int32, (SLOTS, TOK), 0)
    for n, out in enumerate((out0, out1)):
        pick = jnp.where(slot + n * SLOTS == place_t, 1.0, 0.0).astype(BF16)
        out[...] = jnp.dot(pick, normed, preferred_element_type=F32).astype(BF16)


def route_call(*args):
    shapes = [((TOK, DIM), BF16), ((SLOTS, DIM), BF16), ((SLOTS, DIM), BF16)]
    shapes += [((TOK, 1), F32), ((TOK, 1), jnp.int32)]
    return pl.pallas_call(
        route_kernel,
        in_specs=[VMEM] * 5,
        out_specs=[VMEM] * 5,
        out_shape=[jax.ShapeDtypeStruct(*shape) for shape in shapes],
        compiler_params=params(16),
        cost_estimate=cost(3),
        name="route",
    )(*args)


def expert_kernel(which, width, rows, up, down, out, up_in, down_in, sems):
    copies = []
    for n, at in enumerate(range(0, FF, width)):
        part = pl.ds(at, width)
        copies.append(
            (
                pltpu.make_async_copy(up.at[which, :, part], up_in.at[n], sems.at[0, n]),
                pltpu.make_async_copy(down.at[which, part], down_in.at[n], sems.at[1, n]),
            )
        )
    for pair in copies:
        for copy in pair:
            copy.start()
    total = None
    for n, (up_copy, down_copy) in enumerate(copies):
        up_copy.wait()
        z = jnp.dot(rows[...], up_in[n], preferred_element_type=F32)
        act = 0.5 * z * (1.0 + jnp.tanh(0.7978845608028654 * (z + 0.044715 * (z * z * z))))
        down_copy.wait()
        part = jnp.dot(act.astype(BF16), down_in[n], preferred_element_type=F32)
        total = part if total is None else total + part
    out[...] = total.astype(BF16)


def expert_call(which, rows, up, down, width=512):
    count = FF // width
    return pl.pallas_call(
        functools.partial(expert_kernel, which, width),
        in_specs=[VMEM, HBM, HBM],
        out_specs=VMEM,
        out_shape=jax.ShapeDtypeStruct((SLOTS, DIM), BF16),
        scratch_shapes=[
            pltpu.VMEM((count, DIM, width), BF16),
            pltpu.VMEM((count, width, DIM), BF16),
            pltpu.SemaphoreType.DMA((2, count)),
        ],
        compiler_params=params(56),
        cost_estimate=cost(5),
        name=f"expert_{which}",
    )(rows, up, down)


def mix_kernel(embedded, gate, place, back0, back1, out):
    slot = lax.broadcasted_iota(jnp.int32, (TOK, SLOTS), 1)
    result = None
    for n, back in enumerate((back0, back1)):
        pick = jnp.where(slot + n * SLOTS == place[...], 1.0, 0.0).astype(BF16)
        part = jnp.dot(pick, back[...], preferred_element_type=F32)
        result = part if result is None else result + part
    out[...] = (embedded[...].astype(F32) + gate[...] * result).astype(BF16)


def mix_call(*args):
    return pl.pallas_call(
        mix_kernel,
        in_specs=[VMEM] * 5,
        out_specs=VMEM,
        out_shape=jax.ShapeDtypeStruct((TOK, DIM), BF16),
        compiler_params=params(12),
        cost_estimate=cost(2),
        name="mix",
    )(*args)


def neighbours(value, axis, ahead):
    count = lax.axis_size(axis)
    pairs = [(i, i + 1) for i in range(count - 1)]
    return lax.ppermute(value, axis, pairs if ahead else [(j, i) for i, j in pairs])


def exchange(value):
    value = value.reshape(8, CAP, DIM)
    return lax.all_to_all(value, "col", 0, 0, tiled=True).reshape(SLOTS, DIM)


def local(
    scene, conv_first, conv_second, embed_weight, router_weight, expert_ids, expert_up, expert_down
):
    row, col = lax.axis_index("row"), lax.axis_index("col")
    x, high, core = row >> 2, (row >> 1) & 1, row & 1
    place = jnp.stack([row, col]).astype(jnp.int32)

    top = neighbours(scene[ROWS - 2 :], "row", True)
    bottom = neighbours(scene[:2], "row", False)
    left_own = jnp.concatenate([top[:, :2], scene[:, :2], bottom[:, :2]], axis=0)
    right_own = jnp.concatenate([top[:, -2:], scene[:, -2:], bottom[:, -2:]], axis=0)
    left = neighbours(right_own, "col", True)
    right = neighbours(left_own, "col", False)
    strip = jnp.concatenate([right, jnp.zeros((ROWS + 4, 12, CH), BF16), left], axis=1)

    w = embed_weight
    w_minus, w_plus, w_high = send(w, dx=1), send(w, dx=-1), send(w, dh=1, dl=1)
    strip, w_minus, w_plus, w_high = lax.optimization_barrier((strip, w_minus, w_plus, w_high))
    w_far, w_high_plus = send(w_minus, dx=1), send(w_high, dx=-1)
    w_high_minus = send(w_minus, dh=1, dl=1)
    patches = conv_call(place, scene, top, bottom, strip, conv_first, conv_second)
    patches, w_far, w_high_plus, w_high_minus = lax.optimization_barrier(
        (patches, w_far, w_high_plus, w_high_minus)
    )
    last = [
        send(w_high_plus[:176], dx=-1),
        send(w_high_minus[176:352], dx=1),
        send(w_far[352:], dh=1, dl=1),
    ]
    pairs = [[i, i + 1] for i in range(0, 16, 2)]
    patches = lax.all_to_all(patches, "row", 0, 0, axis_index_groups=pairs, tiled=True)

    order = [(a & 3) * 2 + (b & 1) for b in (high, high + 1) for a in (x, x - 1, x + 1, x + 2)]
    order = jnp.stack(order + [core, 1 - core]).astype(jnp.int32)
    whole = [w, w_minus, w_plus, w_far, w_high, w_high_minus, w_high_plus]
    sums = embed_call("embed_a", order, patches, [(n, [a]) for n, a in enumerate(whole)])
    own, partner = embed_call("embed_b", order, patches, [(7, last)], sums)
    came = send(partner, dc=1)
    embedded, out0, out1, gate, slots = route_call(
        own, came, router_weight, expert_ids.reshape(1, TOK), expert_ids.reshape(TOK, 1)
    )
    in0, in1 = exchange(out0), exchange(out1)
    back0 = exchange(expert_call(0, in0, expert_up, expert_down))
    back1 = exchange(expert_call(1, in1, expert_up, expert_down))
    return mix_call(embedded, gate, slots, back0, back1).reshape(1, 1, TOK, DIM)


def solution(mesh):
    return jax.shard_map(
        local,
        mesh=mesh,
        in_specs=(
            P("row", "col", None),
            P(),
            P(),
            P("row", None),
            P(),
            P("row", "col", None, None),
            P("col", None, None),
            P("col", None, None),
        ),
        out_specs=P("row", "col", None, None),
        check_vma=False,
    )
```

```python
import functools

import jax
import jax.numpy as jnp
from jax import lax
from jax.experimental import pallas as pl
from jax.experimental.pallas import tpu as pltpu
from jax.sharding import PartitionSpec as P

ROWS, COLS, CH = 64, 256, 128
WIDE = 272
DIM, FF, CAP, TOK = 768, 3072, 48, 256
SLOTS = 8 * CAP
STEPS, BAND = 4, 2
F32, BF16 = jnp.float32, jnp.bfloat16
ANY = pl.BlockSpec(memory_space=pl.ANY)
VMEM = pl.BlockSpec(memory_space=pltpu.VMEM)
SMEM = pl.BlockSpec(memory_space=pltpu.SMEM)
HBM = pl.BlockSpec(memory_space=pltpu.HBM)


def params(mib):
    return pltpu.CompilerParams(vmem_limit_bytes=mib * 2**20)


def cost(micros):
    return pl.CostEstimate(flops=int(micros * 1.15e9), bytes_accessed=0, transcendentals=0)


def hop(dx=0, dy=0, dh=0, dl=0, dc=0):
    pairs = []
    for x in range(4):
        for h in range(2):
            for c in range(2):
                for low in range(2):
                    for y in range(4):
                        here = (x * 4 + h * 2 + c) * 8 + low * 4 + y
                        there = (
                            ((x + dx) % 4 * 4 + (h + dh) % 2 * 2 + (c + dc) % 2) * 8
                            + (low + dl) % 2 * 4
                            + (y + dy) % 4
                        )
                        pairs.append((here, there))
    return pairs


def send(value, **step):
    return lax.ppermute(value, ("row", "col"), hop(**step))


def pair_weights(source, target):
    zero = jnp.zeros((CH, CH), BF16)
    for j in range(4):
        for dx in range(3):
            rows = pl.ds(j * CH, CH)
            target[rows, pl.ds(dx * 256, CH)] = source[j, dx] if j < 3 else zero
            target[rows, pl.ds(dx * 256 + CH, CH)] = source[j - 1, dx] if j > 0 else zero


def pair_conv(source, weights, pair):
    taps = jnp.concatenate([source[2 * pair + j] for j in range(4)], axis=1)
    parts = jnp.dot(taps, weights[...], preferred_element_type=F32)
    left = pltpu.roll(parts[:, 0:256], 1, 0)
    right = pltpu.roll(parts[:, 512:768], WIDE - 1, 0)
    return left + parts[:, 256:512] + right


def conv_kernel(
    place, scene, top, bottom, strip, first, second, keep, other,
    block, hidden, rows, w1, w2, first_in, second_in, sems, weight_sems,
):
    step = pl.program_id(0)
    chunks = []
    for k in range(STEPS):
        hi = 8 * BAND * (k + 1) + 4
        lo = 0 if k == 0 else hi - 8 * BAND
        a, b = max(lo - 2, 0), min(hi - 2, ROWS)
        copies = [(scene.at[a:b], block.at[a + 2 : b + 2, 0:COLS])]
        if k == 0:
            copies.append((top, block.at[0:2, 0:COLS]))
        if k == STEPS - 1:
            copies.append((bottom, block.at[ROWS + 2 : ROWS + 4, 0:COLS]))
        copies.append((strip.at[lo:hi], block.at[lo:hi, COLS:WIDE]))
        chunks.append(
            [pltpu.make_async_copy(s, d, sems.at[k, n]) for n, (s, d) in enumerate(copies)]
        )
    weights = [
        pltpu.make_async_copy(first, first_in, weight_sems.at[0]),
        pltpu.make_async_copy(second, second_in, weight_sems.at[1]),
    ]
    place_row, place_col, core = place[0], place[1], place[2]
    tail = lax.broadcasted_iota(jnp.int32, (16, 256), 0)
    cut = ((place_col == 0) & (tail >= 8)) | ((place_col == 7) & (tail < 8))
    edge = jnp.where(cut, 0.0, 1.0).astype(F32)

    def conv_first(pair):
        value = jnp.maximum(pair_conv(block, w1, pair), 0.0)
        body, ends = value[0:COLS].astype(BF16), (value[COLS:WIDE] * edge).astype(BF16)
        for i in range(2):
            hidden[2 * pair + i, 0:COLS] = body[:, i * CH : (i + 1) * CH]
            hidden[2 * pair + i, COLS:WIDE] = ends[:, i * CH : (i + 1) * CH]

    @pl.when(step == 0)
    def _():
        for chunk in (chunks[0], weights, chunks[1]):
            for copy in chunk:
                copy.start()
        for copy in weights:
            copy.wait()
        pair_weights(first_in, w1)
        pair_weights(second_in, w2)
        for copy in chunks[0]:
            copy.wait()
        conv_first(0)

        @pl.when(place_row == 0)
        def _():
            hidden[0] = jnp.zeros((WIDE, CH), BF16)

    for k in range(1, STEPS):

        @pl.when(step == k)
        def _(k=k):
            for copy in chunks[k]:
                copy.wait()
            for copy in chunks[k + 1] if k + 1 < STEPS else ():
                copy.start()

    for i in range(4 * BAND):
        conv_first(4 * BAND * step + 1 + i)

    @pl.when((step == STEPS - 1) & (place_row == 15))
    def _():
        hidden[ROWS + 1] = jnp.zeros((WIDE, CH), BF16)

    for i in range(4 * BAND):
        pair = 4 * BAND * step + i
        value = pair_conv(hidden, w2, pair)[0:COLS]
        for n in range(2):
            cells = block[2 * pair + 2 + n, 0:COLS].astype(F32)
            rows[pl.ds((2 * i + n) * COLS, COLS), :] = value[:, n * CH : (n + 1) * CH] + cells
    for line in range(8 * BAND):
        dy, at = line % 8, pl.ds(line // 8 * 32, 32)
        for j in range(4):
            low = rows[pl.ds(line * COLS + j, 32, stride=8), :]
            high = rows[pl.ds(line * COLS + 4 + j, 32, stride=8), :]
            lanes = pl.ds(j * CH, CH)
            keep[dy, at, lanes] = jnp.where(core == 0, low, high).astype(BF16)
            other[dy, at, lanes] = jnp.where(core == 0, high, low).astype(BF16)


def conv_call(*args):
    return pl.pallas_call(
        conv_kernel,
        grid=(STEPS,),
        in_specs=[SMEM, HBM, ANY, ANY, ANY, HBM, HBM],
        out_specs=[pl.BlockSpec((8, 32 * BAND, 512), lambda i: (0, i, 0))] * 2,
        out_shape=[jax.ShapeDtypeStruct((8, TOK, 512), BF16)] * 2,
        scratch_shapes=[
            pltpu.VMEM((ROWS + 4, WIDE, CH), BF16),
            pltpu.VMEM((ROWS + 2, WIDE, CH), BF16),
            pltpu.VMEM((8 * BAND * COLS, CH), F32),
            pltpu.VMEM((512, 768), BF16),
            pltpu.VMEM((512, 768), BF16),
            pltpu.VMEM((3, 3, CH, CH), BF16),
            pltpu.VMEM((3, 3, CH, CH), BF16),
            pltpu.SemaphoreType.DMA((STEPS, 4)),
            pltpu.SemaphoreType.DMA((2,)),
        ],
        compiler_params=params(56),
        cost_estimate=cost(20),
        name="convs",
    )(*args)


def embed_kernel(layout, has_sum, fetched, order, keep, came, *refs):
    count = sum(len(parts) for _, parts in layout)
    pieces, refs = refs[:count], refs[count:]
    sources, refs = refs[:fetched], refs[fetched:]
    given, refs = (refs[0:2], refs[2:]) if has_sum else ((), refs)
    own, partner, refs = refs[0], refs[1], refs[2:]
    targets, refs = refs[: 2 * fetched], refs[2 * fetched :]
    lhs, rhs, lhs_sems, rhs_sems, fetch_sems = refs
    copies, at = [], 0
    for n, (which, parts) in enumerate(layout):
        k = order[which]
        here = [
            pltpu.make_async_copy(source.at[k], lhs.at[n, pl.ds(m * TOK, TOK)], lhs_sems.at[n, m])
            for m, source in enumerate((keep, came))
        ]
        for m, (first, rows) in enumerate(parts):
            target = rhs.at[n, pl.ds(first, rows)]
            here.append(pltpu.make_async_copy(pieces[at], target, rhs_sems.at[n, m]))
            at += 1
        copies.append(here)
    fetches = [
        pltpu.make_async_copy(sources[n // 2].at[n % 2], target, fetch_sems.at[n])
        for n, target in enumerate(targets)
    ]
    for here in copies:
        for copy in here:
            copy.start()
    for copy in fetches:
        copy.start()
    for n in range(len(layout)):
        for copy in copies[n]:
            copy.wait()
        for m, target in ((1, partner), (0, own)):
            part = jnp.dot(lhs[n, pl.ds(m * TOK, TOK)], rhs[n], preferred_element_type=F32)
            if n == 0 and not has_sum:
                target[...] = part
            elif n == 0:
                target[...] = given[m][...] + part
            else:
                target[...] += part
    for copy in fetches:
        copy.wait()


def embed_call(name, order, keep, came, shards, sums=(), fetch=()):
    layout, arrays = [], []
    for which, parts in shards:
        heights = [part.shape[0] for part in parts]
        layout.append((which, [(sum(heights[:m]), rows) for m, rows in enumerate(heights)]))
        arrays.extend(parts)
    shape = jax.ShapeDtypeStruct((TOK, DIM), F32)
    halves = [jax.ShapeDtypeStruct(a.shape[1:], a.dtype) for a in fetch for _ in range(2)]
    count = len(shards)
    return pl.pallas_call(
        functools.partial(embed_kernel, layout, bool(sums), len(fetch)),
        in_specs=[SMEM] + [ANY] * (2 + len(arrays)) + [HBM] * len(fetch) + [VMEM] * len(sums),
        out_specs=[VMEM, VMEM] + [ANY] * len(halves),
        out_shape=[shape, shape] + halves,
        scratch_shapes=[
            pltpu.VMEM((count, 2 * TOK, 512), BF16),
            pltpu.VMEM((count, 512, DIM), BF16),
            pltpu.SemaphoreType.DMA((count, 2)),
            pltpu.SemaphoreType.DMA((count, 4)),
            pltpu.SemaphoreType.DMA((4,)),
        ],
        compiler_params=params(34 if fetch else 16),
        cost_estimate=cost(4),
        name=name,
    )(order, keep, came, *arrays, *fetch, *sums)


def route_kernel(own, came, router, ids_row, ids_col, embedded, out0, out1, gate, place):
    value = (own[...] + came[...]).astype(BF16)
    embedded[...] = value
    wide = value.astype(F32)
    scale = lax.rsqrt(jnp.mean(wide * wide, axis=-1, keepdims=True) + 1e-06)
    normed = (wide * scale).astype(BF16)
    scores = jnp.dot(normed, router[...], preferred_element_type=F32)
    across = lax.broadcasted_iota(jnp.int32, (TOK, TOK), 1)
    down = lax.broadcasted_iota(jnp.int32, (TOK, TOK), 0)
    col, row = ids_col[...], ids_row[...]
    hot = jnp.where(col == lax.broadcasted_iota(jnp.int32, (TOK, 16), 1), 1.0, 0.0)
    gate[...] = jax.nn.sigmoid(jnp.sum(scores * hot, axis=-1, keepdims=True))
    earlier = jnp.where(across < down, 1.0, 0.0).astype(BF16)
    counts = jnp.dot(earlier, hot.astype(BF16), preferred_element_type=F32)
    rank = jnp.sum(counts * hot, axis=-1, keepdims=True).astype(jnp.int32)
    place[...] = (col & 1) * SLOTS + (col >> 1) * CAP + rank
    hot_t = jnp.where(row == lax.broadcasted_iota(jnp.int32, (16, TOK), 0), 1.0, 0.0)
    later = jnp.where(down < across, 1.0, 0.0).astype(BF16)
    counts_t = jnp.dot(hot_t.astype(BF16), later, preferred_element_type=F32)
    rank_t = jnp.sum(counts_t * hot_t, axis=0, keepdims=True).astype(jnp.int32)
    place_t = (row & 1) * SLOTS + (row >> 1) * CAP + rank_t
    slot = lax.broadcasted_iota(jnp.int32, (SLOTS, TOK), 0)
    for n, out in enumerate((out0, out1)):
        pick = jnp.where(slot + n * SLOTS == place_t, 1.0, 0.0).astype(BF16)
        out[...] = jnp.dot(pick, normed, preferred_element_type=F32).astype(BF16)


def route_call(*args):
    shapes = [((TOK, DIM), BF16), ((SLOTS, DIM), BF16), ((SLOTS, DIM), BF16)]
    shapes += [((TOK, 1), F32), ((TOK, 1), jnp.int32)]
    return pl.pallas_call(
        route_kernel,
        in_specs=[VMEM] * 5,
        out_specs=[VMEM] * 5,
        out_shape=[jax.ShapeDtypeStruct(*shape) for shape in shapes],
        compiler_params=params(16),
        cost_estimate=cost(3),
        name="route",
    )(*args)


def expert_kernel(rows, up, down, out, hidden):
    for at in range(0, FF, 512):
        part = pl.ds(at, 512)
        z = jnp.dot(rows[...], up[:, part], preferred_element_type=F32)
        act = 0.5 * z * (1.0 + jnp.tanh(0.7978845608028654 * (z + 0.044715 * (z * z * z))))
        hidden[:, part] = act.astype(BF16)
    out[...] = jnp.dot(hidden[...], down[...], preferred_element_type=F32).astype(BF16)


def expert_call(name, rows, up, down):
    return pl.pallas_call(
        expert_kernel,
        in_specs=[VMEM] * 3,
        out_specs=VMEM,
        out_shape=jax.ShapeDtypeStruct((SLOTS, DIM), BF16),
        scratch_shapes=[pltpu.VMEM((SLOTS, FF), BF16)],
        compiler_params=params(12),
        cost_estimate=cost(5),
        name=name,
    )(rows, up, down)


def mix_kernel(embedded, gate, place, back0, back1, out):
    slot = lax.broadcasted_iota(jnp.int32, (TOK, SLOTS), 1)
    result = None
    for n, back in enumerate((back0, back1)):
        pick = jnp.where(slot + n * SLOTS == place[...], 1.0, 0.0).astype(BF16)
        part = jnp.dot(pick, back[...], preferred_element_type=F32)
        result = part if result is None else result + part
    out[...] = (embedded[...].astype(F32) + gate[...] * result).astype(BF16)


def mix_call(*args):
    return pl.pallas_call(
        mix_kernel,
        in_specs=[VMEM] * 5,
        out_specs=VMEM,
        out_shape=jax.ShapeDtypeStruct((TOK, DIM), BF16),
        compiler_params=params(12),
        cost_estimate=cost(2),
        name="mix",
    )(*args)


def neighbours(value, axis, ahead):
    count = lax.axis_size(axis)
    pairs = [(i, i + 1) for i in range(count - 1)]
    return lax.ppermute(value, axis, pairs if ahead else [(j, i) for i, j in pairs])


def columns(top, scene, bottom, first):
    return jnp.concatenate([a[:, first : first + 2] for a in (top, scene, bottom)], axis=0)


def exchange(value):
    value = value.reshape(8, CAP, DIM)
    return lax.all_to_all(value, "col", 0, 0, tiled=True).reshape(SLOTS, DIM)


def local(
    scene, conv_first, conv_second, embed_weight, router_weight, expert_ids, expert_up, expert_down
):
    row, col = lax.axis_index("row"), lax.axis_index("col")
    x, high, core = row >> 2, (row >> 1) & 1, row & 1
    place = jnp.stack([row, col, core]).astype(jnp.int32)

    top = neighbours(scene[ROWS - 2 :], "row", True)
    bottom = neighbours(scene[:2], "row", False)
    w, top, bottom = lax.optimization_barrier((embed_weight, top, bottom))
    w_minus, w_plus, w_high = send(w, dx=1), send(w, dx=-1), send(w, dh=1, dl=1)
    left = neighbours(columns(top, scene, bottom, COLS - 2), "col", True)
    right = neighbours(columns(top, scene, bottom, 0), "col", False)
    strip = jnp.concatenate([right, jnp.zeros((ROWS + 4, 12, CH), BF16), left], axis=1)
    keep, other = conv_call(place, scene, top, bottom, strip, conv_first, conv_second)
    keep, other, w_minus, w_plus, w_high = lax.optimization_barrier(
        (keep, other, w_minus, w_plus, w_high)
    )
    came = send(other, dc=1)
    w_far, w_high_plus = send(w_minus, dx=1), send(w_high, dx=-1)
    w_high_minus = send(w_minus, dh=1, dl=1)
    order = [(a & 3) * 2 + (b & 1) for b in (high, high + 1) for a in (x, x - 1, x + 1, x + 2)]
    order = jnp.stack(order).astype(jnp.int32)
    shards = [(n, [a]) for n, a in zip((0, 1, 2, 4), (w, w_minus, w_plus, w_high))]
    *sums, up0, up1, down0, down1 = embed_call(
        "embed_a", order, keep, came, shards, fetch=(expert_up, expert_down)
    )
    *sums, w_far, w_high_plus, w_high_minus = lax.optimization_barrier(
        (*sums, w_far, w_high_plus, w_high_minus)
    )
    far = [w_far, w_high_minus, w_high_plus]
    sums = embed_call(
        "embed_b", order, keep, came, [(n, [a]) for n, a in zip((3, 5, 6), far)], sums
    )
    last = [
        send(w_high_plus[:176], dx=-1),
        send(w_high_minus[176:352], dx=1),
        send(w_far[352:], dh=1, dl=1),
    ]
    own, partner = embed_call("embed_c", order, keep, came, [(7, last)], sums)
    came = send(partner, dc=1)
    embedded, out0, out1, gate, slots = route_call(
        own, came, router_weight, expert_ids.reshape(1, TOK), expert_ids.reshape(TOK, 1)
    )
    in0, in1 = exchange(out0), exchange(out1)
    back0 = exchange(expert_call("expert_0", in0, up0, down0))
    back1 = exchange(expert_call("expert_1", in1, up1, down1))
    return mix_call(embedded, gate, slots, back0, back1).reshape(1, 1, TOK, DIM)


def solution(mesh):
    return jax.shard_map(
        local,
        mesh=mesh,
        in_specs=(
            P("row", "col", None),
            P(),
            P(),
            P("row", None),
            P(),
            P("row", "col", None, None),
            P("col", None, None),
            P("col", None, None),
        ),
        out_specs=P("row", "col", None, None),
        check_vma=False,
    )
```

```python
import functools

import jax
import jax.numpy as jnp
from jax import lax
from jax.experimental import pallas as pl
from jax.experimental.pallas import tpu as pltpu
from jax.sharding import PartitionSpec as P

ROWS, COLS, CH = 64, 256, 128
WIDE = 272
DIM, FF, CAP, TOK = 768, 3072, 48, 256
SLOTS = 8 * CAP
STEPS, BAND = 2, 2
F32, BF16 = jnp.float32, jnp.bfloat16
ANY = pl.BlockSpec(memory_space=pl.ANY)
VMEM = pl.BlockSpec(memory_space=pltpu.VMEM)
SMEM = pl.BlockSpec(memory_space=pltpu.SMEM)
HBM = pl.BlockSpec(memory_space=pltpu.HBM)


def params(mib):
    return pltpu.CompilerParams(vmem_limit_bytes=mib * 2**20)


def cost(micros):
    return pl.CostEstimate(flops=int(micros * 1.15e9), bytes_accessed=0, transcendentals=0)


def hop(dx=0, dy=0, dh=0, dl=0, dc=0):
    pairs = []
    for x in range(4):
        for h in range(2):
            for c in range(2):
                for low in range(2):
                    for y in range(4):
                        here = (x * 4 + h * 2 + c) * 8 + low * 4 + y
                        there = (
                            ((x + dx) % 4 * 4 + (h + dh) % 2 * 2 + (c + dc) % 2) * 8
                            + (low + dl) % 2 * 4
                            + (y + dy) % 4
                        )
                        pairs.append((here, there))
    return pairs


def in_hbm(value):
    return pltpu.with_memory_space_constraint(value, pltpu.HBM)


def in_vmem(value):
    return pltpu.with_memory_space_constraint(value, pltpu.VMEM)


def send(value, **step):
    return lax.ppermute(value, ("row", "col"), hop(**step))


def pair_weights(source, target):
    zero = jnp.zeros((CH, CH), BF16)
    for j in range(4):
        for dx in range(3):
            rows = pl.ds(j * CH, CH)
            target[rows, pl.ds(dx * 256, CH)] = source[j, dx] if j < 3 else zero
            target[rows, pl.ds(dx * 256 + CH, CH)] = source[j - 1, dx] if j > 0 else zero


def pair_conv(source, weights, pair):
    taps = jnp.concatenate([source[2 * pair + j] for j in range(4)], axis=1)
    parts = jnp.dot(taps, weights[...], preferred_element_type=F32)
    left = pltpu.roll(parts[:, 0:256], 1, 0)
    right = pltpu.roll(parts[:, 512:768], WIDE - 1, 0)
    return left + parts[:, 256:512] + right


def conv_kernel(start, fetched, place, scene, top, bottom, strip, first, second, *refs):
    sources, refs = refs[:fetched], refs[-11 - 2 * fetched :]
    keep, other, targets, refs = refs[0], refs[1], refs[2 : 2 + 2 * fetched], refs[2 + 2 * fetched :]
    block, hidden, rows, w1, w2, first_in, second_in, sems, weight_sems = refs
    step = pl.program_id(0)
    base = start * 8 * BAND - 2
    height = 8 * BAND * STEPS + 4
    chunks = []
    for k in range(STEPS):
        hi = 8 * BAND * (k + 1) + 4
        lo = 0 if k == 0 else hi - 8 * BAND
        a, b = max(lo + base, 0), min(hi + base, ROWS)
        copies = [(scene.at[a:b], block.at[a - base : b - base, 0:COLS])]
        if lo + base < 0:
            copies.append((top, block.at[0:2, 0:COLS]))
        if hi + base > ROWS:
            copies.append((bottom, block.at[height - 2 : height, 0:COLS]))
        copies.append((strip.at[lo + base + 2 : hi + base + 2], block.at[lo:hi, COLS:WIDE]))
        chunks.append(
            [pltpu.make_async_copy(s, d, sems.at[k, n]) for n, (s, d) in enumerate(copies)]
        )
    fetches = [
        pltpu.make_async_copy(sources[n // 2].at[n % 2], target, weight_sems.at[2 + n])
        for n, target in enumerate(targets)
    ]
    weights = [
        pltpu.make_async_copy(first, first_in, weight_sems.at[0]),
        pltpu.make_async_copy(second, second_in, weight_sems.at[1]),
    ]
    place_row, place_col, core = place[0], place[1], place[2]
    tail = lax.broadcasted_iota(jnp.int32, (16, 256), 0)
    cut = ((place_col == 0) & (tail >= 8)) | ((place_col == 7) & (tail < 8))
    edge = jnp.where(cut, 0.0, 1.0).astype(F32)

    def conv_first(pair):
        value = jnp.maximum(pair_conv(block, w1, pair), 0.0)
        body, ends = value[0:COLS].astype(BF16), (value[COLS:WIDE] * edge).astype(BF16)
        for i in range(2):
            hidden[2 * pair + i, 0:COLS] = body[:, i * CH : (i + 1) * CH]
            hidden[2 * pair + i, COLS:WIDE] = ends[:, i * CH : (i + 1) * CH]

    @pl.when(step == 0)
    def _():
        for chunk in (chunks[0], weights, chunks[1]):
            for copy in chunk:
                copy.start()
        for copy in fetches:
            copy.start()
        for copy in weights:
            copy.wait()
        pair_weights(first_in, w1)
        pair_weights(second_in, w2)
        for copy in chunks[0]:
            copy.wait()
        conv_first(0)
        if start == 0:

            @pl.when(place_row == 0)
            def _():
                hidden[0] = jnp.zeros((WIDE, CH), BF16)

    for k in range(1, STEPS):

        @pl.when(step == k)
        def _(k=k):
            for copy in chunks[k]:
                copy.wait()
            for copy in chunks[k + 1] if k + 1 < STEPS else ():
                copy.start()

    for i in range(4 * BAND):
        conv_first(4 * BAND * step + 1 + i)
    if base + height > ROWS:

        @pl.when((step == STEPS - 1) & (place_row == 15))
        def _():
            hidden[height - 3] = jnp.zeros((WIDE, CH), BF16)

    for i in range(4 * BAND):
        pair = 4 * BAND * step + i
        value = pair_conv(hidden, w2, pair)[0:COLS]
        for n in range(2):
            cells = block[2 * pair + 2 + n, 0:COLS].astype(F32)
            rows[pl.ds((2 * i + n) * COLS, COLS), :] = value[:, n * CH : (n + 1) * CH] + cells
    for line in range(8 * BAND):
        dy, at = line % 8, pl.ds(line // 8 * 32, 32)
        for j in range(4):
            low = rows[pl.ds(line * COLS + j, 32, stride=8), :]
            high = rows[pl.ds(line * COLS + 4 + j, 32, stride=8), :]
            lanes = pl.ds(j * CH, CH)
            keep[dy, at, lanes] = jnp.where(core == 0, low, high).astype(BF16)
            other[dy, at, lanes] = jnp.where(core == 0, high, low).astype(BF16)


    if fetches:

        @pl.when(step == STEPS - 1)
        def _():
            for copy in fetches:
                copy.wait()


def conv_call(start, args, fetch=(), given=()):
    shape = jax.ShapeDtypeStruct((8, TOK, 512), BF16)
    halves = [pltpu.VMEM(a.shape[1:], a.dtype) for a in fetch for _ in range(2)]
    height = 8 * BAND * STEPS
    return pl.pallas_call(
        functools.partial(conv_kernel, start, len(fetch)),
        grid=(STEPS,),
        in_specs=[SMEM, HBM, ANY, ANY, ANY, HBM, HBM] + [HBM] * len(fetch) + [ANY] * len(given),
        out_specs=[pl.BlockSpec((8, 32 * BAND, 512), lambda i: (0, start + i, 0))] * 2
        + [ANY] * len(halves),
        out_shape=[shape, shape] + halves,
        scratch_shapes=[
            pltpu.VMEM((height + 4, WIDE, CH), BF16),
            pltpu.VMEM((height + 2, WIDE, CH), BF16),
            pltpu.VMEM((8 * BAND * COLS, CH), F32),
            pltpu.VMEM((512, 768), BF16),
            pltpu.VMEM((512, 768), BF16),
            pltpu.VMEM((3, 3, CH, CH), BF16),
            pltpu.VMEM((3, 3, CH, CH), BF16),
            pltpu.SemaphoreType.DMA((STEPS, 4)),
            pltpu.SemaphoreType.DMA((6,)),
        ],
        input_output_aliases={7 + len(fetch) + n: n for n in range(len(given))},
        compiler_params=params(28),
        cost_estimate=cost(11),
        name=f"convs_{start}",
    )(*args, *fetch, *given)


def embed_kernel(layout, has_sum, order, tokens, *refs):
    count = sum(len(parts) for _, parts in layout)
    pieces, refs = refs[:count], refs[count:]
    given, refs = (refs[0], refs[1:]) if has_sum else (None, refs)
    total, lhs, rhs, lhs_sems, rhs_sems = refs
    copies, at = [], 0
    for n, (which, parts) in enumerate(layout):
        here = [pltpu.make_async_copy(tokens.at[order[which]], lhs.at[n], lhs_sems.at[n])]
        for m, (first, rows) in enumerate(parts):
            target = rhs.at[n, pl.ds(first, rows)]
            here.append(pltpu.make_async_copy(pieces[at], target, rhs_sems.at[n, m]))
            at += 1
        copies.append(here)
    for here in copies:
        for copy in here:
            copy.start()
    result = given[...] if has_sum else None
    for n in range(len(layout)):
        for copy in copies[n]:
            copy.wait()
        part = jnp.dot(lhs[n], rhs[n], preferred_element_type=F32)
        result = part if result is None else result + part
    total[...] = result.astype(total.dtype)


def embed_call(name, order, tokens, shards, sums=(), dtype=F32, micros=3):
    layout, arrays = [], []
    for which, parts in shards:
        heights = [part.shape[0] for part in parts]
        layout.append((which, [(sum(heights[:m]), rows) for m, rows in enumerate(heights)]))
        arrays.extend(parts)
    count = len(shards)
    return pl.pallas_call(
        functools.partial(embed_kernel, layout, bool(sums)),
        in_specs=[SMEM] + [ANY] * (1 + len(arrays)) + [VMEM] * len(sums),
        out_specs=VMEM,
        out_shape=jax.ShapeDtypeStruct((TOK, DIM), dtype),
        scratch_shapes=[
            pltpu.VMEM((count, TOK, 512), BF16),
            pltpu.VMEM((count, 512, DIM), BF16),
            pltpu.SemaphoreType.DMA((count,)),
            pltpu.SemaphoreType.DMA((count, 4)),
        ],
        compiler_params=params(20),
        cost_estimate=cost(micros),
        name=name,
    )(order, tokens, *arrays, *sums)


def route_kernel(own, came, router, ids_row, ids_col, embedded, out0, out1, gate, place):
    value = (own[...] + came[...].astype(F32)).astype(BF16)
    embedded[...] = value
    wide = value.astype(F32)
    scale = lax.rsqrt(jnp.mean(wide * wide, axis=-1, keepdims=True) + 1e-06)
    normed = (wide * scale).astype(BF16)
    scores = jnp.dot(normed, router[...], preferred_element_type=F32)
    across = lax.broadcasted_iota(jnp.int32, (TOK, TOK), 1)
    down = lax.broadcasted_iota(jnp.int32, (TOK, TOK), 0)
    col, row = ids_col[...], ids_row[...]
    hot = jnp.where(col == lax.broadcasted_iota(jnp.int32, (TOK, 16), 1), 1.0, 0.0)
    gate[...] = jax.nn.sigmoid(jnp.sum(scores * hot, axis=-1, keepdims=True))
    earlier = jnp.where(across < down, 1.0, 0.0).astype(BF16)
    counts = jnp.dot(earlier, hot.astype(BF16), preferred_element_type=F32)
    rank = jnp.sum(counts * hot, axis=-1, keepdims=True).astype(jnp.int32)
    place[...] = (col & 1) * SLOTS + (col >> 1) * CAP + rank
    hot_t = jnp.where(row == lax.broadcasted_iota(jnp.int32, (16, TOK), 0), 1.0, 0.0)
    later = jnp.where(down < across, 1.0, 0.0).astype(BF16)
    counts_t = jnp.dot(hot_t.astype(BF16), later, preferred_element_type=F32)
    rank_t = jnp.sum(counts_t * hot_t, axis=0, keepdims=True).astype(jnp.int32)
    place_t = (row & 1) * SLOTS + (row >> 1) * CAP + rank_t
    slot = lax.broadcasted_iota(jnp.int32, (SLOTS, TOK), 0)
    for n, out in enumerate((out0, out1)):
        pick = jnp.where(slot + n * SLOTS == place_t, 1.0, 0.0).astype(BF16)
        out[...] = jnp.dot(pick, normed, preferred_element_type=F32).astype(BF16)


def route_call(*args):
    shapes = [((TOK, DIM), BF16), ((SLOTS, DIM), BF16), ((SLOTS, DIM), BF16)]
    shapes += [((TOK, 1), F32), ((TOK, 1), jnp.int32)]
    return pl.pallas_call(
        route_kernel,
        in_specs=[VMEM] * 5,
        out_specs=[VMEM] * 5,
        out_shape=[jax.ShapeDtypeStruct(*shape) for shape in shapes],
        compiler_params=params(16),
        cost_estimate=cost(3),
        name="route",
    )(*args)


def expert_kernel(rows, up, down, out, hidden):
    for at in range(0, FF, 512):
        part = pl.ds(at, 512)
        z = jnp.dot(rows[...], up[:, part], preferred_element_type=F32)
        act = 0.5 * z * (1.0 + jnp.tanh(0.7978845608028654 * (z + 0.044715 * (z * z * z))))
        hidden[:, part] = act.astype(BF16)
    out[...] = jnp.dot(hidden[...], down[...], preferred_element_type=F32).astype(BF16)


def expert_call(name, rows, up, down):
    return pl.pallas_call(
        expert_kernel,
        in_specs=[VMEM] * 3,
        out_specs=VMEM,
        out_shape=jax.ShapeDtypeStruct((SLOTS, DIM), BF16),
        scratch_shapes=[pltpu.VMEM((SLOTS, FF), BF16)],
        compiler_params=params(12),
        cost_estimate=cost(5),
        name=name,
    )(rows, up, down)


def mix_kernel(embedded, gate, place, back0, back1, out):
    slot = lax.broadcasted_iota(jnp.int32, (TOK, SLOTS), 1)
    result = None
    for n, back in enumerate((back0, back1)):
        pick = jnp.where(slot + n * SLOTS == place[...], 1.0, 0.0).astype(BF16)
        part = jnp.dot(pick, back[...], preferred_element_type=F32)
        result = part if result is None else result + part
    out[...] = (embedded[...].astype(F32) + gate[...] * result).astype(BF16)


def mix_call(*args):
    return pl.pallas_call(
        mix_kernel,
        in_specs=[VMEM] * 5,
        out_specs=VMEM,
        out_shape=jax.ShapeDtypeStruct((TOK, DIM), BF16),
        compiler_params=params(12),
        cost_estimate=cost(2),
        name="mix",
    )(*args)


def neighbours(value, axis, ahead):
    count = lax.axis_size(axis)
    pairs = [(i, i + 1) for i in range(count - 1)]
    return lax.ppermute(value, axis, pairs if ahead else [(j, i) for i, j in pairs])


def columns(top, scene, bottom, first):
    return jnp.concatenate([a[:, first : first + 2] for a in (top, scene, bottom)], axis=0)


def exchange(value):
    value = value.reshape(8, CAP, DIM)
    return lax.all_to_all(value, "col", 0, 0, tiled=True).reshape(SLOTS, DIM)


def local(
    scene, conv_first, conv_second, embed_weight, router_weight, expert_ids, expert_up, expert_down
):
    row, col = lax.axis_index("row"), lax.axis_index("col")
    x, high, core = row >> 2, (row >> 1) & 1, row & 1
    place = jnp.stack([row, col, core]).astype(jnp.int32)

    top = neighbours(scene[ROWS - 2 :], "row", True)
    bottom = neighbours(scene[:2], "row", False)
    w = embed_weight
    w_minus, w_plus, w_high = send(w, dx=1), send(w, dx=-1), send(w, dh=1, dl=1)
    left = neighbours(columns(top, scene, bottom, COLS - 2), "col", True)
    right = neighbours(columns(top, scene, bottom, 0), "col", False)
    strip = jnp.concatenate([right, jnp.zeros((ROWS + 4, 12, CH), BF16), left], axis=1)
    conv_args = (place, in_hbm(scene), top, bottom, strip, in_hbm(conv_first), in_hbm(conv_second))
    keep, other = conv_call(0, conv_args)
    keep, other, w_minus, w_plus, w_high = lax.optimization_barrier(
        (keep, other, w_minus, w_plus, w_high)
    )
    w_far, w_high_plus = send(w_minus, dx=1), send(w_high, dx=-1)
    w_high_minus = send(w_minus, dh=1, dl=1)
    keep, other, up0, up1, down0, down1 = conv_call(
        STEPS, conv_args, (in_hbm(expert_up), in_hbm(expert_down)), (keep, other)
    )
    came = send(other, dc=1)
    keep, w_far, w_high_plus, w_high_minus = lax.optimization_barrier(
        (keep, w_far, w_high_plus, w_high_minus)
    )
    last = [
        send(w_high_plus[:176], dx=-1),
        send(w_high_minus[176:352], dx=1),
        send(w_far[352:], dh=1, dl=1),
    ]
    order = [(a & 3) * 2 + (b & 1) for b in (high, high + 1) for a in (x, x - 1, x + 1, x + 2)]
    order = jnp.stack(order).astype(jnp.int32)
    shards = [w, w_minus, w_plus, w_far, w_high, w_high_minus, w_high_plus]
    shards = [(n, [a]) for n, a in enumerate(shards)]
    own = embed_call("embed_own", order, keep, shards, micros=40)
    own, came = lax.optimization_barrier((own, came))
    partner = embed_call("embed_partner", order, came, shards)
    partner = embed_call("embed_partner_last", order, came, [(7, last)], [partner], BF16)
    came = send(partner, dc=1)
    own = embed_call("embed_own_last", order, keep, [(7, last)], [own])
    embedded, out0, out1, gate, slots = route_call(
        own, came, router_weight, expert_ids.reshape(1, TOK), expert_ids.reshape(TOK, 1)
    )
    in0, in1 = exchange(out0), exchange(out1)
    back0 = exchange(expert_call("expert_0", in0, in_vmem(up0), in_vmem(down0)))
    back1 = exchange(expert_call("expert_1", in1, in_vmem(up1), in_vmem(down1)))
    return mix_call(embedded, gate, slots, back0, back1).reshape(1, 1, TOK, DIM)


def solution(mesh):
    return jax.shard_map(
        local,
        mesh=mesh,
        in_specs=(
            P("row", "col", None),
            P(),
            P(),
            P("row", None),
            P(),
            P("row", "col", None, None),
            P("col", None, None),
            P("col", None, None),
        ),
        out_specs=P("row", "col", None, None),
        check_vma=False,
    )
```

```python
import functools

import jax
import jax.numpy as jnp
from jax import lax
from jax.experimental import pallas as pl
from jax.experimental.pallas import tpu as pltpu
from jax.sharding import PartitionSpec as P

ROWS, COLS, CH = 64, 256, 128
WIDE = 272
DIM, FF, CAP, TOK = 768, 3072, 48, 256
PAIR = 2 * CAP
STEPS, BAND = 2, 2
F32, BF16 = jnp.float32, jnp.bfloat16
ANY = pl.BlockSpec(memory_space=pl.ANY)
VMEM = pl.BlockSpec(memory_space=pltpu.VMEM)
SMEM = pl.BlockSpec(memory_space=pltpu.SMEM)
HBM = pl.BlockSpec(memory_space=pltpu.HBM)


def params(mib):
    return pltpu.CompilerParams(vmem_limit_bytes=mib * 2**20)


def cost(micros):
    return pl.CostEstimate(flops=int(micros * 1.15e9), bytes_accessed=0, transcendentals=0)


def hop(dx=0, dy=0, dh=0, dl=0, dc=0):
    pairs = []
    for x in range(4):
        for h in range(2):
            for c in range(2):
                for low in range(2):
                    for y in range(4):
                        here = (x * 4 + h * 2 + c) * 8 + low * 4 + y
                        there = (
                            ((x + dx) % 4 * 4 + (h + dh) % 2 * 2 + (c + dc) % 2) * 8
                            + (low + dl) % 2 * 4
                            + (y + dy) % 4
                        )
                        pairs.append((here, there))
    return pairs


def in_hbm(value):
    return pltpu.with_memory_space_constraint(value, pltpu.HBM)


def in_vmem(value):
    return pltpu.with_memory_space_constraint(value, pltpu.VMEM)


def send(value, **step):
    return lax.ppermute(value, ("row", "col"), hop(**step))


def pair_weights(source, target):
    zero = jnp.zeros((CH, CH), BF16)
    for j in range(4):
        for dx in range(3):
            rows = pl.ds(j * CH, CH)
            target[rows, pl.ds(dx * 256, CH)] = source[j, dx] if j < 3 else zero
            target[rows, pl.ds(dx * 256 + CH, CH)] = source[j - 1, dx] if j > 0 else zero


def pair_conv(source, weights, pair):
    taps = jnp.concatenate([source[2 * pair + j] for j in range(4)], axis=1)
    parts = jnp.dot(taps, weights[...], preferred_element_type=F32)
    left = pltpu.roll(parts[:, 0:256], 1, 0)
    right = pltpu.roll(parts[:, 512:768], WIDE - 1, 0)
    return left + parts[:, 256:512] + right


def conv_kernel(start, fetched, place, scene, top, bottom, strip, first, second, *refs):
    sources, refs = refs[:fetched], refs[-11 - 2 * fetched :]
    keep, other, targets, refs = refs[0], refs[1], refs[2 : 2 + 2 * fetched], refs[2 + 2 * fetched :]
    block, hidden, rows, w1, w2, first_in, second_in, sems, weight_sems = refs
    step = pl.program_id(0)
    base = start * 8 * BAND - 2
    height = 8 * BAND * STEPS + 4
    chunks = []
    for k in range(STEPS):
        hi = 8 * BAND * (k + 1) + 4
        lo = 0 if k == 0 else hi - 8 * BAND
        a, b = max(lo + base, 0), min(hi + base, ROWS)
        copies = [(scene.at[a:b], block.at[a - base : b - base, 0:COLS])]
        if lo + base < 0:
            copies.append((top, block.at[0:2, 0:COLS]))
        if hi + base > ROWS:
            copies.append((bottom, block.at[height - 2 : height, 0:COLS]))
        copies.append((strip.at[lo + base + 2 : hi + base + 2], block.at[lo:hi, COLS:WIDE]))
        chunks.append(
            [pltpu.make_async_copy(s, d, sems.at[k, n]) for n, (s, d) in enumerate(copies)]
        )
    fetches = [
        pltpu.make_async_copy(sources[n // 2].at[n % 2], target, weight_sems.at[2 + n])
        for n, target in enumerate(targets)
    ]
    weights = [
        pltpu.make_async_copy(first, first_in, weight_sems.at[0]),
        pltpu.make_async_copy(second, second_in, weight_sems.at[1]),
    ]
    place_row, place_col, core = place[0], place[1], place[2]
    tail = lax.broadcasted_iota(jnp.int32, (16, 256), 0)
    cut = ((place_col == 0) & (tail >= 8)) | ((place_col == 7) & (tail < 8))
    edge = jnp.where(cut, 0.0, 1.0).astype(F32)

    def conv_first(pair):
        value = jnp.maximum(pair_conv(block, w1, pair), 0.0)
        body, ends = value[0:COLS].astype(BF16), (value[COLS:WIDE] * edge).astype(BF16)
        for i in range(2):
            hidden[2 * pair + i, 0:COLS] = body[:, i * CH : (i + 1) * CH]
            hidden[2 * pair + i, COLS:WIDE] = ends[:, i * CH : (i + 1) * CH]

    @pl.when(step == 0)
    def _():
        for chunk in (chunks[0], weights, chunks[1]):
            for copy in chunk:
                copy.start()
        for copy in fetches:
            copy.start()
        for copy in weights:
            copy.wait()
        pair_weights(first_in, w1)
        pair_weights(second_in, w2)
        for copy in chunks[0]:
            copy.wait()
        conv_first(0)
        if start == 0:

            @pl.when(place_row == 0)
            def _():
                hidden[0] = jnp.zeros((WIDE, CH), BF16)

    for k in range(1, STEPS):

        @pl.when(step == k)
        def _(k=k):
            for copy in chunks[k]:
                copy.wait()
            for copy in chunks[k + 1] if k + 1 < STEPS else ():
                copy.start()

    for i in range(4 * BAND):
        conv_first(4 * BAND * step + 1 + i)
    if base + height > ROWS:

        @pl.when((step == STEPS - 1) & (place_row == 15))
        def _():
            hidden[height - 3] = jnp.zeros((WIDE, CH), BF16)

    for i in range(4 * BAND):
        pair = 4 * BAND * step + i
        value = pair_conv(hidden, w2, pair)[0:COLS]
        for n in range(2):
            cells = block[2 * pair + 2 + n, 0:COLS].astype(F32)
            rows[pl.ds((2 * i + n) * COLS, COLS), :] = value[:, n * CH : (n + 1) * CH] + cells
    for line in range(8 * BAND):
        dy, at = line % 8, pl.ds(line // 8 * 32, 32)
        for j in range(4):
            low = rows[pl.ds(line * COLS + j, 32, stride=8), :]
            high = rows[pl.ds(line * COLS + 4 + j, 32, stride=8), :]
            lanes = pl.ds(j * CH, CH)
            keep[dy, at, lanes] = jnp.where(core == 0, low, high).astype(BF16)
            other[dy, at, lanes] = jnp.where(core == 0, high, low).astype(BF16)


    if fetches:

        @pl.when(step == STEPS - 1)
        def _():
            for copy in fetches:
                copy.wait()


def conv_call(start, args, fetch=(), given=()):
    shape = jax.ShapeDtypeStruct((8, TOK, 512), BF16)
    halves = [pltpu.VMEM(a.shape[1:], a.dtype) for a in fetch for _ in range(2)]
    height = 8 * BAND * STEPS
    return pl.pallas_call(
        functools.partial(conv_kernel, start, len(fetch)),
        grid=(STEPS,),
        in_specs=[SMEM, HBM, ANY, ANY, ANY, HBM, HBM] + [HBM] * len(fetch) + [ANY] * len(given),
        out_specs=[pl.BlockSpec((8, 32 * BAND, 512), lambda i: (0, start + i, 0))] * 2
        + [ANY] * len(halves),
        out_shape=[shape, shape] + halves,
        scratch_shapes=[
            pltpu.VMEM((height + 4, WIDE, CH), BF16),
            pltpu.VMEM((height + 2, WIDE, CH), BF16),
            pltpu.VMEM((8 * BAND * COLS, CH), F32),
            pltpu.VMEM((512, 768), BF16),
            pltpu.VMEM((512, 768), BF16),
            pltpu.VMEM((3, 3, CH, CH), BF16),
            pltpu.VMEM((3, 3, CH, CH), BF16),
            pltpu.SemaphoreType.DMA((STEPS, 4)),
            pltpu.SemaphoreType.DMA((6,)),
        ],
        input_output_aliases={7 + len(fetch) + n: n for n in range(len(given))},
        compiler_params=params(28),
        cost_estimate=cost(11),
        name=f"convs_{start}",
    )(*args, *fetch, *given)


def embed_kernel(layout, order, tokens, *refs):
    count = sum(len(parts) for _, parts in layout)
    pieces, given, total, whole = refs[:count], refs[count:-2], refs[-2], refs[-1]
    result = given[0][...] if given else None
    at = 0
    for which, parts in layout:
        shard = pieces[at]
        if len(parts) > 1:
            shard = whole
            for m, (first, rows) in enumerate(parts):
                whole[pl.ds(first, rows)] = pieces[at + m][...]
        at += len(parts)
        part = jnp.dot(tokens[order[which]], shard[...], preferred_element_type=F32)
        result = part if result is None else result + part
    total[...] = result.astype(total.dtype)


def embed_call(name, order, tokens, shards, sums=(), dtype=F32, micros=3):
    layout, arrays = [], []
    for which, parts in shards:
        heights = [part.shape[0] for part in parts]
        layout.append((which, [(sum(heights[:m]), rows) for m, rows in enumerate(heights)]))
        arrays.extend(parts)
    return pl.pallas_call(
        functools.partial(embed_kernel, layout),
        in_specs=[SMEM] + [VMEM] * (1 + len(arrays) + len(sums)),
        out_specs=VMEM,
        out_shape=jax.ShapeDtypeStruct((TOK, DIM), dtype),
        scratch_shapes=[pltpu.VMEM((512, DIM), BF16)],
        compiler_params=params(12),
        cost_estimate=cost(micros),
        name=name,
    )(order, tokens, *arrays, *sums)


def route_kernel(where, own, came, router, ids_row, ids_col, embedded, gate, place, *outs):
    value = (own[...] + came[...].astype(F32)).astype(BF16)
    embedded[...] = value
    wide = value.astype(F32)
    scale = lax.rsqrt(jnp.mean(wide * wide, axis=-1, keepdims=True) + 1e-06)
    normed = (wide * scale).astype(BF16)
    scores = lax.dot_general(
        normed, router[...], (((1,), (1,)), ((), ())), preferred_element_type=F32
    )
    across = lax.broadcasted_iota(jnp.int32, (TOK, TOK), 1)
    down = lax.broadcasted_iota(jnp.int32, (TOK, TOK), 0)
    col, row, me = ids_col[...], ids_row[...], where[1]
    hot = jnp.where(col == lax.broadcasted_iota(jnp.int32, (TOK, 16), 1), 1.0, 0.0)
    gate[...] = jax.nn.sigmoid(jnp.sum(scores * hot, axis=-1, keepdims=True))
    earlier = jnp.where(across < down, 1.0, 0.0).astype(BF16)
    counts = jnp.dot(earlier, hot.astype(BF16), preferred_element_type=F32)
    rank = jnp.sum(counts * hot, axis=-1, keepdims=True).astype(jnp.int32)
    place[...] = ((col >> 1) ^ me) * PAIR + (col & 1) * CAP + rank
    hot_t = jnp.where(row == lax.broadcasted_iota(jnp.int32, (16, TOK), 0), 1.0, 0.0)
    later = jnp.where(down < across, 1.0, 0.0).astype(BF16)
    counts_t = jnp.dot(hot_t.astype(BF16), later, preferred_element_type=F32)
    rank_t = jnp.sum(counts_t * hot_t, axis=0, keepdims=True).astype(jnp.int32)
    place_t = ((row >> 1) ^ me) * PAIR + (row & 1) * CAP + rank_t
    slot = lax.broadcasted_iota(jnp.int32, (8 * PAIR, TOK), 0)
    pick = jnp.where(slot == place_t, 1.0, 0.0).astype(BF16)
    slots = jnp.dot(pick, normed, preferred_element_type=F32).astype(BF16)
    for k, out in enumerate(outs):
        out[...] = slots[k * PAIR : (k + 1) * PAIR]


def route_call(*args):
    shapes = [((TOK, DIM), BF16), ((TOK, 1), F32), ((TOK, 1), jnp.int32)]
    shapes += [((PAIR, DIM), BF16)] * 8
    return pl.pallas_call(
        route_kernel,
        in_specs=[SMEM] + [VMEM] * 5,
        out_specs=[VMEM] * 11,
        out_shape=[jax.ShapeDtypeStruct(*shape) for shape in shapes],
        compiler_params=params(16),
        cost_estimate=cost(3),
        name="route",
    )(*args)


def expert_kernel(*refs):
    count = (len(refs) - 5) // 2
    arrays, weights, outs, hidden = refs[:count], refs[count : count + 4], refs[count + 4 : -1], refs[-1]
    for e in range(2):
        up, down = weights[e], weights[2 + e]
        rows = jnp.concatenate([a[e * CAP : (e + 1) * CAP] for a in arrays], axis=0)
        for at in range(0, FF, 512):
            part = pl.ds(at, 512)
            z = jnp.dot(rows, up[:, part], preferred_element_type=F32)
            act = 0.5 * z * (1.0 + jnp.tanh(0.7978845608028654 * (z + 0.044715 * (z * z * z))))
            hidden[:, part] = act.astype(BF16)
        result = jnp.dot(hidden[...], down[...], preferred_element_type=F32).astype(BF16)
        for n, out in enumerate(outs):
            out[e * CAP : (e + 1) * CAP] = result[n * CAP : (n + 1) * CAP]


def expert_call(name, arrays, weights):
    count = len(arrays)
    return pl.pallas_call(
        expert_kernel,
        in_specs=[VMEM] * (count + 4),
        out_specs=[VMEM] * count,
        out_shape=[jax.ShapeDtypeStruct((PAIR, DIM), BF16)] * count,
        scratch_shapes=[pltpu.VMEM((count * CAP, FF), BF16)],
        compiler_params=params(12),
        cost_estimate=cost(5),
        name=name,
    )(*arrays, *[in_vmem(a) for a in weights])


def mix_kernel(steps, *refs):
    base, gate, place, *arrays, out = refs
    slots = jnp.concatenate([a[...] for a in arrays], axis=0)
    lane = lax.broadcasted_iota(jnp.int32, (TOK, len(steps) * PAIR), 1)
    slot = lane
    for n, k in enumerate(steps):
        slot = jnp.where(lane >= n * PAIR, lane + (k - n) * PAIR, slot)
    pick = jnp.where(slot == place[...], 1.0, 0.0).astype(BF16)
    result = jnp.dot(pick, slots, preferred_element_type=F32)
    out[...] = (base[...].astype(F32) + gate[...] * result).astype(out.dtype)


def mix_call(name, steps, base, gate, place, arrays, dtype, micros):
    return pl.pallas_call(
        functools.partial(mix_kernel, steps),
        in_specs=[VMEM] * (3 + len(arrays)),
        out_specs=VMEM,
        out_shape=jax.ShapeDtypeStruct((TOK, DIM), dtype),
        compiler_params=params(12),
        cost_estimate=cost(micros),
        name=name,
    )(base, gate, place, *arrays)


def neighbours(value, axis, ahead):
    count = lax.axis_size(axis)
    pairs = [(i, i + 1) for i in range(count - 1)]
    return lax.ppermute(value, axis, pairs if ahead else [(j, i) for i, j in pairs])


def columns(top, scene, bottom, first):
    return jnp.concatenate([a[:, first : first + 2] for a in (top, scene, bottom)], axis=0)


def exchange(arrays, steps):
    return [lax.ppermute(arrays[k], "col", [(i, i ^ k) for i in range(8)]) for k in steps]


def local(
    scene, conv_first, conv_second, embed_weight, router_weight, expert_ids, expert_up, expert_down
):
    row, col = lax.axis_index("row"), lax.axis_index("col")
    x, high, core = row >> 2, (row >> 1) & 1, row & 1
    place = jnp.stack([row, col, core]).astype(jnp.int32)

    top = neighbours(scene[ROWS - 2 :], "row", True)
    bottom = neighbours(scene[:2], "row", False)
    w = embed_weight
    w_minus, w_plus, w_high = send(w, dx=1), send(w, dx=-1), send(w, dh=1, dl=1)
    left = neighbours(columns(top, scene, bottom, COLS - 2), "col", True)
    right = neighbours(columns(top, scene, bottom, 0), "col", False)
    strip = jnp.concatenate([right, jnp.zeros((ROWS + 4, 12, CH), BF16), left], axis=1)
    conv_args = (place, in_hbm(scene), top, bottom, strip, in_hbm(conv_first), in_hbm(conv_second))
    keep, other = conv_call(0, conv_args)
    keep, other, w_minus, w_plus, w_high = lax.optimization_barrier(
        (keep, other, w_minus, w_plus, w_high)
    )
    w_far, w_high_plus = send(w_minus, dx=1), send(w_high, dx=-1)
    w_high_minus = send(w_minus, dh=1, dl=1)
    keep, other, up0, up1, down0, down1 = conv_call(
        STEPS, conv_args, (in_hbm(expert_up), in_hbm(expert_down)), (keep, other)
    )
    came = send(other, dc=1)
    keep, w_far, w_high_plus, w_high_minus = lax.optimization_barrier(
        (keep, w_far, w_high_plus, w_high_minus)
    )
    last = [
        send(w_high_plus[:176], dx=-1),
        send(w_high_minus[176:352], dx=1),
        send(w_far[352:], dh=1, dl=1),
    ]
    order = [(a & 3) * 2 + (b & 1) for b in (high, high + 1) for a in (x, x - 1, x + 1, x + 2)]
    order = jnp.stack(order).astype(jnp.int32)
    shards = [w, w_minus, w_plus, w_far, w_high, w_high_minus, w_high_plus]
    shards = [(n, [a]) for n, a in enumerate(shards)]
    own = embed_call("embed_own", order, keep, shards, micros=40)
    own, came = lax.optimization_barrier((own, came))
    partner = embed_call("embed_partner", order, came, shards)
    partner = embed_call("embed_partner_last", order, came, [(7, last)], [partner], BF16)
    came = send(partner, dc=1)
    own = embed_call("embed_own_last", order, keep, [(7, last)], [own])
    embedded, gate, slots, *outs = route_call(
        place, own, came, router_weight.T, expert_ids.reshape(1, TOK), expert_ids.reshape(TOK, 1)
    )
    first, second, weights = (4, 1, 3), (2, 6, 5, 7), (up0, up1, down0, down1)
    in_first, outs = lax.optimization_barrier((exchange(outs, first), outs))
    in_second = exchange(outs, second)
    back_first = expert_call("experts_first", [outs[0], *in_first], weights)
    in_second, back_first = lax.optimization_barrier((in_second, back_first))
    back = dict(zip((0, *first), back_first))
    back_first = [back[0], *exchange(back, first)]
    back = dict(zip(second, expert_call("experts_second", in_second, weights)))
    back_second = exchange(back, second)
    mixed = mix_call("mix_first", (0, *first), embedded, gate, slots, back_first, F32, 20)
    mixed = mix_call("mix_second", second, mixed, gate, slots, back_second, BF16, 2)
    return mixed.reshape(1, 1, TOK, DIM)


def solution(mesh):
    return jax.shard_map(
        local,
        mesh=mesh,
        in_specs=(
            P("row", "col", None),
            P(),
            P(),
            P("row", None),
            P(),
            P("row", "col", None, None),
            P("col", None, None),
            P("col", None, None),
        ),
        out_specs=P("row", "col", None, None),
        check_vma=False,
    )
```

```python
import functools

import jax
import jax.numpy as jnp
from jax import lax
from jax.experimental import pallas as pl
from jax.experimental.pallas import tpu as pltpu
from jax.sharding import PartitionSpec as P

ROWS, COLS, CH = 64, 256, 128
WIDE = 272
DIM, FF, CAP, TOK = 768, 3072, 48, 256
PAIR = 2 * CAP
BAND = 2
F32, BF16 = jnp.float32, jnp.bfloat16
ANY = pl.BlockSpec(memory_space=pl.ANY)
VMEM = pl.BlockSpec(memory_space=pltpu.VMEM)
SMEM = pl.BlockSpec(memory_space=pltpu.SMEM)
HBM = pl.BlockSpec(memory_space=pltpu.HBM)


def params(mib):
    return pltpu.CompilerParams(vmem_limit_bytes=mib * 2**20)


def cost(micros):
    return pl.CostEstimate(flops=int(micros * 1.15e9), bytes_accessed=0, transcendentals=0)


def hop(dx=0, dy=0, dh=0, dl=0, dc=0):
    pairs = []
    for x in range(4):
        for h in range(2):
            for c in range(2):
                for low in range(2):
                    for y in range(4):
                        here = (x * 4 + h * 2 + c) * 8 + low * 4 + y
                        there = (
                            ((x + dx) % 4 * 4 + (h + dh) % 2 * 2 + (c + dc) % 2) * 8
                            + (low + dl) % 2 * 4
                            + (y + dy) % 4
                        )
                        pairs.append((here, there))
    return pairs


def in_hbm(value):
    return pltpu.with_memory_space_constraint(value, pltpu.HBM)


def in_vmem(value):
    return pltpu.with_memory_space_constraint(value, pltpu.VMEM)


def send(value, **step):
    return lax.ppermute(value, ("row", "col"), hop(**step))


def pair_weights(source, target):
    zero = jnp.zeros((CH, CH), BF16)
    for j in range(4):
        for dx in range(3):
            rows = pl.ds(j * CH, CH)
            target[rows, pl.ds(dx * 256, CH)] = source[j, dx] if j < 3 else zero
            target[rows, pl.ds(dx * 256 + CH, CH)] = source[j - 1, dx] if j > 0 else zero


def pair_conv(source, weights, start):
    taps = jnp.concatenate([source[start + j] for j in range(4)], axis=1)
    parts = jnp.dot(taps, weights[...], preferred_element_type=F32)
    left = pltpu.roll(parts[:, 0:256], 1, 0)
    right = pltpu.roll(parts[:, 512:768], WIDE - 1, 0)
    return left + parts[:, 256:512] + right


def conv_kernel(outer, fetched, place, scene, strip, *refs):
    (top, bottom), refs = (refs[:2], refs[2:]) if outer else ((None, None), refs)
    first, second, *sources = refs[: 2 + fetched]
    keep, other, *refs = refs[-11 - 2 * fetched :]
    targets, refs = refs[: 2 * fetched], refs[2 * fetched :]
    block, hidden, rows, w1, w2, first_in, second_in, sems, weight_sems = refs
    step = pl.program_id(0)

    def arrive(a, b, at, k):
        return [
            pltpu.make_async_copy(scene.at[a:b], block.at[at : at + b - a, 0:COLS], sems.at[k, 0]),
            pltpu.make_async_copy(
                strip.at[a:b], block.at[at : at + b - a, COLS:WIDE], sems.at[k, 1]
            ),
        ]

    if outer:
        chunks = [arrive(0, 18, 2, 0), arrive(ROWS - 18, ROWS, 20, 1)]
        chunks[0].append(pltpu.make_async_copy(top, block.at[0:2], sems.at[0, 2]))
        chunks[1].append(pltpu.make_async_copy(bottom, block.at[38:40], sems.at[1, 2]))
    else:
        chunks = [arrive(14, 34, 0, 0), arrive(34, 50, 20, 1)]
    weights = [
        pltpu.make_async_copy(first, first_in, weight_sems.at[0]),
        pltpu.make_async_copy(second, second_in, weight_sems.at[1]),
    ]
    fetches = [
        pltpu.make_async_copy(sources[n // 2].at[n % 2], target, weight_sems.at[2 + n])
        for n, target in enumerate(targets)
    ]
    place_row, place_col, core = place[0], place[1], place[2]
    tail = lax.broadcasted_iota(jnp.int32, (16, 256), 0)
    cut = ((place_col == 0) & (tail >= 8)) | ((place_col == 7) & (tail < 8))
    edge = jnp.where(cut, 0.0, 1.0).astype(F32)

    def conv_first(start, target):
        value = jnp.maximum(pair_conv(block, w1, start), 0.0)
        body, ends = value[0:COLS].astype(BF16), (value[COLS:WIDE] * edge).astype(BF16)
        for i in range(2):
            hidden[target + i, 0:COLS] = body[:, i * CH : (i + 1) * CH]
            hidden[target + i, COLS:WIDE] = ends[:, i * CH : (i + 1) * CH]

    @pl.when(step == 0)
    def _():
        for copy in [*chunks[0], *weights, *chunks[1], *fetches]:
            copy.start()
        for copy in weights:
            copy.wait()
        pair_weights(first_in, w1)
        pair_weights(second_in, w2)
        for copy in chunks[0]:
            copy.wait()
        if not outer:
            conv_first(0, 0)

    @pl.when(step == 1)
    def _():
        for copy in chunks[1]:
            copy.wait()

    block_at, hidden_at = (20 * step, 18 * step) if outer else (16 * step, 16 * step)
    for i in range(0 if outer else 1, 4 * BAND + 1):
        conv_first(block_at + 2 * i, hidden_at + 2 * i)
    if outer:

        @pl.when((step == 0) & (place_row == 0))
        def _():
            hidden[0] = jnp.zeros((WIDE, CH), BF16)

        @pl.when((step == 1) & (place_row == 15))
        def _():
            hidden[35] = jnp.zeros((WIDE, CH), BF16)

    for i in range(4 * BAND):
        value = pair_conv(hidden, w2, hidden_at + 2 * i)[0:COLS]
        for n in range(2):
            cells = block[block_at + 2 * i + 2 + n, 0:COLS].astype(F32)
            rows[pl.ds((2 * i + n) * COLS, COLS), :] = value[:, n * CH : (n + 1) * CH] + cells
    for line in range(8 * BAND):
        dy, at = line % 8, pl.ds(line // 8 * 32, 32)
        for j in range(4):
            low = rows[pl.ds(line * COLS + j, 32, stride=8), :]
            high = rows[pl.ds(line * COLS + 4 + j, 32, stride=8), :]
            lanes = pl.ds(j * CH, CH)
            keep[dy, at, lanes] = jnp.where(core == 0, low, high).astype(BF16)
            other[dy, at, lanes] = jnp.where(core == 0, high, low).astype(BF16)
    if fetches:

        @pl.when(step == 1)
        def _():
            for copy in fetches:
                copy.wait()


def conv_call(place, scene, strip, halo, weights, fetch=(), given=()):
    outer = bool(halo)
    shape = jax.ShapeDtypeStruct((8, TOK, 512), BF16)
    halves = [pltpu.VMEM(a.shape[1:], a.dtype) for a in fetch for _ in range(2)]
    bands = pl.BlockSpec((8, 32 * BAND, 512), lambda i: (0, 3 * i if outer else 1 + i, 0))
    before = 5 + len(halo) + len(fetch)
    return pl.pallas_call(
        functools.partial(conv_kernel, outer, len(fetch)),
        grid=(2,),
        in_specs=[SMEM, HBM]
        + [ANY] * (1 + len(halo))
        + [HBM] * (2 + len(fetch))
        + [ANY] * len(given),
        out_specs=[bands, bands] + [ANY] * len(halves),
        out_shape=[shape, shape] + halves,
        scratch_shapes=[
            pltpu.VMEM((40 if outer else 36, WIDE, CH), BF16),
            pltpu.VMEM((36 if outer else 34, WIDE, CH), BF16),
            pltpu.VMEM((8 * BAND * COLS, CH), F32),
            pltpu.VMEM((512, 768), BF16),
            pltpu.VMEM((512, 768), BF16),
            pltpu.VMEM((3, 3, CH, CH), BF16),
            pltpu.VMEM((3, 3, CH, CH), BF16),
            pltpu.SemaphoreType.DMA((2, 3)),
            pltpu.SemaphoreType.DMA((6,)),
        ],
        input_output_aliases={before + n: n for n in range(len(given))},
        compiler_params=params(28),
        cost_estimate=cost(11),
        name="convs_outer" if outer else "convs_inner",
    )(place, scene, strip, *halo, *weights, *fetch, *given)


def embed_kernel(layout, order, tokens, *refs):
    count = sum(len(parts) for _, parts in layout)
    pieces, given, total, whole = refs[:count], refs[count:-2], refs[-2], refs[-1]
    result = given[0][...] if given else None
    at = 0
    for which, parts in layout:
        shard = pieces[at]
        if len(parts) > 1:
            shard = whole
            for m, (first, rows) in enumerate(parts):
                whole[pl.ds(first, rows)] = pieces[at + m][...]
        at += len(parts)
        part = jnp.dot(tokens[order[which]], shard[...], preferred_element_type=F32)
        result = part if result is None else result + part
    total[...] = result.astype(total.dtype)


def embed_call(name, order, tokens, shards, sums=(), dtype=F32, micros=3):
    layout, arrays = [], []
    for which, parts in shards:
        heights = [part.shape[0] for part in parts]
        layout.append((which, [(sum(heights[:m]), rows) for m, rows in enumerate(heights)]))
        arrays.extend(parts)
    return pl.pallas_call(
        functools.partial(embed_kernel, layout),
        in_specs=[SMEM] + [VMEM] * (1 + len(arrays) + len(sums)),
        out_specs=VMEM,
        out_shape=jax.ShapeDtypeStruct((TOK, DIM), dtype),
        scratch_shapes=[pltpu.VMEM((512, DIM), BF16)],
        compiler_params=params(12),
        cost_estimate=cost(micros),
        name=name,
    )(order, tokens, *arrays, *sums)


def route_kernel(where, own, came, router, ids_row, embedded, gate, place, *outs):
    value = (own[...] + came[...].astype(F32)).astype(BF16)
    embedded[...] = value
    wide = value.astype(F32)
    scale = lax.rsqrt(jnp.mean(wide * wide, axis=-1, keepdims=True) + 1e-06)
    normed = (wide * scale).astype(BF16)
    scores = lax.dot_general(
        normed, router[...], (((1,), (1,)), ((), ())), preferred_element_type=F32
    )
    across = lax.broadcasted_iota(jnp.int32, (TOK, TOK), 1)
    down = lax.broadcasted_iota(jnp.int32, (TOK, TOK), 0)
    row, me = ids_row[...], where[1]
    expert = lax.broadcasted_iota(jnp.int32, (16, TOK), 0)
    hot_t = jnp.where(row == expert, 1.0, 0.0)
    same = jnp.where(across == down, 1.0, 0.0).astype(BF16)
    turn = (((1,), (1,)), ((), ()))
    hot = lax.dot_general(same, hot_t.astype(BF16), turn, preferred_element_type=F32)
    gate[...] = jax.nn.sigmoid(jnp.sum(scores * hot, axis=-1, keepdims=True))
    earlier = jnp.where(across < down, 1.0, 0.0).astype(BF16)
    counts = jnp.dot(earlier, hot.astype(BF16), preferred_element_type=F32)
    number = lax.broadcasted_iota(jnp.int32, (TOK, 16), 1)
    start = ((number >> 1) ^ me) * PAIR + (number & 1) * CAP
    slots = (counts + start.astype(F32)) * hot
    place[...] = jnp.sum(slots, axis=-1, keepdims=True).astype(jnp.int32)
    later = jnp.where(down < across, 1.0, 0.0).astype(BF16)
    counts_t = jnp.dot(hot_t.astype(BF16), later, preferred_element_type=F32)
    rank_t = jnp.sum(counts_t * hot_t, axis=0, keepdims=True).astype(jnp.int32)
    place_t = ((row >> 1) ^ me) * PAIR + (row & 1) * CAP + rank_t
    slot = lax.broadcasted_iota(jnp.int32, (8 * PAIR, TOK), 0)
    pick = jnp.where(slot == place_t, 1.0, 0.0).astype(BF16)
    slots = jnp.dot(pick, normed, preferred_element_type=F32).astype(BF16)
    for k, out in enumerate(outs):
        out[...] = slots[k * PAIR : (k + 1) * PAIR]


def route_call(*args):
    shapes = [((TOK, DIM), BF16), ((TOK, 1), F32), ((TOK, 1), jnp.int32)]
    shapes += [((PAIR, DIM), BF16)] * 8
    return pl.pallas_call(
        route_kernel,
        in_specs=[SMEM] + [VMEM] * 4,
        out_specs=[VMEM] * 11,
        out_shape=[jax.ShapeDtypeStruct(*shape) for shape in shapes],
        compiler_params=params(16),
        cost_estimate=cost(3),
        name="route",
    )(*args)


def expert_kernel(*refs):
    count = (len(refs) - 5) // 2
    arrays, weights, outs, hidden = refs[:count], refs[count : count + 4], refs[count + 4 : -1], refs[-1]
    for e in range(2):
        up, down = weights[e], weights[2 + e]
        rows = jnp.concatenate([a[e * CAP : (e + 1) * CAP] for a in arrays], axis=0)
        for at in range(0, FF, 512):
            part = pl.ds(at, 512)
            z = jnp.dot(rows, up[:, part], preferred_element_type=F32)
            act = 0.5 * z * (1.0 + jnp.tanh(0.7978845608028654 * (z + 0.044715 * (z * z * z))))
            hidden[:, part] = act.astype(BF16)
        result = jnp.dot(hidden[...], down[...], preferred_element_type=F32).astype(BF16)
        for n, out in enumerate(outs):
            out[e * CAP : (e + 1) * CAP] = result[n * CAP : (n + 1) * CAP]


def expert_call(name, arrays, weights):
    count = len(arrays)
    return pl.pallas_call(
        expert_kernel,
        in_specs=[VMEM] * (count + 4),
        out_specs=[VMEM] * count,
        out_shape=[jax.ShapeDtypeStruct((PAIR, DIM), BF16)] * count,
        scratch_shapes=[pltpu.VMEM((count * CAP, FF), BF16)],
        compiler_params=params(12),
        cost_estimate=cost(5),
        name=name,
    )(*arrays, *[in_vmem(a) for a in weights])


def mix_kernel(steps, *refs):
    base, gate, place, *arrays, out = refs
    slots = jnp.concatenate([a[...] for a in arrays], axis=0)
    lane = lax.broadcasted_iota(jnp.int32, (TOK, len(steps) * PAIR), 1)
    slot = lane
    for n, k in enumerate(steps):
        slot = jnp.where(lane >= n * PAIR, lane + (k - n) * PAIR, slot)
    pick = jnp.where(slot == place[...], 1.0, 0.0).astype(BF16)
    result = jnp.dot(pick, slots, preferred_element_type=F32)
    out[...] = (base[...].astype(F32) + gate[...] * result).astype(out.dtype)


def mix_call(name, steps, base, gate, place, arrays, dtype, micros):
    return pl.pallas_call(
        functools.partial(mix_kernel, steps),
        in_specs=[VMEM] * (3 + len(arrays)),
        out_specs=VMEM,
        out_shape=jax.ShapeDtypeStruct((TOK, DIM), dtype),
        compiler_params=params(12),
        cost_estimate=cost(micros),
        name=name,
    )(base, gate, place, *arrays)


def neighbours(value, axis, ahead):
    count = lax.axis_size(axis)
    pairs = [(i, i + 1) for i in range(count - 1)]
    return lax.ppermute(value, axis, pairs if ahead else [(j, i) for i, j in pairs])


def exchange(arrays, steps):
    return [lax.ppermute(arrays[k], "col", [(i, i ^ k) for i in range(8)]) for k in steps]


def local(
    scene, conv_first, conv_second, embed_weight, router_weight, expert_ids, expert_up, expert_down
):
    row, col = lax.axis_index("row"), lax.axis_index("col")
    x, high, core = row >> 2, (row >> 1) & 1, row & 1
    place = jnp.stack([row, col, core]).astype(jnp.int32)

    w = embed_weight
    w_minus, w_plus, w_high = send(w, dx=1), send(w, dx=-1), send(w, dh=1, dl=1)
    left = neighbours(scene[:, COLS - 2 :], "col", True)
    right = neighbours(scene[:, :2], "col", False)
    strip = jnp.concatenate([right, jnp.zeros((ROWS, 12, CH), BF16), left], axis=1)
    lines = [jnp.concatenate([scene[a:b], strip[a:b]], axis=1) for a, b in ((62, 64), (0, 2))]
    halo = neighbours(lines[0], "row", True), neighbours(lines[1], "row", False)
    kernels, cells = (in_hbm(conv_first), in_hbm(conv_second)), in_hbm(scene)
    given = conv_call(place, cells, strip, (), kernels)
    *given, w_minus, w_plus, w_high = lax.optimization_barrier((*given, w_minus, w_plus, w_high))
    w_far, w_high_plus = send(w_minus, dx=1), send(w_high, dx=-1)
    w_high_minus = send(w_minus, dh=1, dl=1)
    fetch = in_hbm(expert_up), in_hbm(expert_down)
    keep, other, up0, up1, down0, down1 = conv_call(
        place, cells, strip, halo, kernels, fetch, given
    )
    came = send(other, dc=1)
    keep, w_far, w_high_plus, w_high_minus = lax.optimization_barrier(
        (keep, w_far, w_high_plus, w_high_minus)
    )
    last = [
        send(w_high_plus[:176], dx=-1),
        send(w_high_minus[176:352], dx=1),
        send(w_far[352:], dh=1, dl=1),
    ]
    order = [(a & 3) * 2 + (b & 1) for b in (high, high + 1) for a in (x, x - 1, x + 1, x + 2)]
    order = jnp.stack(order).astype(jnp.int32)
    shards = [w, w_minus, w_plus, w_far, w_high, w_high_minus, w_high_plus]
    shards = [(n, [a]) for n, a in enumerate(shards)]
    own = embed_call("embed_own", order, keep, shards, micros=40)
    own, came = lax.optimization_barrier((own, came))
    partner = embed_call("embed_partner", order, came, shards)
    partner = embed_call("embed_partner_last", order, came, [(7, last)], [partner], BF16)
    came = send(partner, dc=1)
    own = embed_call("embed_own_last", order, keep, [(7, last)], [own])
    embedded, gate, slots, *outs = route_call(
        place, own, came, router_weight.T, expert_ids.reshape(1, TOK)
    )
    first, second, weights = (4, 1, 3), (2, 6, 5, 7), (up0, up1, down0, down1)
    in_first, in_second = exchange(outs, first), exchange(outs, second)
    back_first = expert_call("experts_first", [outs[0], *in_first], weights)
    in_second, back_first = lax.optimization_barrier((in_second, back_first))
    back = dict(zip((0, *first), back_first))
    back_first = [back[0], *exchange(back, first)]
    back = dict(zip(second, expert_call("experts_second", in_second, weights)))
    back_second = exchange(back, second)
    mixed = mix_call("mix_first", (0, *first), embedded, gate, slots, back_first, F32, 20)
    mixed = mix_call("mix_second", second, mixed, gate, slots, back_second, BF16, 2)
    return mixed.reshape(1, 1, TOK, DIM)


def solution(mesh):
    return jax.shard_map(
        local,
        mesh=mesh,
        in_specs=(
            P("row", "col", None),
            P(),
            P(),
            P("row", None),
            P(),
            P("row", "col", None, None),
            P("col", None, None),
            P("col", None, None),
        ),
        out_specs=P("row", "col", None, None),
        check_vma=False,
    )
```

```python
import functools

import jax
import jax.numpy as jnp
from jax import lax
from jax.experimental import pallas as pl
from jax.experimental.pallas import tpu as pltpu
from jax.sharding import PartitionSpec as P

ROWS, COLS, CH = 64, 256, 128
WIDE = 272
DIM, FF, CAP, TOK = 768, 3072, 48, 256
PAIR = 2 * CAP
STEPS, BAND = 4, 2
F32, BF16 = jnp.float32, jnp.bfloat16
ANY = pl.BlockSpec(memory_space=pl.ANY)
VMEM = pl.BlockSpec(memory_space=pltpu.VMEM)
SMEM = pl.BlockSpec(memory_space=pltpu.SMEM)
HBM = pl.BlockSpec(memory_space=pltpu.HBM)


def params(mib):
    return pltpu.CompilerParams(vmem_limit_bytes=mib * 2**20)


def cost(micros):
    return pl.CostEstimate(flops=int(micros * 1.15e9), bytes_accessed=0, transcendentals=0)


def hop(dx=0, dy=0, dh=0, dl=0, dc=0):
    pairs = []
    for x in range(4):
        for h in range(2):
            for c in range(2):
                for low in range(2):
                    for y in range(4):
                        here = (x * 4 + h * 2 + c) * 8 + low * 4 + y
                        there = (
                            ((x + dx) % 4 * 4 + (h + dh) % 2 * 2 + (c + dc) % 2) * 8
                            + (low + dl) % 2 * 4
                            + (y + dy) % 4
                        )
                        pairs.append((here, there))
    return pairs


def in_hbm(value):
    return pltpu.with_memory_space_constraint(value, pltpu.HBM)


def in_vmem(value):
    return pltpu.with_memory_space_constraint(value, pltpu.VMEM)


def send(value, **step):
    return lax.ppermute(value, ("row", "col"), hop(**step))


def pair_weights(source, target):
    zero = jnp.zeros((CH, CH), BF16)
    for j in range(4):
        for dx in range(3):
            rows = pl.ds(j * CH, CH)
            target[rows, pl.ds(dx * 256, CH)] = source[j, dx] if j < 3 else zero
            target[rows, pl.ds(dx * 256 + CH, CH)] = source[j - 1, dx] if j > 0 else zero


def pair_conv(source, weights, pair):
    taps = jnp.concatenate([source[2 * pair + j] for j in range(4)], axis=1)
    parts = jnp.dot(taps, weights[...], preferred_element_type=F32)
    left = pltpu.roll(parts[:, 0:256], 1, 0)
    right = pltpu.roll(parts[:, 512:768], WIDE - 1, 0)
    return left + parts[:, 256:512] + right


def conv_kernel(fetched, place, scene, strip, top, bottom, first, second, *refs):
    sources, (keep, other, *refs) = refs[:fetched], refs[fetched:]
    targets, refs = refs[: 2 * fetched], refs[2 * fetched :]
    block, hidden, rows, w1, w2, first_in, second_in, sems, weight_sems = refs
    step = pl.program_id(0)
    chunks = []
    for k in range(STEPS):
        hi = 8 * BAND * (k + 1) + 4
        lo = 0 if k == 0 else hi - 8 * BAND
        a, b = max(lo - 2, 0), min(hi - 2, ROWS)
        part = pl.ds(a + 2, b - a)
        copies = [
            pltpu.make_async_copy(scene.at[a:b], block.at[part, 0:COLS], sems.at[k, 0]),
            pltpu.make_async_copy(strip.at[a:b], block.at[part, COLS:WIDE], sems.at[k, 1]),
        ]
        if k == 0:
            copies.append(pltpu.make_async_copy(top, block.at[0:2], sems.at[k, 2]))
        if k == STEPS - 1:
            end = block.at[ROWS + 2 : ROWS + 4]
            copies.append(pltpu.make_async_copy(bottom, end, sems.at[k, 2]))
        chunks.append(copies)
    weights = [
        pltpu.make_async_copy(first, first_in, weight_sems.at[0]),
        pltpu.make_async_copy(second, second_in, weight_sems.at[1]),
    ]
    fetches = [
        pltpu.make_async_copy(sources[n // 2].at[n % 2], target, weight_sems.at[2 + n])
        for n, target in enumerate(targets)
    ]
    place_row, place_col, core = place[0], place[1], place[2]
    tail = lax.broadcasted_iota(jnp.int32, (16, 256), 0)
    cut = ((place_col == 0) & (tail >= 8)) | ((place_col == 7) & (tail < 8))
    edge = jnp.where(cut, 0.0, 1.0).astype(F32)

    def conv_first(pair):
        value = jnp.maximum(pair_conv(block, w1, pair), 0.0)
        body, ends = value[0:COLS].astype(BF16), (value[COLS:WIDE] * edge).astype(BF16)
        for i in range(2):
            hidden[2 * pair + i, 0:COLS] = body[:, i * CH : (i + 1) * CH]
            hidden[2 * pair + i, COLS:WIDE] = ends[:, i * CH : (i + 1) * CH]

    @pl.when(step == 0)
    def _():
        for copy in [*chunks[0], *weights, *chunks[1]]:
            copy.start()
        for copy in weights:
            copy.wait()
        pair_weights(first_in, w1)
        pair_weights(second_in, w2)
        for copy in chunks[0]:
            copy.wait()
        conv_first(0)

        @pl.when(place_row == 0)
        def _():
            hidden[0] = jnp.zeros((WIDE, CH), BF16)

    for k in range(1, STEPS):

        @pl.when(step == k)
        def _(k=k):
            for copy in chunks[k]:
                copy.wait()
            for copy in chunks[k + 1] if k + 1 < STEPS else ():
                copy.start()
            for copy in fetches if k == 1 else ():
                copy.start()

    first_pair = 4 * BAND * step
    for i in range(4 * BAND):
        conv_first(first_pair + 1 + i)

    @pl.when((step == STEPS - 1) & (place_row == 15))
    def _():
        hidden[ROWS + 1] = jnp.zeros((WIDE, CH), BF16)

    for i in range(4 * BAND):
        pair = first_pair + i
        value = pair_conv(hidden, w2, pair)[0:COLS]
        for n in range(2):
            cells = block[2 * pair + 2 + n, 0:COLS].astype(F32)
            rows[pl.ds((2 * i + n) * COLS, COLS), :] = value[:, n * CH : (n + 1) * CH] + cells
    for line in range(8 * BAND):
        dy, at = line % 8, pl.ds(line // 8 * 32, 32)
        for j in range(4):
            low = rows[pl.ds(line * COLS + j, 32, stride=8), :]
            high = rows[pl.ds(line * COLS + 4 + j, 32, stride=8), :]
            lanes = pl.ds(j * CH, CH)
            keep[dy, at, lanes] = jnp.where(core == 0, low, high).astype(BF16)
            other[dy, at, lanes] = jnp.where(core == 0, high, low).astype(BF16)
    if fetches:

        @pl.when(step == STEPS - 1)
        def _():
            for copy in fetches:
                copy.wait()


def conv_call(place, scene, strip, top, bottom, first, second, fetch):
    shape = jax.ShapeDtypeStruct((8, TOK, 512), BF16)
    halves = [pltpu.VMEM(a.shape[1:], a.dtype) for a in fetch for _ in range(2)]
    band = pl.BlockSpec((8, 32 * BAND, 512), lambda i: (0, i, 0))
    return pl.pallas_call(
        functools.partial(conv_kernel, len(fetch)),
        grid=(STEPS,),
        in_specs=[SMEM, HBM, ANY, ANY, ANY, HBM, HBM] + [HBM] * len(fetch),
        out_specs=[band, band] + [ANY] * len(halves),
        out_shape=[shape, shape] + halves,
        scratch_shapes=[
            pltpu.VMEM((ROWS + 4, WIDE, CH), BF16),
            pltpu.VMEM((ROWS + 2, WIDE, CH), BF16),
            pltpu.VMEM((8 * BAND * COLS, CH), F32),
            pltpu.VMEM((512, 768), BF16),
            pltpu.VMEM((512, 768), BF16),
            pltpu.VMEM((3, 3, CH, CH), BF16),
            pltpu.VMEM((3, 3, CH, CH), BF16),
            pltpu.SemaphoreType.DMA((STEPS, 3)),
            pltpu.SemaphoreType.DMA((6,)),
        ],
        compiler_params=params(28),
        cost_estimate=cost(20),
        name="convs",
    )(place, scene, strip, top, bottom, first, second, *fetch)


def embed_kernel(layout, order, tokens, *refs):
    count = sum(len(parts) for _, parts in layout)
    pieces, given, total, whole = refs[:count], refs[count:-2], refs[-2], refs[-1]
    result = given[0][...] if given else None
    at = 0
    for which, parts in layout:
        shard = pieces[at]
        if len(parts) > 1:
            shard = whole
            for m, (first, rows) in enumerate(parts):
                whole[pl.ds(first, rows)] = pieces[at + m][...]
        at += len(parts)
        part = jnp.dot(tokens[order[which]], shard[...], preferred_element_type=F32)
        result = part if result is None else result + part
    total[...] = result.astype(total.dtype)


def embed_call(name, order, tokens, shards, sums=(), dtype=F32, micros=3):
    layout, arrays = [], []
    for which, parts in shards:
        heights = [part.shape[0] for part in parts]
        layout.append((which, [(sum(heights[:m]), rows) for m, rows in enumerate(heights)]))
        arrays.extend(parts)
    return pl.pallas_call(
        functools.partial(embed_kernel, layout),
        in_specs=[SMEM] + [VMEM] * (1 + len(arrays) + len(sums)),
        out_specs=VMEM,
        out_shape=jax.ShapeDtypeStruct((TOK, DIM), dtype),
        scratch_shapes=[pltpu.VMEM((512, DIM), BF16)],
        compiler_params=params(12),
        cost_estimate=cost(micros),
        name=name,
    )(order, tokens, *arrays, *sums)


def route_kernel(where, own, came, router, ids_row, embedded, gate, place, *outs):
    value = (own[...] + came[...].astype(F32)).astype(BF16)
    embedded[...] = value
    wide = value.astype(F32)
    scale = lax.rsqrt(jnp.mean(wide * wide, axis=-1, keepdims=True) + 1e-06)
    normed = (wide * scale).astype(BF16)
    scores = lax.dot_general(
        normed, router[...], (((1,), (1,)), ((), ())), preferred_element_type=F32
    )
    across = lax.broadcasted_iota(jnp.int32, (TOK, TOK), 1)
    down = lax.broadcasted_iota(jnp.int32, (TOK, TOK), 0)
    row, me = ids_row[...], where[1]
    expert = lax.broadcasted_iota(jnp.int32, (16, TOK), 0)
    hot_t = jnp.where(row == expert, 1.0, 0.0)
    same = jnp.where(across == down, 1.0, 0.0).astype(BF16)
    turn = (((1,), (1,)), ((), ()))
    hot = lax.dot_general(same, hot_t.astype(BF16), turn, preferred_element_type=F32)
    gate[...] = jax.nn.sigmoid(jnp.sum(scores * hot, axis=-1, keepdims=True))
    earlier = jnp.where(across < down, 1.0, 0.0).astype(BF16)
    counts = jnp.dot(earlier, hot.astype(BF16), preferred_element_type=F32)
    number = lax.broadcasted_iota(jnp.int32, (TOK, 16), 1)
    start = ((number >> 1) ^ me) * PAIR + (number & 1) * CAP
    slots = (counts + start.astype(F32)) * hot
    place[...] = jnp.sum(slots, axis=-1, keepdims=True).astype(jnp.int32)
    later = jnp.where(down < across, 1.0, 0.0).astype(BF16)
    counts_t = jnp.dot(hot_t.astype(BF16), later, preferred_element_type=F32)
    rank_t = jnp.sum(counts_t * hot_t, axis=0, keepdims=True).astype(jnp.int32)
    place_t = ((row >> 1) ^ me) * PAIR + (row & 1) * CAP + rank_t
    slot = lax.broadcasted_iota(jnp.int32, (8 * PAIR, TOK), 0)
    pick = jnp.where(slot == place_t, 1.0, 0.0).astype(BF16)
    slots = jnp.dot(pick, normed, preferred_element_type=F32).astype(BF16)
    for k, out in enumerate(outs):
        out[...] = slots[k * PAIR : (k + 1) * PAIR]


def route_call(*args):
    shapes = [((TOK, DIM), BF16), ((TOK, 1), F32), ((TOK, 1), jnp.int32)]
    shapes += [((PAIR, DIM), BF16)] * 8
    return pl.pallas_call(
        route_kernel,
        in_specs=[SMEM] + [VMEM] * 4,
        out_specs=[VMEM] * 11,
        out_shape=[jax.ShapeDtypeStruct(*shape) for shape in shapes],
        compiler_params=params(16),
        cost_estimate=cost(3),
        name="route",
    )(*args)


def expert_kernel(*refs):
    count = (len(refs) - 5) // 2
    arrays, weights, outs, hidden = refs[:count], refs[count : count + 4], refs[count + 4 : -1], refs[-1]
    for e in range(2):
        up, down = weights[e], weights[2 + e]
        rows = jnp.concatenate([a[e * CAP : (e + 1) * CAP] for a in arrays], axis=0)
        for at in range(0, FF, 512):
            part = pl.ds(at, 512)
            z = jnp.dot(rows, up[:, part], preferred_element_type=F32)
            act = 0.5 * z * (1.0 + jnp.tanh(0.7978845608028654 * (z + 0.044715 * (z * z * z))))
            hidden[:, part] = act.astype(BF16)
        result = jnp.dot(hidden[...], down[...], preferred_element_type=F32).astype(BF16)
        for n, out in enumerate(outs):
            out[e * CAP : (e + 1) * CAP] = result[n * CAP : (n + 1) * CAP]


def expert_call(name, arrays, weights):
    count = len(arrays)
    return pl.pallas_call(
        expert_kernel,
        in_specs=[VMEM] * (count + 4),
        out_specs=[VMEM] * count,
        out_shape=[jax.ShapeDtypeStruct((PAIR, DIM), BF16)] * count,
        scratch_shapes=[pltpu.VMEM((count * CAP, FF), BF16)],
        compiler_params=params(12),
        cost_estimate=cost(5),
        name=name,
    )(*arrays, *[in_vmem(a) for a in weights])


def mix_kernel(steps, *refs):
    base, gate, place, *arrays, out = refs
    slots = jnp.concatenate([a[...] for a in arrays], axis=0)
    lane = lax.broadcasted_iota(jnp.int32, (TOK, len(steps) * PAIR), 1)
    slot = lane
    for n, k in enumerate(steps):
        slot = jnp.where(lane >= n * PAIR, lane + (k - n) * PAIR, slot)
    pick = jnp.where(slot == place[...], 1.0, 0.0).astype(BF16)
    result = jnp.dot(pick, slots, preferred_element_type=F32)
    out[...] = (base[...].astype(F32) + gate[...] * result).astype(out.dtype)


def mix_call(name, steps, base, gate, place, arrays, dtype, micros):
    return pl.pallas_call(
        functools.partial(mix_kernel, steps),
        in_specs=[VMEM] * (3 + len(arrays)),
        out_specs=VMEM,
        out_shape=jax.ShapeDtypeStruct((TOK, DIM), dtype),
        compiler_params=params(12),
        cost_estimate=cost(micros),
        name=name,
    )(base, gate, place, *arrays)


def neighbours(value, axis, ahead):
    count = lax.axis_size(axis)
    pairs = [(i, i + 1) for i in range(count - 1)]
    return lax.ppermute(value, axis, pairs if ahead else [(j, i) for i, j in pairs])


def exchange(arrays, steps):
    return [lax.ppermute(arrays[k], "col", [(i, i ^ k) for i in range(8)]) for k in steps]


def local(
    scene, conv_first, conv_second, embed_weight, router_weight, expert_ids, expert_up, expert_down
):
    row, col = lax.axis_index("row"), lax.axis_index("col")
    x, high, core = row >> 2, (row >> 1) & 1, row & 1
    place = jnp.stack([row, col, core]).astype(jnp.int32)

    w = embed_weight
    w_minus, w_plus, w_high = send(w, dx=1), send(w, dx=-1), send(w, dh=1, dl=1)
    left = neighbours(scene[:, COLS - 2 :], "col", True)
    right = neighbours(scene[:, :2], "col", False)
    strip = jnp.concatenate([right, jnp.zeros((ROWS, 12, CH), BF16), left], axis=1)
    lines = [jnp.concatenate([scene[a:b], strip[a:b]], axis=1) for a, b in ((62, 64), (0, 2))]
    top, bottom = neighbours(lines[0], "row", True), neighbours(lines[1], "row", False)
    strip, w_minus, w_plus, w_high = lax.optimization_barrier((strip, w_minus, w_plus, w_high))
    w_far, w_high_plus = send(w_minus, dx=1), send(w_high, dx=-1)
    w_high_minus = send(w_minus, dh=1, dl=1)
    keep, other, up0, up1, down0, down1 = conv_call(
        place,
        in_hbm(scene),
        strip,
        top,
        bottom,
        in_hbm(conv_first),
        in_hbm(conv_second),
        (in_hbm(expert_up), in_hbm(expert_down)),
    )
    came = send(other, dc=1)
    keep, w_far, w_high_plus, w_high_minus = lax.optimization_barrier(
        (keep, w_far, w_high_plus, w_high_minus)
    )
    last = [
        send(w_high_plus[:176], dx=-1),
        send(w_high_minus[176:352], dx=1),
        send(w_far[352:], dh=1, dl=1),
    ]
    order = [(a & 3) * 2 + (b & 1) for b in (high, high + 1) for a in (x, x - 1, x + 1, x + 2)]
    order = jnp.stack(order).astype(jnp.int32)
    shards = [w, w_minus, w_plus, w_far, w_high, w_high_minus, w_high_plus]
    shards = [(n, [a]) for n, a in enumerate(shards)]
    own = embed_call("embed_own", order, keep, shards, micros=40)
    own, came = lax.optimization_barrier((own, came))
    partner = embed_call("embed_partner", order, came, shards)
    partner = embed_call("embed_partner_last", order, came, [(7, last)], [partner], BF16)
    came = send(partner, dc=1)
    own = embed_call("embed_own_last", order, keep, [(7, last)], [own])
    embedded, gate, slots, *outs = route_call(
        place, own, came, router_weight.T, expert_ids.reshape(1, TOK)
    )
    first, second, weights = (4, 1, 3), (2, 6, 5, 7), (up0, up1, down0, down1)
    in_first, in_second = exchange(outs, first), exchange(outs, second)
    back_first = expert_call("experts_first", [outs[0], *in_first], weights)
    in_second, back_first = lax.optimization_barrier((in_second, back_first))
    back = dict(zip((0, *first), back_first))
    back_first = [back[0], *exchange(back, first)]
    back = dict(zip(second, expert_call("experts_second", in_second, weights)))
    back_second = exchange(back, second)
    mixed = mix_call("mix_first", (0, *first), embedded, gate, slots, back_first, F32, 20)
    mixed = mix_call("mix_second", second, mixed, gate, slots, back_second, BF16, 2)
    return mixed.reshape(1, 1, TOK, DIM)


def solution(mesh):
    return jax.shard_map(
        local,
        mesh=mesh,
        in_specs=(
            P("row", "col", None),
            P(),
            P(),
            P("row", None),
            P(),
            P("row", "col", None, None),
            P("col", None, None),
            P("col", None, None),
        ),
        out_specs=P("row", "col", None, None),
        check_vma=False,
    )
```

```python
import functools

import jax
import jax.numpy as jnp
from jax import lax
from jax.experimental import pallas as pl
from jax.experimental.pallas import tpu as pltpu
from jax.sharding import PartitionSpec as P

ROWS, COLS, CH = 64, 256, 128
WIDE = 272
DIM, FF, CAP, TOK = 768, 3072, 48, 256
PAIR = 2 * CAP
STEPS, BAND = 4, 2
F32, BF16 = jnp.float32, jnp.bfloat16
ANY = pl.BlockSpec(memory_space=pl.ANY)
VMEM = pl.BlockSpec(memory_space=pltpu.VMEM)
SMEM = pl.BlockSpec(memory_space=pltpu.SMEM)
HBM = pl.BlockSpec(memory_space=pltpu.HBM)


def params(mib):
    return pltpu.CompilerParams(vmem_limit_bytes=mib * 2**20)


def cost(micros):
    return pl.CostEstimate(flops=int(micros * 1.15e9), bytes_accessed=0, transcendentals=0)


def hop(dx=0, dy=0, dh=0, dl=0, dc=0):
    pairs = []
    for x in range(4):
        for h in range(2):
            for c in range(2):
                for low in range(2):
                    for y in range(4):
                        here = (x * 4 + h * 2 + c) * 8 + low * 4 + y
                        there = (
                            ((x + dx) % 4 * 4 + (h + dh) % 2 * 2 + (c + dc) % 2) * 8
                            + (low + dl) % 2 * 4
                            + (y + dy) % 4
                        )
                        pairs.append((here, there))
    return pairs


def in_hbm(value):
    return pltpu.with_memory_space_constraint(value, pltpu.HBM)


def in_vmem(value):
    return pltpu.with_memory_space_constraint(value, pltpu.VMEM)


def send(value, **step):
    return lax.ppermute(value, ("row", "col"), hop(**step))


def pair_weights(source, target):
    zero = jnp.zeros((CH, CH), BF16)
    for j in range(4):
        for dx in range(3):
            rows = pl.ds(j * CH, CH)
            target[rows, pl.ds(dx * 256, CH)] = source[j, dx] if j < 3 else zero
            target[rows, pl.ds(dx * 256 + CH, CH)] = source[j - 1, dx] if j > 0 else zero


def pair_conv(source, weights, pair):
    taps = jnp.concatenate([source[2 * pair + j] for j in range(4)], axis=1)
    parts = jnp.dot(taps, weights[...], preferred_element_type=F32)
    left = pltpu.roll(parts[:, 0:256], 1, 0)
    right = pltpu.roll(parts[:, 512:768], WIDE - 1, 0)
    return left + parts[:, 256:512] + right


def conv_kernel(fetched, place, scene, strip, top, bottom, first, second, *refs):
    sources, (keep, other, *refs) = refs[:fetched], refs[fetched:]
    targets, refs = refs[: 2 * fetched], refs[2 * fetched :]
    block, hidden, rows, w1, w2, first_in, second_in, sems, weight_sems = refs
    step = pl.program_id(0)
    chunks = []
    for k in range(STEPS):
        hi = 8 * BAND * (k + 1) + 4
        lo = 0 if k == 0 else hi - 8 * BAND
        a, b = max(lo - 2, 0), min(hi - 2, ROWS)
        part = pl.ds(a + 2, b - a)
        copies = [
            pltpu.make_async_copy(scene.at[a:b], block.at[part, 0:COLS], sems.at[k, 0]),
            pltpu.make_async_copy(strip.at[a:b], block.at[part, COLS:WIDE], sems.at[k, 1]),
        ]
        if k == 0:
            copies.append(pltpu.make_async_copy(top, block.at[0:2], sems.at[k, 2]))
        if k == STEPS - 1:
            end = block.at[ROWS + 2 : ROWS + 4]
            copies.append(pltpu.make_async_copy(bottom, end, sems.at[k, 2]))
        chunks.append(copies)
    weights = [
        pltpu.make_async_copy(first, first_in, weight_sems.at[0]),
        pltpu.make_async_copy(second, second_in, weight_sems.at[1]),
    ]
    fetches = [
        pltpu.make_async_copy(sources[n // 2].at[n % 2], target, weight_sems.at[2 + n])
        for n, target in enumerate(targets)
    ]
    place_row, place_col, core = place[0], place[1], place[2]
    tail = lax.broadcasted_iota(jnp.int32, (16, 256), 0)
    cut = ((place_col == 0) & (tail >= 8)) | ((place_col == 7) & (tail < 8))
    edge = jnp.where(cut, 0.0, 1.0).astype(F32)

    def conv_first(pair):
        value = jnp.maximum(pair_conv(block, w1, pair), 0.0)
        body, ends = value[0:COLS].astype(BF16), (value[COLS:WIDE] * edge).astype(BF16)
        for i in range(2):
            hidden[2 * pair + i, 0:COLS] = body[:, i * CH : (i + 1) * CH]
            hidden[2 * pair + i, COLS:WIDE] = ends[:, i * CH : (i + 1) * CH]

    @pl.when(step == 0)
    def _():
        for copy in [*chunks[0], *weights, *chunks[1]]:
            copy.start()
        for copy in weights:
            copy.wait()
        pair_weights(first_in, w1)
        pair_weights(second_in, w2)
        for copy in chunks[0]:
            copy.wait()
        conv_first(0)

        @pl.when(place_row == 0)
        def _():
            hidden[0] = jnp.zeros((WIDE, CH), BF16)

    for k in range(1, STEPS):

        @pl.when(step == k)
        def _(k=k):
            for copy in chunks[k]:
                copy.wait()
            for copy in chunks[k + 1] if k + 1 < STEPS else ():
                copy.start()
            for copy in fetches if k == 1 else ():
                copy.start()

    first_pair = 4 * BAND * step
    for i in range(4 * BAND):
        conv_first(first_pair + 1 + i)

    @pl.when((step == STEPS - 1) & (place_row == 15))
    def _():
        hidden[ROWS + 1] = jnp.zeros((WIDE, CH), BF16)

    for i in range(4 * BAND):
        pair = first_pair + i
        value = pair_conv(hidden, w2, pair)[0:COLS]
        for n in range(2):
            cells = block[2 * pair + 2 + n, 0:COLS].astype(F32)
            rows[pl.ds((2 * i + n) * COLS, COLS), :] = value[:, n * CH : (n + 1) * CH] + cells
    for line in range(8 * BAND):
        dy, at = line % 8, pl.ds(line // 8 * 32, 32)
        for j in range(4):
            low = rows[pl.ds(line * COLS + j, 32, stride=8), :]
            high = rows[pl.ds(line * COLS + 4 + j, 32, stride=8), :]
            lanes = pl.ds(j * CH, CH)
            keep[dy, at, lanes] = jnp.where(core == 0, low, high).astype(BF16)
            other[dy, at, lanes] = jnp.where(core == 0, high, low).astype(BF16)
    if fetches:

        @pl.when(step == STEPS - 1)
        def _():
            for copy in fetches:
                copy.wait()


def conv_call(place, scene, strip, top, bottom, first, second, fetch):
    shape = jax.ShapeDtypeStruct((8, TOK, 512), BF16)
    halves = [pltpu.VMEM(a.shape[1:], a.dtype) for a in fetch for _ in range(2)]
    band = pl.BlockSpec((8, 32 * BAND, 512), lambda i: (0, i, 0))
    return pl.pallas_call(
        functools.partial(conv_kernel, len(fetch)),
        grid=(STEPS,),
        in_specs=[SMEM, HBM, ANY, ANY, ANY, HBM, HBM] + [HBM] * len(fetch),
        out_specs=[band, band] + [ANY] * len(halves),
        out_shape=[shape, shape] + halves,
        scratch_shapes=[
            pltpu.VMEM((ROWS + 4, WIDE, CH), BF16),
            pltpu.VMEM((ROWS + 2, WIDE, CH), BF16),
            pltpu.VMEM((8 * BAND * COLS, CH), F32),
            pltpu.VMEM((512, 768), BF16),
            pltpu.VMEM((512, 768), BF16),
            pltpu.VMEM((3, 3, CH, CH), BF16),
            pltpu.VMEM((3, 3, CH, CH), BF16),
            pltpu.SemaphoreType.DMA((STEPS, 3)),
            pltpu.SemaphoreType.DMA((6,)),
        ],
        compiler_params=params(28),
        cost_estimate=cost(20),
        name="convs",
    )(place, scene, strip, top, bottom, first, second, *fetch)


def embed_kernel(layout, order, tokens, *refs):
    count = sum(len(parts) for _, parts in layout)
    pieces, given, total, whole = refs[:count], refs[count:-2], refs[-2], refs[-1]
    result = given[0][...] if given else None
    at = 0
    for which, parts in layout:
        shard = pieces[at]
        if len(parts) > 1:
            shard = whole
            for m, (first, rows) in enumerate(parts):
                whole[pl.ds(first, rows)] = pieces[at + m][...]
        at += len(parts)
        part = jnp.dot(tokens[order[which]], shard[...], preferred_element_type=F32)
        result = part if result is None else result + part
    total[...] = result.astype(total.dtype)


def embed_call(name, order, tokens, shards, sums=(), dtype=F32, micros=3):
    layout, arrays = [], []
    for which, parts in shards:
        heights = [part.shape[0] for part in parts]
        layout.append((which, [(sum(heights[:m]), rows) for m, rows in enumerate(heights)]))
        arrays.extend(parts)
    return pl.pallas_call(
        functools.partial(embed_kernel, layout),
        in_specs=[SMEM] + [VMEM] * (1 + len(arrays) + len(sums)),
        out_specs=VMEM,
        out_shape=jax.ShapeDtypeStruct((TOK, DIM), dtype),
        scratch_shapes=[pltpu.VMEM((512, DIM), BF16)],
        compiler_params=params(12),
        cost_estimate=cost(micros),
        name=name,
    )(order, tokens, *arrays, *sums)


def route_kernel(where, order, keep, own, came, router, ids_row, *refs):
    pieces, (embedded, gate, place, *outs), whole = refs[:-12], refs[-12:-1], refs[-1]
    at = 0
    for piece in pieces:
        whole[pl.ds(at, piece.shape[0])] = piece[...]
        at += piece.shape[0]
    part = jnp.dot(keep[order[7]], whole[...], preferred_element_type=F32)
    value = (own[...] + part + came[...].astype(F32)).astype(BF16)
    embedded[...] = value
    wide = value.astype(F32)
    scale = lax.rsqrt(jnp.mean(wide * wide, axis=-1, keepdims=True) + 1e-06)
    normed = (wide * scale).astype(BF16)
    scores = lax.dot_general(
        normed, router[...], (((1,), (1,)), ((), ())), preferred_element_type=F32
    )
    across = lax.broadcasted_iota(jnp.int32, (TOK, TOK), 1)
    down = lax.broadcasted_iota(jnp.int32, (TOK, TOK), 0)
    row, me = ids_row[...], where[1]
    expert = lax.broadcasted_iota(jnp.int32, (16, TOK), 0)
    hot_t = jnp.where(row == expert, 1.0, 0.0)
    same = jnp.where(across == down, 1.0, 0.0).astype(BF16)
    turn = (((1,), (1,)), ((), ()))
    hot = lax.dot_general(same, hot_t.astype(BF16), turn, preferred_element_type=F32)
    gate[...] = jax.nn.sigmoid(jnp.sum(scores * hot, axis=-1, keepdims=True))
    earlier = jnp.where(across < down, 1.0, 0.0).astype(BF16)
    counts = jnp.dot(earlier, hot.astype(BF16), preferred_element_type=F32)
    number = lax.broadcasted_iota(jnp.int32, (TOK, 16), 1)
    start = ((number >> 1) ^ me) * PAIR + (number & 1) * CAP
    slots = (counts + start.astype(F32)) * hot
    place[...] = jnp.sum(slots, axis=-1, keepdims=True).astype(jnp.int32)
    later = jnp.where(down < across, 1.0, 0.0).astype(BF16)
    counts_t = jnp.dot(hot_t.astype(BF16), later, preferred_element_type=F32)
    rank_t = jnp.sum(counts_t * hot_t, axis=0, keepdims=True).astype(jnp.int32)
    place_t = ((row >> 1) ^ me) * PAIR + (row & 1) * CAP + rank_t
    slot = lax.broadcasted_iota(jnp.int32, (8 * PAIR, TOK), 0)
    pick = jnp.where(slot == place_t, 1.0, 0.0).astype(BF16)
    slots = jnp.dot(pick, normed, preferred_element_type=F32).astype(BF16)
    for k, out in enumerate(outs):
        out[...] = slots[k * PAIR : (k + 1) * PAIR]


def route_call(*args):
    shapes = [((TOK, DIM), BF16), ((TOK, 1), F32), ((TOK, 1), jnp.int32)]
    shapes += [((PAIR, DIM), BF16)] * 8
    return pl.pallas_call(
        route_kernel,
        in_specs=[SMEM] * 2 + [VMEM] * (len(args) - 2),
        out_specs=[VMEM] * 11,
        out_shape=[jax.ShapeDtypeStruct(*shape) for shape in shapes],
        scratch_shapes=[pltpu.VMEM((512, DIM), BF16)],
        compiler_params=params(16),
        cost_estimate=cost(3),
        name="route",
    )(*args)


def expert_kernel(*refs):
    count = (len(refs) - 5) // 2
    arrays, weights, outs, hidden = refs[:count], refs[count : count + 4], refs[count + 4 : -1], refs[-1]
    for e in range(2):
        up, down = weights[e], weights[2 + e]
        rows = jnp.concatenate([a[e * CAP : (e + 1) * CAP] for a in arrays], axis=0)
        for at in range(0, FF, 512):
            part = pl.ds(at, 512)
            z = jnp.dot(rows, up[:, part], preferred_element_type=F32)
            act = 0.5 * z * (1.0 + jnp.tanh(0.7978845608028654 * (z + 0.044715 * (z * z * z))))
            hidden[:, part] = act.astype(BF16)
        result = jnp.dot(hidden[...], down[...], preferred_element_type=F32).astype(BF16)
        for n, out in enumerate(outs):
            out[e * CAP : (e + 1) * CAP] = result[n * CAP : (n + 1) * CAP]


def expert_call(name, arrays, weights):
    count = len(arrays)
    return pl.pallas_call(
        expert_kernel,
        in_specs=[VMEM] * (count + 4),
        out_specs=[VMEM] * count,
        out_shape=[jax.ShapeDtypeStruct((PAIR, DIM), BF16)] * count,
        scratch_shapes=[pltpu.VMEM((count * CAP, FF), BF16)],
        compiler_params=params(12),
        cost_estimate=cost(5),
        name=name,
    )(*arrays, *[in_vmem(a) for a in weights])


def mix_kernel(steps, *refs):
    base, gate, place, *arrays, out = refs
    slots = jnp.concatenate([a[...] for a in arrays], axis=0)
    lane = lax.broadcasted_iota(jnp.int32, (TOK, len(steps) * PAIR), 1)
    slot = lane
    for n, k in enumerate(steps):
        slot = jnp.where(lane >= n * PAIR, lane + (k - n) * PAIR, slot)
    pick = jnp.where(slot == place[...], 1.0, 0.0).astype(BF16)
    result = jnp.dot(pick, slots, preferred_element_type=F32)
    out[...] = (base[...].astype(F32) + gate[...] * result).astype(out.dtype)


def mix_call(name, steps, base, gate, place, arrays, dtype, micros):
    return pl.pallas_call(
        functools.partial(mix_kernel, steps),
        in_specs=[VMEM] * (3 + len(arrays)),
        out_specs=VMEM,
        out_shape=jax.ShapeDtypeStruct((TOK, DIM), dtype),
        compiler_params=params(12),
        cost_estimate=cost(micros),
        name=name,
    )(base, gate, place, *arrays)


def neighbours(value, axis, ahead):
    count = lax.axis_size(axis)
    pairs = [(i, i + 1) for i in range(count - 1)]
    return lax.ppermute(value, axis, pairs if ahead else [(j, i) for i, j in pairs])


def exchange(arrays, steps):
    return [lax.ppermute(arrays[k], "col", [(i, i ^ k) for i in range(8)]) for k in steps]


def local(
    scene, conv_first, conv_second, embed_weight, router_weight, expert_ids, expert_up, expert_down
):
    row, col = lax.axis_index("row"), lax.axis_index("col")
    x, high, core = row >> 2, (row >> 1) & 1, row & 1
    place = jnp.stack([row, col, core]).astype(jnp.int32)

    w = embed_weight
    w_minus, w_plus, w_high = send(w, dx=1), send(w, dx=-1), send(w, dh=1, dl=1)
    left = neighbours(scene[:, COLS - 2 :], "col", True)
    right = neighbours(scene[:, :2], "col", False)
    strip = jnp.concatenate([right, jnp.zeros((ROWS, 12, CH), BF16), left], axis=1)
    lines = [jnp.concatenate([scene[a:b], strip[a:b]], axis=1) for a, b in ((62, 64), (0, 2))]
    top, bottom = neighbours(lines[0], "row", True), neighbours(lines[1], "row", False)
    strip, w_minus, w_plus, w_high = lax.optimization_barrier((strip, w_minus, w_plus, w_high))
    w_far, w_high_plus = send(w_minus, dx=1), send(w_high, dx=-1)
    w_high_minus = send(w_minus, dh=1, dl=1)
    keep, other, up0, up1, down0, down1 = conv_call(
        place,
        in_hbm(scene),
        strip,
        top,
        bottom,
        in_hbm(conv_first),
        in_hbm(conv_second),
        (in_hbm(expert_up), in_hbm(expert_down)),
    )
    keep, w_far, w_high_plus, w_high_minus = lax.optimization_barrier(
        (keep, w_far, w_high_plus, w_high_minus)
    )
    last = (w_high_plus[:176], w_high_minus[176:352], w_far[352:])
    *last, other = lax.optimization_barrier((*last, other))
    last = [send(last[0], dx=-1), send(last[1], dx=1), send(last[2], dh=1, dl=1)]
    came = send(other, dc=1)
    order = [(a & 3) * 2 + (b & 1) for b in (high, high + 1) for a in (x, x - 1, x + 1, x + 2)]
    order = jnp.stack(order).astype(jnp.int32)
    shards = [w, w_minus, w_plus, w_far, w_high, w_high_minus, w_high_plus]
    shards = [(n, [a]) for n, a in enumerate(shards)]
    own = embed_call("embed_own", order, keep, shards, micros=40)
    own, came = lax.optimization_barrier((own, came))
    partner = embed_call("embed_partner", order, came, shards)
    partner = embed_call("embed_partner_last", order, came, [(7, last)], [partner], BF16)
    came = send(partner, dc=1)
    embedded, gate, slots, *outs = route_call(
        place, order, keep, own, came, router_weight.T, expert_ids.reshape(1, TOK), *last
    )
    first, second, weights = (4, 1, 3), (2, 6, 5, 7), (up0, up1, down0, down1)
    in_first, in_second = exchange(outs, first), exchange(outs, second)
    back_first = expert_call("experts_first", [outs[0], *in_first], weights)
    in_second, back_first = lax.optimization_barrier((in_second, back_first))
    back = dict(zip((0, *first), back_first))
    back_first = [back[0], *exchange(back, first)]
    back = dict(zip(second, expert_call("experts_second", in_second, weights)))
    back_second = exchange(back, second)
    mixed = mix_call("mix_first", (0, *first), embedded, gate, slots, back_first, F32, 20)
    mixed = mix_call("mix_second", second, mixed, gate, slots, back_second, BF16, 2)
    return mixed.reshape(1, 1, TOK, DIM)


def solution(mesh):
    return jax.shard_map(
        local,
        mesh=mesh,
        in_specs=(
            P("row", "col", None),
            P(),
            P(),
            P("row", None),
            P(),
            P("row", "col", None, None),
            P("col", None, None),
            P("col", None, None),
        ),
        out_specs=P("row", "col", None, None),
        check_vma=False,
    )
```

```python
import functools

import jax
import jax.numpy as jnp
from jax import lax
from jax.experimental import pallas as pl
from jax.experimental.pallas import tpu as pltpu
from jax.sharding import PartitionSpec as P

ROWS, COLS, CH = 64, 256, 128
WIDE = 272
DIM, FF, CAP, TOK = 768, 3072, 48, 256
PAIR = 2 * CAP
STEPS, BAND = 4, 2
F32, BF16 = jnp.float32, jnp.bfloat16
ANY = pl.BlockSpec(memory_space=pl.ANY)
VMEM = pl.BlockSpec(memory_space=pltpu.VMEM)
SMEM = pl.BlockSpec(memory_space=pltpu.SMEM)
HBM = pl.BlockSpec(memory_space=pltpu.HBM)


def params(mib):
    return pltpu.CompilerParams(vmem_limit_bytes=mib * 2**20)


def cost(micros):
    return pl.CostEstimate(flops=int(micros * 1.15e9), bytes_accessed=0, transcendentals=0)


def hop(dx=0, dy=0, dh=0, dl=0, dc=0):
    pairs = []
    for x in range(4):
        for h in range(2):
            for c in range(2):
                for low in range(2):
                    for y in range(4):
                        here = (x * 4 + h * 2 + c) * 8 + low * 4 + y
                        there = (
                            ((x + dx) % 4 * 4 + (h + dh) % 2 * 2 + (c + dc) % 2) * 8
                            + (low + dl) % 2 * 4
                            + (y + dy) % 4
                        )
                        pairs.append((here, there))
    return pairs


def in_hbm(value):
    return pltpu.with_memory_space_constraint(value, pltpu.HBM)


def in_vmem(value):
    return pltpu.with_memory_space_constraint(value, pltpu.VMEM)


def send(value, **step):
    return lax.ppermute(value, ("row", "col"), hop(**step))


def pair_weights(source, target):
    zero = jnp.zeros((CH, CH), BF16)
    for j in range(4):
        for dx in range(3):
            rows = pl.ds(j * CH, CH)
            target[rows, pl.ds(dx * 256, CH)] = source[j, dx] if j < 3 else zero
            target[rows, pl.ds(dx * 256 + CH, CH)] = source[j - 1, dx] if j > 0 else zero


def pair_conv(source, weights, pair):
    taps = jnp.concatenate([source[2 * pair + j] for j in range(4)], axis=1)
    parts = jnp.dot(taps, weights[...], preferred_element_type=F32)
    left = pltpu.roll(parts[:, 0:256], 1, 0)
    right = pltpu.roll(parts[:, 512:768], WIDE - 1, 0)
    return left + parts[:, 256:512] + right


def conv_kernel(fetched, place, scene, strip, top, bottom, first, second, *refs):
    sources, (keep, other, *refs) = refs[:fetched], refs[fetched:]
    targets, refs = refs[: 2 * fetched], refs[2 * fetched :]
    block, hidden, rows, w1, w2, first_in, second_in, sems, weight_sems = refs
    step = pl.program_id(0)
    chunks = []
    for k in range(STEPS):
        hi = 8 * BAND * (k + 1) + 4
        lo = 0 if k == 0 else hi - 8 * BAND
        a, b = max(lo - 2, 0), min(hi - 2, ROWS)
        part = pl.ds(a + 2, b - a)
        copies = [
            pltpu.make_async_copy(scene.at[a:b], block.at[part, 0:COLS], sems.at[k, 0]),
            pltpu.make_async_copy(strip.at[a:b], block.at[part, COLS:WIDE], sems.at[k, 1]),
        ]
        if k == 0:
            copies.append(pltpu.make_async_copy(top, block.at[0:2], sems.at[k, 2]))
        if k == STEPS - 1:
            end = block.at[ROWS + 2 : ROWS + 4]
            copies.append(pltpu.make_async_copy(bottom, end, sems.at[k, 2]))
        chunks.append(copies)
    weights = [
        pltpu.make_async_copy(first, first_in, weight_sems.at[0]),
        pltpu.make_async_copy(second, second_in, weight_sems.at[1]),
    ]
    fetches = [
        pltpu.make_async_copy(sources[n // 2].at[n % 2], target, weight_sems.at[2 + n])
        for n, target in enumerate(targets)
    ]
    place_row, place_col, core = place[0], place[1], place[2]
    tail = lax.broadcasted_iota(jnp.int32, (16, 256), 0)
    cut = ((place_col == 0) & (tail >= 8)) | ((place_col == 7) & (tail < 8))
    edge = jnp.where(cut, 0.0, 1.0).astype(F32)

    def conv_first(pair):
        value = jnp.maximum(pair_conv(block, w1, pair), 0.0)
        body, ends = value[0:COLS].astype(BF16), (value[COLS:WIDE] * edge).astype(BF16)
        for i in range(2):
            hidden[2 * pair + i, 0:COLS] = body[:, i * CH : (i + 1) * CH]
            hidden[2 * pair + i, COLS:WIDE] = ends[:, i * CH : (i + 1) * CH]

    @pl.when(step == 0)
    def _():
        for copy in [*weights, *chunks[0]]:
            copy.start()
        for copy in weights:
            copy.wait()
        pair_weights(first_in, w1)
        pair_weights(second_in, w2)
        for copy in chunks[0]:
            copy.wait()
        for copy in chunks[1]:
            copy.start()
        conv_first(0)

        @pl.when(place_row == 0)
        def _():
            hidden[0] = jnp.zeros((WIDE, CH), BF16)

    for k in range(1, STEPS):

        @pl.when(step == k)
        def _(k=k):
            for copy in chunks[k]:
                copy.wait()
            for copy in chunks[k + 1] if k + 1 < STEPS else ():
                copy.start()
            for copy in fetches if k == 1 else ():
                copy.start()

    first_pair = 4 * BAND * step
    for i in range(4 * BAND):
        conv_first(first_pair + 1 + i)

    @pl.when((step == STEPS - 1) & (place_row == 15))
    def _():
        hidden[ROWS + 1] = jnp.zeros((WIDE, CH), BF16)

    for i in range(4 * BAND):
        pair = first_pair + i
        value = pair_conv(hidden, w2, pair)[0:COLS]
        for n in range(2):
            cells = block[2 * pair + 2 + n, 0:COLS].astype(F32)
            rows[pl.ds((2 * i + n) * COLS, COLS), :] = value[:, n * CH : (n + 1) * CH] + cells
        for line in (2 * i, 2 * i + 1):
            dy, at = line % 8, pl.ds(line // 8 * 32, 32)
            for j in range(4):
                low = rows[pl.ds(line * COLS + j, 32, stride=8), :]
                high = rows[pl.ds(line * COLS + 4 + j, 32, stride=8), :]
                lanes = pl.ds(j * CH, CH)
                keep[dy, at, lanes] = jnp.where(core == 0, low, high).astype(BF16)
                other[dy, at, lanes] = jnp.where(core == 0, high, low).astype(BF16)
    if fetches:

        @pl.when(step == STEPS - 1)
        def _():
            for copy in fetches:
                copy.wait()


def conv_call(place, scene, strip, top, bottom, first, second, fetch):
    shape = jax.ShapeDtypeStruct((8, TOK, 512), BF16)
    halves = [pltpu.VMEM(a.shape[1:], a.dtype) for a in fetch for _ in range(2)]
    band = pl.BlockSpec((8, 32 * BAND, 512), lambda i: (0, i, 0))
    return pl.pallas_call(
        functools.partial(conv_kernel, len(fetch)),
        grid=(STEPS,),
        in_specs=[SMEM, HBM, ANY, ANY, ANY, HBM, HBM] + [HBM] * len(fetch),
        out_specs=[band, band] + [ANY] * len(halves),
        out_shape=[shape, shape] + halves,
        scratch_shapes=[
            pltpu.VMEM((ROWS + 4, WIDE, CH), BF16),
            pltpu.VMEM((ROWS + 2, WIDE, CH), BF16),
            pltpu.VMEM((8 * BAND * COLS + 16, CH), F32),
            pltpu.VMEM((512, 768), BF16),
            pltpu.VMEM((512, 768), BF16),
            pltpu.VMEM((3, 3, CH, CH), BF16),
            pltpu.VMEM((3, 3, CH, CH), BF16),
            pltpu.SemaphoreType.DMA((STEPS, 3)),
            pltpu.SemaphoreType.DMA((6,)),
        ],
        compiler_params=params(28),
        cost_estimate=cost(20),
        name="convs",
    )(place, scene, strip, top, bottom, first, second, *fetch)


def embed_kernel(layout, order, tokens, *refs):
    count = sum(len(parts) for _, parts in layout)
    pieces, given, total, whole = refs[:count], refs[count:-2], refs[-2], refs[-1]
    result = given[0][...] if given else None
    at = 0
    for which, parts in layout:
        shard = pieces[at]
        if len(parts) > 1:
            shard = whole
            for m, (first, rows) in enumerate(parts):
                whole[pl.ds(first, rows)] = pieces[at + m][...]
        at += len(parts)
        part = jnp.dot(tokens[order[which]], shard[...], preferred_element_type=F32)
        result = part if result is None else result + part
    total[...] = result.astype(total.dtype)


def embed_call(name, order, tokens, shards, sums=(), dtype=F32, micros=3):
    layout, arrays = [], []
    for which, parts in shards:
        heights = [part.shape[0] for part in parts]
        layout.append((which, [(sum(heights[:m]), rows) for m, rows in enumerate(heights)]))
        arrays.extend(parts)
    return pl.pallas_call(
        functools.partial(embed_kernel, layout),
        in_specs=[SMEM] + [VMEM] * (1 + len(arrays) + len(sums)),
        out_specs=VMEM,
        out_shape=jax.ShapeDtypeStruct((TOK, DIM), dtype),
        scratch_shapes=[pltpu.VMEM((512, DIM), BF16)],
        compiler_params=params(12),
        cost_estimate=cost(micros),
        name=name,
    )(order, tokens, *arrays, *sums)


def route_kernel(where, order, keep, own, came, router, ids_row, *refs):
    pieces, (embedded, gate, place, *outs), whole = refs[:-12], refs[-12:-1], refs[-1]
    at = 0
    for piece in pieces:
        whole[pl.ds(at, piece.shape[0])] = piece[...]
        at += piece.shape[0]
    part = jnp.dot(keep[order[7]], whole[...], preferred_element_type=F32)
    value = (own[...] + part + came[...].astype(F32)).astype(BF16)
    embedded[...] = value
    wide = value.astype(F32)
    scale = lax.rsqrt(jnp.mean(wide * wide, axis=-1, keepdims=True) + 1e-06)
    normed = (wide * scale).astype(BF16)
    scores = lax.dot_general(
        normed, router[...], (((1,), (1,)), ((), ())), preferred_element_type=F32
    )
    across = lax.broadcasted_iota(jnp.int32, (TOK, TOK), 1)
    down = lax.broadcasted_iota(jnp.int32, (TOK, TOK), 0)
    row, me = ids_row[...], where[1]
    expert = lax.broadcasted_iota(jnp.int32, (16, TOK), 0)
    hot_t = jnp.where(row == expert, 1.0, 0.0)
    same = jnp.where(across == down, 1.0, 0.0).astype(BF16)
    turn = (((1,), (1,)), ((), ()))
    hot = lax.dot_general(same, hot_t.astype(BF16), turn, preferred_element_type=F32)
    gate[...] = jax.nn.sigmoid(jnp.sum(scores * hot, axis=-1, keepdims=True))
    earlier = jnp.where(across < down, 1.0, 0.0).astype(BF16)
    counts = jnp.dot(earlier, hot.astype(BF16), preferred_element_type=F32)
    number = lax.broadcasted_iota(jnp.int32, (TOK, 16), 1)
    start = ((number >> 1) ^ me) * PAIR + (number & 1) * CAP
    slots = (counts + start.astype(F32)) * hot
    place[...] = jnp.sum(slots, axis=-1, keepdims=True).astype(jnp.int32)
    later = jnp.where(down < across, 1.0, 0.0).astype(BF16)
    counts_t = jnp.dot(hot_t.astype(BF16), later, preferred_element_type=F32)
    rank_t = jnp.sum(counts_t * hot_t, axis=0, keepdims=True).astype(jnp.int32)
    place_t = ((row >> 1) ^ me) * PAIR + (row & 1) * CAP + rank_t
    slot = lax.broadcasted_iota(jnp.int32, (8 * PAIR, TOK), 0)
    pick = jnp.where(slot == place_t, 1.0, 0.0).astype(BF16)
    slots = jnp.dot(pick, normed, preferred_element_type=F32).astype(BF16)
    for k, out in enumerate(outs):
        out[...] = slots[k * PAIR : (k + 1) * PAIR]


def route_call(*args):
    shapes = [((TOK, DIM), BF16), ((TOK, 1), F32), ((TOK, 1), jnp.int32)]
    shapes += [((PAIR, DIM), BF16)] * 8
    return pl.pallas_call(
        route_kernel,
        in_specs=[SMEM] * 2 + [VMEM] * (len(args) - 2),
        out_specs=[VMEM] * 11,
        out_shape=[jax.ShapeDtypeStruct(*shape) for shape in shapes],
        scratch_shapes=[pltpu.VMEM((512, DIM), BF16)],
        compiler_params=params(16),
        cost_estimate=cost(3),
        name="route",
    )(*args)


def expert_kernel(*refs):
    count = (len(refs) - 5) // 2
    arrays, weights, outs, hidden = refs[:count], refs[count : count + 4], refs[count + 4 : -1], refs[-1]
    for e in range(2):
        up, down = weights[e], weights[2 + e]
        rows = jnp.concatenate([a[e * CAP : (e + 1) * CAP] for a in arrays], axis=0)
        for at in range(0, FF, 512):
            part = pl.ds(at, 512)
            z = jnp.dot(rows, up[:, part], preferred_element_type=F32)
            act = 0.5 * z * (1.0 + jnp.tanh(0.7978845608028654 * (z + 0.044715 * (z * z * z))))
            hidden[:, part] = act.astype(BF16)
        result = jnp.dot(hidden[...], down[...], preferred_element_type=F32).astype(BF16)
        for n, out in enumerate(outs):
            out[e * CAP : (e + 1) * CAP] = result[n * CAP : (n + 1) * CAP]


def expert_call(name, arrays, weights):
    count = len(arrays)
    return pl.pallas_call(
        expert_kernel,
        in_specs=[VMEM] * (count + 4),
        out_specs=[VMEM] * count,
        out_shape=[jax.ShapeDtypeStruct((PAIR, DIM), BF16)] * count,
        scratch_shapes=[pltpu.VMEM((count * CAP, FF), BF16)],
        compiler_params=params(12),
        cost_estimate=cost(5),
        name=name,
    )(*arrays, *[in_vmem(a) for a in weights])


def mix_kernel(steps, *refs):
    base, gate, place, *arrays, out = refs
    slots = jnp.concatenate([a[...] for a in arrays], axis=0)
    lane = lax.broadcasted_iota(jnp.int32, (TOK, len(steps) * PAIR), 1)
    slot = lane
    for n, k in enumerate(steps):
        slot = jnp.where(lane >= n * PAIR, lane + (k - n) * PAIR, slot)
    pick = jnp.where(slot == place[...], 1.0, 0.0).astype(BF16)
    result = jnp.dot(pick, slots, preferred_element_type=F32)
    out[...] = (base[...].astype(F32) + gate[...] * result).astype(out.dtype)


def mix_call(name, steps, base, gate, place, arrays, dtype, micros):
    return pl.pallas_call(
        functools.partial(mix_kernel, steps),
        in_specs=[VMEM] * (3 + len(arrays)),
        out_specs=VMEM,
        out_shape=jax.ShapeDtypeStruct((TOK, DIM), dtype),
        compiler_params=params(12),
        cost_estimate=cost(micros),
        name=name,
    )(base, gate, place, *arrays)


def neighbours(value, axis, ahead):
    count = lax.axis_size(axis)
    pairs = [(i, i + 1) for i in range(count - 1)]
    return lax.ppermute(value, axis, pairs if ahead else [(j, i) for i, j in pairs])


def exchange(arrays, steps):
    return [lax.ppermute(arrays[k], "col", [(i, i ^ k) for i in range(8)]) for k in steps]


def local(
    scene, conv_first, conv_second, embed_weight, router_weight, expert_ids, expert_up, expert_down
):
    row, col = lax.axis_index("row"), lax.axis_index("col")
    x, high, core = row >> 2, (row >> 1) & 1, row & 1
    place = jnp.stack([row, col, core]).astype(jnp.int32)

    w = embed_weight
    w_minus, w_plus, w_high = send(w, dx=1), send(w, dx=-1), send(w, dh=1, dl=1)
    left = neighbours(scene[:, COLS - 2 :], "col", True)
    right = neighbours(scene[:, :2], "col", False)
    strip = jnp.concatenate([right, jnp.zeros((ROWS, 12, CH), BF16), left], axis=1)
    lines = [jnp.concatenate([scene[a:b], strip[a:b]], axis=1) for a, b in ((62, 64), (0, 2))]
    top, bottom = neighbours(lines[0], "row", True), neighbours(lines[1], "row", False)
    strip, w_minus, w_plus, w_high = lax.optimization_barrier((strip, w_minus, w_plus, w_high))
    w_far, w_high_plus = send(w_minus, dx=1), send(w_high, dx=-1)
    w_high_minus = send(w_minus, dh=1, dl=1)
    keep, other, up0, up1, down0, down1 = conv_call(
        place,
        in_hbm(scene),
        strip,
        top,
        bottom,
        in_hbm(conv_first),
        in_hbm(conv_second),
        (in_hbm(expert_up), in_hbm(expert_down)),
    )
    came = send(other, dc=1)
    keep, w_far, w_high_plus, w_high_minus = lax.optimization_barrier(
        (keep, w_far, w_high_plus, w_high_minus)
    )
    last = [
        send(w_high_plus[:176], dx=-1),
        send(w_high_minus[176:352], dx=1),
        send(w_far[352:], dh=1, dl=1),
    ]
    order = [(a & 3) * 2 + (b & 1) for b in (high, high + 1) for a in (x, x - 1, x + 1, x + 2)]
    order = jnp.stack(order).astype(jnp.int32)
    shards = [w, w_minus, w_plus, w_far, w_high, w_high_minus, w_high_plus]
    shards = [(n, [a]) for n, a in enumerate(shards)]
    own = embed_call("embed_own", order, keep, shards, micros=40)
    own, came = lax.optimization_barrier((own, came))
    partner = embed_call("embed_partner", order, came, shards)
    partner = embed_call("embed_partner_last", order, came, [(7, last)], [partner], BF16)
    came = send(partner, dc=1)
    embedded, gate, slots, *outs = route_call(
        place, order, keep, own, came, router_weight.T, expert_ids.reshape(1, TOK), *last
    )
    first, second, weights = (4, 1, 3), (2, 6, 5, 7), (up0, up1, down0, down1)
    in_first, in_second = exchange(outs, first), exchange(outs, second)
    back_first = expert_call("experts_first", [outs[0], *in_first], weights)
    in_second, back_first = lax.optimization_barrier((in_second, back_first))
    back = dict(zip((0, *first), back_first))
    back_first = [back[0], *exchange(back, first)]
    back = dict(zip(second, expert_call("experts_second", in_second, weights)))
    back_second = exchange(back, second)
    mixed = mix_call("mix_first", (0, *first), embedded, gate, slots, back_first, F32, 20)
    mixed = mix_call("mix_second", second, mixed, gate, slots, back_second, BF16, 2)
    return mixed.reshape(1, 1, TOK, DIM)


def solution(mesh):
    return jax.shard_map(
        local,
        mesh=mesh,
        in_specs=(
            P("row", "col", None),
            P(),
            P(),
            P("row", None),
            P(),
            P("row", "col", None, None),
            P("col", None, None),
            P("col", None, None),
        ),
        out_specs=P("row", "col", None, None),
        check_vma=False,
    )
```

```python
import functools

import jax
import jax.numpy as jnp
from jax import lax
from jax.experimental import pallas as pl
from jax.experimental.pallas import tpu as pltpu
from jax.sharding import PartitionSpec as P

ROWS, COLS, CH = 64, 256, 128
WIDE = 272
DIM, FF, CAP, TOK = 768, 3072, 48, 256
PAIR = 2 * CAP
STEPS, BAND = 4, 2
F32, BF16 = jnp.float32, jnp.bfloat16
ANY = pl.BlockSpec(memory_space=pl.ANY)
VMEM = pl.BlockSpec(memory_space=pltpu.VMEM)
SMEM = pl.BlockSpec(memory_space=pltpu.SMEM)
HBM = pl.BlockSpec(memory_space=pltpu.HBM)


def params(mib):
    return pltpu.CompilerParams(vmem_limit_bytes=mib * 2**20)


def cost(micros):
    return pl.CostEstimate(flops=int(micros * 1.15e9), bytes_accessed=0, transcendentals=0)


def hop(dx=0, dy=0, dh=0, dl=0, dc=0):
    pairs = []
    for x in range(4):
        for h in range(2):
            for c in range(2):
                for low in range(2):
                    for y in range(4):
                        here = (x * 4 + h * 2 + c) * 8 + low * 4 + y
                        there = (
                            ((x + dx) % 4 * 4 + (h + dh) % 2 * 2 + (c + dc) % 2) * 8
                            + (low + dl) % 2 * 4
                            + (y + dy) % 4
                        )
                        pairs.append((here, there))
    return pairs


def in_hbm(value):
    return pltpu.with_memory_space_constraint(value, pltpu.HBM)


def in_vmem(value):
    return pltpu.with_memory_space_constraint(value, pltpu.VMEM)


def send(value, **step):
    return lax.ppermute(value, ("row", "col"), hop(**step))


def pair_weights(source, target):
    zero = jnp.zeros((CH, CH), BF16)
    for j in range(4):
        for dx in range(3):
            rows = pl.ds(j * CH, CH)
            target[rows, pl.ds(dx * 256, CH)] = source[j, dx] if j < 3 else zero
            target[rows, pl.ds(dx * 256 + CH, CH)] = source[j - 1, dx] if j > 0 else zero


def pair_conv(source, weights, pair):
    taps = jnp.concatenate([source[2 * pair + j] for j in range(4)], axis=1)
    parts = jnp.dot(taps, weights[...], preferred_element_type=F32)
    left = pltpu.roll(parts[:, 0:256], 1, 0)
    right = pltpu.roll(parts[:, 512:768], WIDE - 1, 0)
    return left + parts[:, 256:512] + right


def conv_kernel(fetched, place, scene, strip, top, bottom, first, second, *refs):
    sources, (keep, other, *refs) = refs[:fetched], refs[fetched:]
    targets, refs = refs[: 2 * fetched], refs[2 * fetched :]
    block, hidden, rows, w1, w2, first_in, second_in, sems, weight_sems = refs
    step = pl.program_id(0)
    chunks = []
    for k in range(STEPS):
        hi = 8 * BAND * (k + 1) + 4
        lo = 0 if k == 0 else hi - 8 * BAND
        a, b = max(lo - 2, 0), min(hi - 2, ROWS)
        part = pl.ds(a + 2, b - a)
        copies = [
            pltpu.make_async_copy(scene.at[a:b], block.at[part, 0:COLS], sems.at[k, 0]),
            pltpu.make_async_copy(strip.at[a:b], block.at[part, COLS:WIDE], sems.at[k, 1]),
        ]
        if k == 0:
            copies.append(pltpu.make_async_copy(top, block.at[0:2], sems.at[k, 2]))
        if k == STEPS - 1:
            end = block.at[ROWS + 2 : ROWS + 4]
            copies.append(pltpu.make_async_copy(bottom, end, sems.at[k, 2]))
        chunks.append(copies)
    weights = [
        pltpu.make_async_copy(first, first_in, weight_sems.at[0]),
        pltpu.make_async_copy(second, second_in, weight_sems.at[1]),
    ]
    fetches = [
        pltpu.make_async_copy(sources[n // 2].at[n % 2], target, weight_sems.at[2 + n])
        for n, target in enumerate(targets)
    ]
    place_row, place_col, core = place[0], place[1], place[2]
    tail = lax.broadcasted_iota(jnp.int32, (16, 256), 0)
    cut = ((place_col == 0) & (tail >= 8)) | ((place_col == 7) & (tail < 8))
    edge = jnp.where(cut, 0.0, 1.0).astype(F32)

    def conv_first(pair):
        value = jnp.maximum(pair_conv(block, w1, pair), 0.0)
        body, ends = value[0:COLS].astype(BF16), (value[COLS:WIDE] * edge).astype(BF16)
        for i in range(2):
            hidden[2 * pair + i, 0:COLS] = body[:, i * CH : (i + 1) * CH]
            hidden[2 * pair + i, COLS:WIDE] = ends[:, i * CH : (i + 1) * CH]

    @pl.when(step == 0)
    def _():
        for copy in [*weights, *chunks[0]]:
            copy.start()
        for copy in weights:
            copy.wait()
        pair_weights(first_in, w1)
        pair_weights(second_in, w2)
        for copy in chunks[0]:
            copy.wait()
        for copy in chunks[1]:
            copy.start()
        conv_first(0)

        @pl.when(place_row == 0)
        def _():
            hidden[0] = jnp.zeros((WIDE, CH), BF16)

    for k in range(1, STEPS):

        @pl.when(step == k)
        def _(k=k):
            for copy in chunks[k]:
                copy.wait()
            for copy in chunks[k + 1] if k + 1 < STEPS else ():
                copy.start()
            for copy in fetches if k == 1 else ():
                copy.start()

    first_pair = 4 * BAND * step
    for i in range(4 * BAND):
        conv_first(first_pair + 1 + i)

    @pl.when((step == STEPS - 1) & (place_row == 15))
    def _():
        hidden[ROWS + 1] = jnp.zeros((WIDE, CH), BF16)

    for i in range(4 * BAND):
        pair = first_pair + i
        value = pair_conv(hidden, w2, pair)[0:COLS]
        for n in range(2):
            cells = block[2 * pair + 2 + n, 0:COLS].astype(F32)
            rows[pl.ds((2 * i + n) * COLS, COLS), :] = value[:, n * CH : (n + 1) * CH] + cells
        for line in (2 * i, 2 * i + 1):
            dy, at = line % 8, pl.ds(line // 8 * 32, 32)
            for j in range(4):
                low = rows[pl.ds(line * COLS + j, 32, stride=8), :]
                high = rows[pl.ds(line * COLS + 4 + j, 32, stride=8), :]
                lanes = pl.ds(j * CH, CH)
                keep[dy, at, lanes] = jnp.where(core == 0, low, high).astype(BF16)
                other[dy, at, lanes] = jnp.where(core == 0, high, low).astype(BF16)
    if fetches:

        @pl.when(step == STEPS - 1)
        def _():
            for copy in fetches:
                copy.wait()


def conv_call(place, scene, strip, top, bottom, first, second, fetch):
    shape = jax.ShapeDtypeStruct((8, TOK, 512), BF16)
    halves = [pltpu.VMEM(a.shape[1:], a.dtype) for a in fetch for _ in range(2)]
    band = pl.BlockSpec((8, 32 * BAND, 512), lambda i: (0, i, 0))
    return pl.pallas_call(
        functools.partial(conv_kernel, len(fetch)),
        grid=(STEPS,),
        in_specs=[SMEM, HBM, ANY, ANY, ANY, HBM, HBM] + [HBM] * len(fetch),
        out_specs=[band, band] + [ANY] * len(halves),
        out_shape=[shape, shape] + halves,
        scratch_shapes=[
            pltpu.VMEM((ROWS + 4, WIDE, CH), BF16),
            pltpu.VMEM((ROWS + 2, WIDE, CH), BF16),
            pltpu.VMEM((8 * BAND * COLS + 16, CH), F32),
            pltpu.VMEM((512, 768), BF16),
            pltpu.VMEM((512, 768), BF16),
            pltpu.VMEM((3, 3, CH, CH), BF16),
            pltpu.VMEM((3, 3, CH, CH), BF16),
            pltpu.SemaphoreType.DMA((STEPS, 3)),
            pltpu.SemaphoreType.DMA((6,)),
        ],
        compiler_params=params(28),
        cost_estimate=cost(20),
        name="convs",
    )(place, scene, strip, top, bottom, first, second, *fetch)


def embed_kernel(layout, order, tokens, *refs):
    count = sum(len(parts) for _, parts in layout)
    pieces, given, total, whole = refs[:count], refs[count:-2], refs[-2], refs[-1]
    result = given[0][...] if given else None
    at = 0
    for which, parts in layout:
        shard = pieces[at]
        if len(parts) > 1:
            shard = whole
            for m, (first, rows) in enumerate(parts):
                whole[pl.ds(first, rows)] = pieces[at + m][...]
        at += len(parts)
        part = jnp.dot(tokens[order[which]], shard[...], preferred_element_type=F32)
        result = part if result is None else result + part
    total[...] = result.astype(total.dtype)


def embed_call(name, order, tokens, shards, sums=(), dtype=F32, micros=3):
    layout, arrays = [], []
    for which, parts in shards:
        heights = [part.shape[0] for part in parts]
        layout.append((which, [(sum(heights[:m]), rows) for m, rows in enumerate(heights)]))
        arrays.extend(parts)
    return pl.pallas_call(
        functools.partial(embed_kernel, layout),
        in_specs=[SMEM] + [VMEM] * (1 + len(arrays) + len(sums)),
        out_specs=VMEM,
        out_shape=jax.ShapeDtypeStruct((TOK, DIM), dtype),
        scratch_shapes=[pltpu.VMEM((512, DIM), BF16)],
        compiler_params=params(12),
        cost_estimate=cost(micros),
        name=name,
    )(order, tokens, *arrays, *sums)


def route_kernel(where, own, came, router, ids_row, embedded, gate, place, *outs):
    value = (own[...] + came[...].astype(F32)).astype(BF16)
    embedded[...] = value
    wide = value.astype(F32)
    scale = lax.rsqrt(jnp.mean(wide * wide, axis=-1, keepdims=True) + 1e-06)
    normed = (wide * scale).astype(BF16)
    scores = lax.dot_general(
        normed, router[...], (((1,), (1,)), ((), ())), preferred_element_type=F32
    )
    across = lax.broadcasted_iota(jnp.int32, (TOK, TOK), 1)
    down = lax.broadcasted_iota(jnp.int32, (TOK, TOK), 0)
    row, me = ids_row[...], where[1]
    expert = lax.broadcasted_iota(jnp.int32, (16, TOK), 0)
    hot_t = jnp.where(row == expert, 1.0, 0.0)
    same = jnp.where(across == down, 1.0, 0.0).astype(BF16)
    turn = (((1,), (1,)), ((), ()))
    hot = lax.dot_general(same, hot_t.astype(BF16), turn, preferred_element_type=F32)
    gate[...] = jax.nn.sigmoid(jnp.sum(scores * hot, axis=-1, keepdims=True))
    earlier = jnp.where(across < down, 1.0, 0.0).astype(BF16)
    counts = jnp.dot(earlier, hot.astype(BF16), preferred_element_type=F32)
    number = lax.broadcasted_iota(jnp.int32, (TOK, 16), 1)
    start = ((number >> 1) ^ me) * PAIR + (number & 1) * CAP
    slots = (counts + start.astype(F32)) * hot
    place[...] = jnp.sum(slots, axis=-1, keepdims=True).astype(jnp.int32)
    later = jnp.where(down < across, 1.0, 0.0).astype(BF16)
    counts_t = jnp.dot(hot_t.astype(BF16), later, preferred_element_type=F32)
    rank_t = jnp.sum(counts_t * hot_t, axis=0, keepdims=True).astype(jnp.int32)
    place_t = ((row >> 1) ^ me) * PAIR + (row & 1) * CAP + rank_t
    slot = lax.broadcasted_iota(jnp.int32, (8 * PAIR, TOK), 0)
    pick = jnp.where(slot == place_t, 1.0, 0.0).astype(BF16)
    slots = jnp.dot(pick, normed, preferred_element_type=F32).astype(BF16)
    for k, out in enumerate(outs):
        out[...] = slots[k * PAIR : (k + 1) * PAIR]


def route_call(*args):
    shapes = [((TOK, DIM), BF16), ((TOK, 1), F32), ((TOK, 1), jnp.int32)]
    shapes += [((PAIR, DIM), BF16)] * 8
    return pl.pallas_call(
        route_kernel,
        in_specs=[SMEM] + [VMEM] * 4,
        out_specs=[VMEM] * 11,
        out_shape=[jax.ShapeDtypeStruct(*shape) for shape in shapes],
        compiler_params=params(16),
        cost_estimate=cost(3),
        name="route",
    )(*args)


def expert_kernel(*refs):
    count = (len(refs) - 5) // 2
    arrays, weights, outs, hidden = refs[:count], refs[count : count + 4], refs[count + 4 : -1], refs[-1]
    for e in range(2):
        up, down = weights[e], weights[2 + e]
        rows = jnp.concatenate([a[e * CAP : (e + 1) * CAP] for a in arrays], axis=0)
        for at in range(0, FF, 512):
            part = pl.ds(at, 512)
            z = jnp.dot(rows, up[:, part], preferred_element_type=F32)
            act = 0.5 * z * (1.0 + jnp.tanh(0.7978845608028654 * (z + 0.044715 * (z * z * z))))
            hidden[:, part] = act.astype(BF16)
        result = jnp.dot(hidden[...], down[...], preferred_element_type=F32).astype(BF16)
        for n, out in enumerate(outs):
            out[e * CAP : (e + 1) * CAP] = result[n * CAP : (n + 1) * CAP]


def expert_call(name, arrays, weights):
    count = len(arrays)
    return pl.pallas_call(
        expert_kernel,
        in_specs=[VMEM] * (count + 4),
        out_specs=[VMEM] * count,
        out_shape=[jax.ShapeDtypeStruct((PAIR, DIM), BF16)] * count,
        scratch_shapes=[pltpu.VMEM((count * CAP, FF), BF16)],
        compiler_params=params(12),
        cost_estimate=cost(5),
        name=name,
    )(*arrays, *[in_vmem(a) for a in weights])


def mix_kernel(steps, *refs):
    base, gate, place, *arrays, out = refs
    slots = jnp.concatenate([a[...] for a in arrays], axis=0)
    lane = lax.broadcasted_iota(jnp.int32, (TOK, len(steps) * PAIR), 1)
    slot = lane
    for n, k in enumerate(steps):
        slot = jnp.where(lane >= n * PAIR, lane + (k - n) * PAIR, slot)
    pick = jnp.where(slot == place[...], 1.0, 0.0).astype(BF16)
    result = jnp.dot(pick, slots, preferred_element_type=F32)
    out[...] = (base[...].astype(F32) + gate[...] * result).astype(out.dtype)


def mix_call(name, steps, base, gate, place, arrays, dtype, micros):
    return pl.pallas_call(
        functools.partial(mix_kernel, steps),
        in_specs=[VMEM] * (3 + len(arrays)),
        out_specs=VMEM,
        out_shape=jax.ShapeDtypeStruct((TOK, DIM), dtype),
        compiler_params=params(12),
        cost_estimate=cost(micros),
        name=name,
    )(base, gate, place, *arrays)


def neighbours(value, axis, ahead):
    count = lax.axis_size(axis)
    pairs = [(i, i + 1) for i in range(count - 1)]
    return lax.ppermute(value, axis, pairs if ahead else [(j, i) for i, j in pairs])


def exchange(arrays, steps):
    return [lax.ppermute(arrays[k], "col", [(i, i ^ k) for i in range(8)]) for k in steps]


def local(
    scene, conv_first, conv_second, embed_weight, router_weight, expert_ids, expert_up, expert_down
):
    row, col = lax.axis_index("row"), lax.axis_index("col")
    x, high, core = row >> 2, (row >> 1) & 1, row & 1
    place = jnp.stack([row, col, core]).astype(jnp.int32)

    w = embed_weight
    w_minus, w_plus, w_high = send(w, dx=1), send(w, dx=-1), send(w, dh=1, dl=1)
    left = neighbours(scene[:, COLS - 2 :], "col", True)
    right = neighbours(scene[:, :2], "col", False)
    strip = jnp.concatenate([right, jnp.zeros((ROWS, 12, CH), BF16), left], axis=1)
    lines = [jnp.concatenate([scene[a:b], strip[a:b]], axis=1) for a, b in ((62, 64), (0, 2))]
    top, bottom = neighbours(lines[0], "row", True), neighbours(lines[1], "row", False)
    strip, w_minus, w_plus, w_high = lax.optimization_barrier((strip, w_minus, w_plus, w_high))
    w_far, w_high_plus = send(w_minus, dx=1), send(w_high, dx=-1)
    w_high_minus = send(w_minus, dh=1, dl=1)
    keep, other, up0, up1, down0, down1 = conv_call(
        place,
        in_hbm(scene),
        strip,
        top,
        bottom,
        in_hbm(conv_first),
        in_hbm(conv_second),
        (in_hbm(expert_up), in_hbm(expert_down)),
    )
    came = send(other, dc=1)
    keep, w_far, w_high_plus, w_high_minus = lax.optimization_barrier(
        (keep, w_far, w_high_plus, w_high_minus)
    )
    last = [
        send(w_high_plus[:176], dx=-1),
        send(w_high_minus[176:352], dx=1),
        send(w_far[352:], dh=1, dl=1),
    ]
    order = [(a & 3) * 2 + (b & 1) for b in (high, high + 1) for a in (x, x - 1, x + 1, x + 2)]
    order = jnp.stack(order).astype(jnp.int32)
    shards = [w, w_minus, w_plus, w_far, w_high, w_high_minus, w_high_plus]
    shards = [(n, [a]) for n, a in enumerate(shards)]
    own = embed_call("embed_own", order, keep, shards, micros=40)
    own, came = lax.optimization_barrier((own, came))
    partner = embed_call("embed_partner", order, came, shards)
    partner = embed_call("embed_partner_last", order, came, [(7, last)], [partner], BF16)
    came = send(partner, dc=1)
    own = embed_call("embed_own_last", order, keep, [(7, last)], [own])
    embedded, gate, slots, *outs = route_call(
        place, own, came, router_weight.T, expert_ids.reshape(1, TOK)
    )
    first, second, weights = (4, 1, 3), (2, 6, 5, 7), (up0, up1, down0, down1)
    in_first, in_second = exchange(outs, first), exchange(outs, second)
    back_first = expert_call("experts_first", [outs[0], *in_first], weights)
    in_second, back_first = lax.optimization_barrier((in_second, back_first))
    back = dict(zip((0, *first), back_first))
    back_first = [back[0], *exchange(back, first)]
    back = dict(zip(second, expert_call("experts_second", in_second, weights)))
    back_second = exchange(back, second)
    mixed = mix_call("mix_first", (0, *first), embedded, gate, slots, back_first, F32, 20)
    mixed = mix_call("mix_second", second, mixed, gate, slots, back_second, BF16, 2)
    return mixed.reshape(1, 1, TOK, DIM)


def solution(mesh):
    return jax.shard_map(
        local,
        mesh=mesh,
        in_specs=(
            P("row", "col", None),
            P(),
            P(),
            P("row", None),
            P(),
            P("row", "col", None, None),
            P("col", None, None),
            P("col", None, None),
        ),
        out_specs=P("row", "col", None, None),
        check_vma=False,
    )
```

```python
import functools

import jax
import jax.numpy as jnp
from jax import lax
from jax.experimental import pallas as pl
from jax.experimental.pallas import tpu as pltpu
from jax.sharding import PartitionSpec as P

ROWS, COLS, CH = 64, 256, 128
WIDE = 272
DIM, FF, CAP, TOK = 768, 3072, 48, 256
PAIR = 2 * CAP
STEPS, BAND = 4, 2
F32, BF16 = jnp.float32, jnp.bfloat16
ANY = pl.BlockSpec(memory_space=pl.ANY)
VMEM = pl.BlockSpec(memory_space=pltpu.VMEM)
SMEM = pl.BlockSpec(memory_space=pltpu.SMEM)
HBM = pl.BlockSpec(memory_space=pltpu.HBM)


def params(mib):
    return pltpu.CompilerParams(vmem_limit_bytes=mib * 2**20)


def cost(micros):
    return pl.CostEstimate(flops=int(micros * 1.15e9), bytes_accessed=0, transcendentals=0)


def hop(dx=0, dy=0, dh=0, dl=0, dc=0):
    pairs = []
    for x in range(4):
        for h in range(2):
            for c in range(2):
                for low in range(2):
                    for y in range(4):
                        here = (x * 4 + h * 2 + c) * 8 + low * 4 + y
                        there = (
                            ((x + dx) % 4 * 4 + (h + dh) % 2 * 2 + (c + dc) % 2) * 8
                            + (low + dl) % 2 * 4
                            + (y + dy) % 4
                        )
                        pairs.append((here, there))
    return pairs


def in_hbm(value):
    return pltpu.with_memory_space_constraint(value, pltpu.HBM)


def in_vmem(value):
    return pltpu.with_memory_space_constraint(value, pltpu.VMEM)


def send(value, **step):
    return lax.ppermute(value, ("row", "col"), hop(**step))


def pair_weights(source, target):
    zero = jnp.zeros((CH, CH), BF16)
    for j in range(4):
        for dx in range(3):
            rows = pl.ds(j * CH, CH)
            target[rows, pl.ds(dx * 256, CH)] = source[j, dx] if j < 3 else zero
            target[rows, pl.ds(dx * 256 + CH, CH)] = source[j - 1, dx] if j > 0 else zero


def pair_conv(source, weights, pair):
    taps = jnp.concatenate([source[2 * pair + j] for j in range(4)], axis=1)
    parts = jnp.dot(taps, weights[...], preferred_element_type=F32)
    left = pltpu.roll(parts[:, 0:256], 1, 0)
    right = pltpu.roll(parts[:, 512:768], WIDE - 1, 0)
    return left + parts[:, 256:512] + right


def conv_kernel(fetched, place, scene, strip, top, bottom, first, second, *refs):
    sources, (keep, other, *refs) = refs[:fetched], refs[fetched:]
    targets, refs = refs[: 2 * fetched], refs[2 * fetched :]
    block, hidden, rows, w1, w2, first_in, second_in, sems, weight_sems = refs
    step = pl.program_id(0)
    chunks = []
    for k in range(STEPS):
        hi = 8 * BAND * (k + 1) + 4
        lo = 0 if k == 0 else hi - 8 * BAND
        a, b = max(lo - 2, 0), min(hi - 2, ROWS)
        part = pl.ds(a + 2, b - a)
        copies = [
            pltpu.make_async_copy(scene.at[a:b], block.at[part, 0:COLS], sems.at[k, 0]),
            pltpu.make_async_copy(strip.at[a:b], block.at[part, COLS:WIDE], sems.at[k, 1]),
        ]
        if k == 0:
            copies.append(pltpu.make_async_copy(top, block.at[0:2], sems.at[k, 2]))
        if k == STEPS - 1:
            end = block.at[ROWS + 2 : ROWS + 4]
            copies.append(pltpu.make_async_copy(bottom, end, sems.at[k, 2]))
        chunks.append(copies)
    weights = [
        pltpu.make_async_copy(first, first_in, weight_sems.at[0]),
        pltpu.make_async_copy(second, second_in, weight_sems.at[1]),
    ]
    fetches = [
        pltpu.make_async_copy(sources[n // 2].at[n % 2], target, weight_sems.at[2 + n])
        for n, target in enumerate(targets)
    ]
    place_row, place_col, core = place[0], place[1], place[2]
    tail = lax.broadcasted_iota(jnp.int32, (16, 256), 0)
    cut = ((place_col == 0) & (tail >= 8)) | ((place_col == 7) & (tail < 8))
    edge = jnp.where(cut, 0.0, 1.0).astype(F32)

    def conv_first(pair):
        value = jnp.maximum(pair_conv(block, w1, pair), 0.0)
        body, ends = value[0:COLS].astype(BF16), (value[COLS:WIDE] * edge).astype(BF16)
        for i in range(2):
            hidden[2 * pair + i, 0:COLS] = body[:, i * CH : (i + 1) * CH]
            hidden[2 * pair + i, COLS:WIDE] = ends[:, i * CH : (i + 1) * CH]

    @pl.when(step == 0)
    def _():
        for copy in [*chunks[0], *weights, *chunks[1]]:
            copy.start()
        for copy in weights:
            copy.wait()
        pair_weights(first_in, w1)
        pair_weights(second_in, w2)
        for copy in chunks[0]:
            copy.wait()
        conv_first(0)

        @pl.when(place_row == 0)
        def _():
            hidden[0] = jnp.zeros((WIDE, CH), BF16)

    for k in range(1, STEPS):

        @pl.when(step == k)
        def _(k=k):
            for copy in chunks[k]:
                copy.wait()
            for copy in chunks[k + 1] if k + 1 < STEPS else ():
                copy.start()
            for copy in fetches if k == 1 else ():
                copy.start()

    first_pair = 4 * BAND * step
    for i in range(4 * BAND):
        conv_first(first_pair + 1 + i)

    @pl.when((step == STEPS - 1) & (place_row == 15))
    def _():
        hidden[ROWS + 1] = jnp.zeros((WIDE, CH), BF16)

    for i in range(4 * BAND):
        pair = first_pair + i
        value = pair_conv(hidden, w2, pair)[0:COLS]
        for n in range(2):
            cells = block[2 * pair + 2 + n, 0:COLS].astype(F32)
            rows[pl.ds((2 * i + n) * COLS, COLS), :] = value[:, n * CH : (n + 1) * CH] + cells
    for line in range(8 * BAND):
        dy, at = line % 8, pl.ds(line // 8 * 32, 32)
        for j in range(4):
            low = rows[pl.ds(line * COLS + j, 32, stride=8), :]
            high = rows[pl.ds(line * COLS + 4 + j, 32, stride=8), :]
            lanes = pl.ds(j * CH, CH)
            keep[dy, at, lanes] = jnp.where(core == 0, low, high).astype(BF16)
            other[dy, at, lanes] = jnp.where(core == 0, high, low).astype(BF16)
    if fetches:

        @pl.when(step == STEPS - 1)
        def _():
            for copy in fetches:
                copy.wait()


def conv_call(place, scene, strip, top, bottom, first, second, fetch):
    shape = jax.ShapeDtypeStruct((8, TOK, 512), BF16)
    halves = [pltpu.VMEM(a.shape[1:], a.dtype) for a in fetch for _ in range(2)]
    band = pl.BlockSpec((8, 32 * BAND, 512), lambda i: (0, i, 0))
    return pl.pallas_call(
        functools.partial(conv_kernel, len(fetch)),
        grid=(STEPS,),
        in_specs=[SMEM, HBM, ANY, ANY, ANY, HBM, HBM] + [HBM] * len(fetch),
        out_specs=[band, band] + [ANY] * len(halves),
        out_shape=[shape, shape] + halves,
        scratch_shapes=[
            pltpu.VMEM((ROWS + 4, WIDE, CH), BF16),
            pltpu.VMEM((ROWS + 2, WIDE, CH), BF16),
            pltpu.VMEM((8 * BAND * COLS + 16, CH), F32),
            pltpu.VMEM((512, 768), BF16),
            pltpu.VMEM((512, 768), BF16),
            pltpu.VMEM((3, 3, CH, CH), BF16),
            pltpu.VMEM((3, 3, CH, CH), BF16),
            pltpu.SemaphoreType.DMA((STEPS, 3)),
            pltpu.SemaphoreType.DMA((6,)),
        ],
        compiler_params=params(28),
        cost_estimate=cost(20),
        name="convs",
    )(place, scene, strip, top, bottom, first, second, *fetch)


def embed_kernel(layout, order, tokens, *refs):
    count = sum(len(parts) for _, parts in layout)
    pieces, given, total, whole = refs[:count], refs[count:-2], refs[-2], refs[-1]
    result = given[0][...] if given else None
    at = 0
    for which, parts in layout:
        shard = pieces[at]
        if len(parts) > 1:
            shard = whole
            for m, (first, rows) in enumerate(parts):
                whole[pl.ds(first, rows)] = pieces[at + m][...]
        at += len(parts)
        part = jnp.dot(tokens[order[which]], shard[...], preferred_element_type=F32)
        result = part if result is None else result + part
    total[...] = result.astype(total.dtype)


def embed_call(name, order, tokens, shards, sums=(), dtype=F32, micros=3):
    layout, arrays = [], []
    for which, parts in shards:
        heights = [part.shape[0] for part in parts]
        layout.append((which, [(sum(heights[:m]), rows) for m, rows in enumerate(heights)]))
        arrays.extend(parts)
    return pl.pallas_call(
        functools.partial(embed_kernel, layout),
        in_specs=[SMEM] + [VMEM] * (1 + len(arrays) + len(sums)),
        out_specs=VMEM,
        out_shape=jax.ShapeDtypeStruct((TOK, DIM), dtype),
        scratch_shapes=[pltpu.VMEM((512, DIM), BF16)],
        compiler_params=params(12),
        cost_estimate=cost(micros),
        name=name,
    )(order, tokens, *arrays, *sums)


def route_kernel(where, own, came, router, ids_row, embedded, gate, place, *outs):
    value = (own[...] + came[...].astype(F32)).astype(BF16)
    embedded[...] = value
    wide = value.astype(F32)
    scale = lax.rsqrt(jnp.mean(wide * wide, axis=-1, keepdims=True) + 1e-06)
    normed = (wide * scale).astype(BF16)
    scores = lax.dot_general(
        normed, router[...], (((1,), (1,)), ((), ())), preferred_element_type=F32
    )
    across = lax.broadcasted_iota(jnp.int32, (TOK, TOK), 1)
    down = lax.broadcasted_iota(jnp.int32, (TOK, TOK), 0)
    row, me = ids_row[...], where[1]
    expert = lax.broadcasted_iota(jnp.int32, (16, TOK), 0)
    hot_t = jnp.where(row == expert, 1.0, 0.0)
    same = jnp.where(across == down, 1.0, 0.0).astype(BF16)
    turn = (((1,), (1,)), ((), ()))
    hot = lax.dot_general(same, hot_t.astype(BF16), turn, preferred_element_type=F32)
    gate[...] = jax.nn.sigmoid(jnp.sum(scores * hot, axis=-1, keepdims=True))
    earlier = jnp.where(across < down, 1.0, 0.0).astype(BF16)
    counts = jnp.dot(earlier, hot.astype(BF16), preferred_element_type=F32)
    number = lax.broadcasted_iota(jnp.int32, (TOK, 16), 1)
    start = ((number >> 1) ^ me) * PAIR + (number & 1) * CAP
    slots = (counts + start.astype(F32)) * hot
    place[...] = jnp.sum(slots, axis=-1, keepdims=True).astype(jnp.int32)
    later = jnp.where(down < across, 1.0, 0.0).astype(BF16)
    counts_t = jnp.dot(hot_t.astype(BF16), later, preferred_element_type=F32)
    rank_t = jnp.sum(counts_t * hot_t, axis=0, keepdims=True).astype(jnp.int32)
    place_t = ((row >> 1) ^ me) * PAIR + (row & 1) * CAP + rank_t
    slot = lax.broadcasted_iota(jnp.int32, (8 * PAIR, TOK), 0)
    pick = jnp.where(slot == place_t, 1.0, 0.0).astype(BF16)
    slots = jnp.dot(pick, normed, preferred_element_type=F32).astype(BF16)
    for k, out in enumerate(outs):
        out[...] = slots[k * PAIR : (k + 1) * PAIR]


def route_call(*args):
    shapes = [((TOK, DIM), BF16), ((TOK, 1), F32), ((TOK, 1), jnp.int32)]
    shapes += [((PAIR, DIM), BF16)] * 8
    return pl.pallas_call(
        route_kernel,
        in_specs=[SMEM] + [VMEM] * 4,
        out_specs=[VMEM] * 11,
        out_shape=[jax.ShapeDtypeStruct(*shape) for shape in shapes],
        compiler_params=params(16),
        cost_estimate=cost(3),
        name="route",
    )(*args)


def expert_kernel(*refs):
    count = (len(refs) - 5) // 2
    arrays, weights, outs, hidden = refs[:count], refs[count : count + 4], refs[count + 4 : -1], refs[-1]
    for e in range(2):
        up, down = weights[e], weights[2 + e]
        rows = jnp.concatenate([a[e * CAP : (e + 1) * CAP] for a in arrays], axis=0)
        for at in range(0, FF, 512):
            part = pl.ds(at, 512)
            z = jnp.dot(rows, up[:, part], preferred_element_type=F32)
            act = 0.5 * z * (1.0 + jnp.tanh(0.7978845608028654 * (z + 0.044715 * (z * z * z))))
            hidden[:, part] = act.astype(BF16)
        result = jnp.dot(hidden[...], down[...], preferred_element_type=F32).astype(BF16)
        for n, out in enumerate(outs):
            out[e * CAP : (e + 1) * CAP] = result[n * CAP : (n + 1) * CAP]


def expert_call(name, arrays, weights):
    count = len(arrays)
    return pl.pallas_call(
        expert_kernel,
        in_specs=[VMEM] * (count + 4),
        out_specs=[VMEM] * count,
        out_shape=[jax.ShapeDtypeStruct((PAIR, DIM), BF16)] * count,
        scratch_shapes=[pltpu.VMEM((count * CAP, FF), BF16)],
        compiler_params=params(12),
        cost_estimate=cost(5),
        name=name,
    )(*arrays, *[in_vmem(a) for a in weights])


def mix_kernel(steps, *refs):
    base, gate, place, *arrays, out = refs
    slots = jnp.concatenate([a[...] for a in arrays], axis=0)
    lane = lax.broadcasted_iota(jnp.int32, (TOK, len(steps) * PAIR), 1)
    slot = lane
    for n, k in enumerate(steps):
        slot = jnp.where(lane >= n * PAIR, lane + (k - n) * PAIR, slot)
    pick = jnp.where(slot == place[...], 1.0, 0.0).astype(BF16)
    result = jnp.dot(pick, slots, preferred_element_type=F32)
    out[...] = (base[...].astype(F32) + gate[...] * result).astype(out.dtype)


def mix_call(name, steps, base, gate, place, arrays, dtype, micros):
    return pl.pallas_call(
        functools.partial(mix_kernel, steps),
        in_specs=[VMEM] * (3 + len(arrays)),
        out_specs=VMEM,
        out_shape=jax.ShapeDtypeStruct((TOK, DIM), dtype),
        compiler_params=params(12),
        cost_estimate=cost(micros),
        name=name,
    )(base, gate, place, *arrays)


def neighbours(value, axis, ahead):
    count = lax.axis_size(axis)
    pairs = [(i, i + 1) for i in range(count - 1)]
    return lax.ppermute(value, axis, pairs if ahead else [(j, i) for i, j in pairs])


def exchange(arrays, steps):
    return [lax.ppermute(arrays[k], "col", [(i, i ^ k) for i in range(8)]) for k in steps]


def local(
    scene, conv_first, conv_second, embed_weight, router_weight, expert_ids, expert_up, expert_down
):
    row, col = lax.axis_index("row"), lax.axis_index("col")
    x, high, core = row >> 2, (row >> 1) & 1, row & 1
    place = jnp.stack([row, col, core]).astype(jnp.int32)

    w = embed_weight
    w_minus, w_plus, w_high = send(w, dx=1), send(w, dx=-1), send(w, dh=1, dl=1)
    left = neighbours(scene[:, COLS - 2 :], "col", True)
    right = neighbours(scene[:, :2], "col", False)
    strip = jnp.concatenate([right, jnp.zeros((ROWS, 12, CH), BF16), left], axis=1)
    lines = [jnp.concatenate([scene[a:b], strip[a:b]], axis=1) for a, b in ((62, 64), (0, 2))]
    top, bottom = neighbours(lines[0], "row", True), neighbours(lines[1], "row", False)
    strip, w_minus, w_plus, w_high = lax.optimization_barrier((strip, w_minus, w_plus, w_high))
    w_far, w_high_plus = send(w_minus, dx=1), send(w_high, dx=-1)
    w_high_minus = send(w_minus, dh=1, dl=1)
    keep, other, up0, up1, down0, down1 = conv_call(
        place,
        in_hbm(scene),
        strip,
        top,
        bottom,
        in_hbm(conv_first),
        in_hbm(conv_second),
        (in_hbm(expert_up), in_hbm(expert_down)),
    )
    came = send(other, dc=1)
    keep, w_far, w_high_plus, w_high_minus = lax.optimization_barrier(
        (keep, w_far, w_high_plus, w_high_minus)
    )
    last = [
        send(w_high_plus[:176], dx=-1),
        send(w_high_minus[176:352], dx=1),
        send(w_far[352:], dh=1, dl=1),
    ]
    order = [(a & 3) * 2 + (b & 1) for b in (high, high + 1) for a in (x, x - 1, x + 1, x + 2)]
    order = jnp.stack(order).astype(jnp.int32)
    shards = [w, w_minus, w_plus, w_far, w_high, w_high_minus, w_high_plus]
    shards = [(n, [a]) for n, a in enumerate(shards)]
    own = embed_call("embed_own", order, keep, shards, micros=40)
    own, came = lax.optimization_barrier((own, came))
    partner = embed_call("embed_partner", order, came, shards)
    partner = embed_call("embed_partner_last", order, came, [(7, last)], [partner], BF16)
    came = send(partner, dc=1)
    own = embed_call("embed_own_last", order, keep, [(7, last)], [own])
    embedded, gate, slots, *outs = route_call(
        place, own, came, router_weight.T, expert_ids.reshape(1, TOK)
    )
    first, second, weights = (4, 1, 3), (2, 6, 5, 7), (up0, up1, down0, down1)
    in_first, in_second = exchange(outs, first), exchange(outs, second)
    back_first = expert_call("experts_first", [outs[0], *in_first], weights)
    in_second, back_first = lax.optimization_barrier((in_second, back_first))
    back = dict(zip((0, *first), back_first))
    back_first = [back[0], *exchange(back, first)]
    back = dict(zip(second, expert_call("experts_second", in_second, weights)))
    back_second = exchange(back, second)
    mixed = mix_call("mix_first", (0, *first), embedded, gate, slots, back_first, F32, 20)
    mixed = mix_call("mix_second", second, mixed, gate, slots, back_second, BF16, 2)
    return mixed.reshape(1, 1, TOK, DIM)


def solution(mesh):
    return jax.shard_map(
        local,
        mesh=mesh,
        in_specs=(
            P("row", "col", None),
            P(),
            P(),
            P("row", None),
            P(),
            P("row", "col", None, None),
            P("col", None, None),
            P("col", None, None),
        ),
        out_specs=P("row", "col", None, None),
        check_vma=False,
    )
```
